128 devices in a mesh: row: 8 (over y, core), col: 16 (over x, z).
Axes of the slice: x: 4, y: 4, z: 4, core: 2. Of those that a mesh axis runs over, the one named last changes fastest.
Arguments:
- child_fronts: float32 [16384, 8192], P('row', 'col'), may hold values from -3 to 28, as said below
- root_front: float32 [12288, 12288], P('row', 'col'), may hold values from -3 to 28, as said below
- child_map: int32 [2, 60], replicated, may hold values from 0 to 95, as said below
- panel_order: int32 [3], replicated, may hold values from 0 to 47, as said below
Outputs:
- child_factors: float32 [16384, 8192], P('row', 'col')
- root_factors: float32 [12288, 12288], P('row', 'col')
The draws below stay inside these ranges and needn't reach their ends.
Inputs may be any that keep to these rules, and one draw needn't show every extreme that they name: Each row of child_map holds distinct root blocks; with t = (m mod 6) * 16 + m // 6 for an entry m, t rises by 1 or 2 from one entry of a row to the next. `panel_order`: distinct panels; the last panel of the root front is always among them. `child_fronts`: the diagonal entries lie in 14 to 28, the others in -3 to 3. `root_front`: the diagonal entries lie in 14 to 28, the others in -3 to 3.
All inputs are finite; a program needn't handle non-finite values.
Results may differ from the reference program's by a relative error of at most 0.0003.
Values sent between devices are 32-bit elements; how exact they have to be, the bound alone decides.
A program may use at most 192 MiB of HBM per device.

```python
import jax
import jax.numpy as jnp
from jax import lax

FC = 8192
FR = 12288
PANEL = 256
BLK = 128
CPAN = 2
RPAN = 3
NEWTON = 4
N_ROW = 8
N_COL = 16


def assemble_front(off_diagonal, diagonal, total_rows, order):
    row_of = jnp.arange(total_rows)[:, None] % order
    col_of = jnp.arange(order)[None, :]
    return jnp.where(row_of == col_of, diagonal, off_diagonal)


def draw_child_fronts(key, part):
    key = jax.random.fold_in(key, 1)
    noise_key, diag_key = jax.random.split(key, 2)
    off_diagonal = jnp.clip(0.75 * jax.random.normal(noise_key, (2 * FC, FC), jnp.float32), -3.0, 3.0)
    diagonal = jax.random.uniform(diag_key, (2 * FC, 1), jnp.float32, 14.0, 28.0)
    return assemble_front(off_diagonal, diagonal, 2 * FC, FC)


def draw_root_front(key, part):
    key = jax.random.fold_in(key, 2)
    noise_key, diag_key = jax.random.split(key, 2)
    off_diagonal = jnp.clip(0.75 * jax.random.normal(noise_key, (FR, FR), jnp.float32), -3.0, 3.0)
    diagonal = jax.random.uniform(diag_key, (FR, 1), jnp.float32, 14.0, 28.0)
    return assemble_front(off_diagonal, diagonal, FR, FR)


def draw_child_map(key, part):
    key = jax.random.fold_in(key, 3)
    step_key, start_key = jax.random.split(key, 2)
    root_blocks = FR // BLK
    count = (FC - CPAN * PANEL) // BLK
    limit = root_blocks - count
    first = FC // BLK // (N_ROW // 2) - CPAN * PANEL // BLK
    run_length = (N_COL - 2) // 2
    extras = jax.random.randint(step_key, (2, count), 0, 2)
    extras = extras.at[:, 0].set(0)
    places = jnp.arange(count)
    forced = jnp.where(places == first + 1, 0, jnp.where((places >= first + 2) & (places <= first + 1 + run_length), 1, jnp.where((places == first + 2 + run_length) | (places == first + 3 + run_length), 0, -1)))
    leading = jnp.where(forced >= 0, forced, extras[0])
    before = jnp.sum(jnp.where(places < first, leading, 0))
    leading = jnp.where(places == first, (first + before) % 2, leading)
    extras = extras.at[0].set(leading)
    rising = places[None, :] + jnp.minimum(jnp.cumsum(extras, axis=1), limit)
    room = root_blocks - rising[:, -1:]
    starts = 2 * jax.random.randint(start_key, (2, 1), 0, (room + 1) // 2)
    cyclic = starts + rising
    per_device = root_blocks // N_COL
    return (cyclic % N_COL * per_device + cyclic // N_COL).astype(jnp.int32)


def draw_panel_order(key, part):
    key = jax.random.fold_in(key, 4)
    perm_key, place_key = jax.random.split(key, 2)
    last_panel = FR // PANEL - 1
    others = jax.random.permutation(perm_key, last_panel)[:RPAN - 1].astype(jnp.int32)
    others = jnp.concatenate([others, jnp.zeros((1,), jnp.int32)])
    where_last = jax.random.randint(place_key, (), 0, RPAN)
    places = jnp.arange(RPAN)
    shifted = jnp.clip(places - 1, 0, RPAN - 1)
    picked = jnp.where(places < where_last, others[places], others[shifted])
    return jnp.where(places == where_last, last_panel, picked).astype(jnp.int32)


def setup_inputs(seed: int = 0) -> dict:
    key_list = jax.random.split(jax.random.key(seed), 5)
    return {
        "child_fronts": draw_child_fronts(jax.random.fold_in(key_list[4], 71), 0),
        "root_front": draw_root_front(jax.random.fold_in(key_list[4], 71), 0),
        "child_map": draw_child_map(jax.random.fold_in(key_list[4], 71), 0),
        "panel_order": draw_panel_order(jax.random.fold_in(key_list[4], 71), 0),
    }


highest = lax.Precision.HIGHEST


def newton(pivot_block):
    identity = jnp.eye(pivot_block.shape[0], dtype=jnp.float32)
    inverse = jnp.diag(1.0 / jnp.diagonal(pivot_block))
    for sweep in range(NEWTON):
        inverse = jnp.dot(inverse, 2.0 * identity - jnp.dot(pivot_block, inverse, precision=highest), precision=highest)
    return inverse


def pivot_step(matrix, panel_start, remaining):
    column_band = lax.dynamic_slice_in_dim(matrix, panel_start, PANEL, 1)
    row_band = lax.dynamic_slice_in_dim(matrix, panel_start, PANEL, 0)
    pivot_block = lax.dynamic_slice_in_dim(row_band, panel_start, PANEL, 1)
    factor_cols = jnp.where(remaining[:, None], jnp.dot(column_band, newton(pivot_block), precision=highest), 0.0)
    factor_rows = jnp.where(remaining[None, :], row_band, 0.0)
    updated = matrix - jnp.dot(factor_cols, factor_rows, precision=highest)
    kept = lax.dynamic_slice_in_dim(updated, panel_start, PANEL, 1)
    return lax.dynamic_update_slice_in_dim(updated, jnp.where(remaining[:, None], factor_cols, kept), panel_start, 1)


def reference(child_fronts, root_front, child_map, panel_order):
    child_index = jnp.arange(FC)
    results = []
    for which in range(2):
        matrix = child_fronts[which * FC:(which + 1) * FC]
        for column_step in range(CPAN):
            matrix = pivot_step(matrix, jnp.int32(column_step * PANEL), child_index >= (column_step + 1) * PANEL)
        results.append(matrix)
    factors = jnp.concatenate(results, 0)
    skip_rows = CPAN * PANEL
    count = (FC - skip_rows) // BLK
    root_blocks = FR // BLK
    assembled = root_front.reshape(root_blocks, BLK, root_blocks, BLK)
    for which in range(2):
        schur = results[which][skip_rows:, skip_rows:].reshape(count, BLK, count, BLK).transpose(0, 2, 1, 3)
        targets = child_map[which]
        assembled = assembled.at[targets[:, None], :, targets[None, :], :].add(schur)
    matrix = assembled.reshape(FR, FR)
    panel_of = (jnp.arange(FR) // PANEL).astype(jnp.int32)
    for column_step in range(RPAN):
        remaining = jnp.all(panel_of[:, None] != panel_order[None, :column_step + 1], axis=1)
        matrix = pivot_step(matrix, (panel_order[column_step] * PANEL).astype(jnp.int32), remaining)
    return factors, matrix
```

```python
import functools

import jax
import jax.numpy as jnp
from jax import lax
from jax.experimental import pallas as pl
from jax.experimental.pallas import tpu as pltpu
from jax.sharding import Mesh
from jax.sharding import PartitionSpec as P

PANEL = 256
BLK = 128
CPAN = 2
RPAN = 3
NEWTON = 4


ROW = ("y", "core")
COL = ("x", "z")
MESH = pl.DeviceIdType.MESH

highest = lax.Precision.HIGHEST


def broadcast(block, axis, source):
    block = jnp.where(lax.axis_index(axis) == source, block, jnp.zeros_like(block))
    return lax.psum(block, axis)


def newton(pivot_block):
    identity = jnp.eye(pivot_block.shape[0], dtype=jnp.float32)
    inverse = jnp.diag(1.0 / jnp.diagonal(pivot_block))
    for sweep in range(NEWTON):
        inverse = jnp.dot(
            inverse,
            2.0 * identity - jnp.dot(pivot_block, inverse, precision=highest),
            precision=highest,
        )
    return inverse


def fetch_rows(row_band, is_source, slot_count, slot_index):
    selector = (jnp.arange(slot_count) == slot_index).astype(jnp.float32)
    contrib = selector[:, None, None] * jnp.where(is_source, row_band, 0.0)[None]
    totals = lax.psum(contrib, ROW)
    return lax.dynamic_index_in_dim(totals, slot_index, 0, keepdims=False)


def multipliers(matrix, pivot_band, plan_entry):
    column_band = lax.dynamic_slice_in_dim(matrix, plan_entry["col_off"], PANEL, 1)
    pivot_block = lax.dynamic_slice_in_dim(pivot_band, plan_entry["col_off"], PANEL, 1)
    column_band, pivot_block = (
        broadcast(column_band, COL, plan_entry["col_owner"]),
        broadcast(pivot_block, COL, plan_entry["col_owner"]),
    )
    factor_cols = jnp.dot(column_band, newton(pivot_block), precision=highest)
    factor_cols = jnp.where(plan_entry["rest_rows"][:, None], factor_cols, 0.0)
    factor_rows = jnp.where(plan_entry["rest_cols"][None, :], pivot_band, 0.0)
    return (factor_cols, factor_rows)


def apply_update(row_band, factor_part, factor_rows, rest_part, plan_entry):
    updated = row_band - jnp.dot(factor_part, factor_rows, precision=highest)
    column_band = lax.dynamic_slice_in_dim(updated, plan_entry["col_off"], PANEL, 1)
    rewritten = lax.dynamic_update_slice_in_dim(
        updated, jnp.where(rest_part[:, None], factor_part, column_band), plan_entry["col_off"], 1
    )
    return jnp.where(plan_entry["col_mine"], rewritten, updated)


def eliminate(matrix, plan, slot_count, slot_index):
    for plan_entry in plan:
        row_band = lax.dynamic_slice_in_dim(matrix, plan_entry["row_off"], PANEL, 0)
        pivot_band = fetch_rows(row_band, plan_entry["row_mine"], slot_count, slot_index)
        factor_cols, factor_rows = multipliers(matrix, pivot_band, plan_entry)
        matrix = apply_update(matrix, factor_cols, factor_rows, plan_entry["rest_rows"], plan_entry)
    return matrix


def peers_of(axes):
    if axes == ROW:
        me = 2 * lax.axis_index("y") + lax.axis_index("core")
        return me, 8, lambda p: {"y": p // 2, "core": lax.rem(p, 2)}
    return lax.axis_index(axes), 4, lambda p: {axes: p}


def exchange(arrays, axes, collective_id):
    n = len(arrays)

    def kernel(*refs):
        ins, outs = refs[:n], refs[n : 2 * n]
        send_sem, recv_sem, own_sem = refs[2 * n :]
        barrier = pltpu.get_barrier_semaphore()
        total = 0
        for ax in axes:
            me, size, ident = peers_of(ax)
            for d in range(1, size):
                pl.semaphore_signal(
                    barrier, inc=1, device_id=ident(lax.rem(me + d, size)), device_id_type=MESH
                )
            total += size - 1
        own = []
        for i, ax in enumerate(axes):
            me, size, ident = peers_of(ax)
            copy = pltpu.make_async_copy(ins[i].at[me], outs[i].at[me], own_sem.at[i])
            copy.start()
            own.append(copy)
        pl.semaphore_wait(barrier, total)
        copies = []
        for i, ax in enumerate(axes):
            me, size, ident = peers_of(ax)
            for d in sorted(range(1, size), key=lambda d: -min(d, size - d)):
                p = lax.rem(me + d, size)
                copy = pltpu.make_async_remote_copy(
                    src_ref=ins[i].at[p],
                    dst_ref=outs[i].at[me],
                    send_sem=send_sem.at[i, d],
                    recv_sem=recv_sem.at[i, d],
                    device_id=ident(p),
                    device_id_type=MESH,
                )
                copy.start()
                copies.append(copy)
        for copy in own + copies:
            copy.wait()

    return pl.pallas_call(
        kernel,
        out_shape=[jax.ShapeDtypeStruct(a.shape, a.dtype) for a in arrays],
        in_specs=[pl.BlockSpec(memory_space=pl.ANY)] * n,
        out_specs=[pl.BlockSpec(memory_space=pl.ANY)] * n,
        scratch_shapes=[
            pltpu.SemaphoreType.DMA((n, 8)),
            pltpu.SemaphoreType.DMA((n, 8)),
            pltpu.SemaphoreType.DMA((n,)),
        ],
        compiler_params=pltpu.CompilerParams(collective_id=collective_id, has_side_effects=True),
    )(*arrays)


def rank_in(key, group, valid):
    n = key.shape[1]
    earlier = jnp.arange(n)[None, :] < jnp.arange(n)[:, None]
    same = (key[:, :, None] == key[:, None, :]) & (group[:, None] == group[None, :])[None]
    return jnp.sum((same & valid[:, None, :] & earlier[None]).astype(jnp.int32), axis=2)


def find(match, value):
    return jnp.sum(jnp.where(match, value + 1, 0), axis=-1) - 1


def routes(child_map):
    y, core = lax.axis_index("y"), lax.axis_index("core")
    x, z = lax.axis_index("x"), lax.axis_index("z")
    my_child, within = y // 2, lax.rem(y, 2) * 2 + core
    r, o = 2 * y + core, 4 * x + z
    blocks = jnp.arange(64)
    skip = CPAN * PANEL // BLK
    cyclic = (child_map % 6) * 16 + child_map // 6
    t = jnp.concatenate([jnp.zeros((2, skip), jnp.int32), cyclic], axis=1)
    valid = jnp.broadcast_to(blocks >= skip, (2, 64))
    kz = rank_in(t % 4, blocks // 4, valid)
    kx = rank_in(t % 16, blocks // 16, valid)
    kr = rank_in(t % 16 // 2, blocks // 16, valid)
    four, two = jnp.arange(4), jnp.arange(2)

    mine = valid & (blocks // 4 == o)[None]
    z_pick = find(
        mine[:, None, None]
        & ((t % 4)[:, None, None] == four[None, :, None, None])
        & (kz[:, None, None] == two[None, None, :, None]),
        blocks % 4,
    )
    mine = valid & (blocks // 16 == x)[None] & (t % 4 == z)
    x_pick = find(
        mine[:, None, None]
        & ((t % 16 // 4)[:, None, None] == four[None, :, None, None])
        & (kx[:, None, None] == two[None, None, :, None]),
        ((blocks // 4 % 4)[None] * 2 + kz)[:, None, None],
    )
    slots = jnp.arange(6)
    col_from = find(
        valid[:, None] & (t[:, None] == (slots * 16 + o)[None, :, None]),
        ((blocks // 16)[None] * 2 + kx)[:, None],
    )
    mine = valid & (blocks // 16 == within)[None]
    own = lambda a: lax.dynamic_index_in_dim(a, my_child, 0, keepdims=False)
    r_pick = find(
        own(mine)[None, None]
        & (own(t % 16 // 2)[None, None] == jnp.arange(8)[:, None, None])
        & (own(kr)[None, None] == four[None, :, None]),
        blocks % 16,
    )
    slots = jnp.arange(12)
    row_from = find(
        valid[:, None] & (t[:, None] == (slots % 6 * 16 + 2 * r + slots // 6)[None, :, None]),
        ((jnp.arange(2)[:, None] * 4 + (blocks // 16)[None]) * 4 + kr)[:, None],
    )
    return own(z_pick), z_pick, x_pick, own(x_pick), col_from, own(col_from), r_pick, row_from


Z_OWN, Z_PICK, X_PICK, X_OWN, COL_FROM, COL_OWN, R_PICK, ROW_FROM = 0, 8, 24, 40, 48, 60, 66, 98


def whole(shape):
    return pl.BlockSpec(shape, lambda g, tab: (0,) * len(shape))


def part(shape):
    return pl.BlockSpec((1,) + shape, lambda g, tab: (g,) + (0,) * len(shape))


def local_call(kernel, grid, table, operands, in_specs, out_shapes, out_specs):
    return pl.pallas_call(
        kernel,
        grid_spec=pltpu.PrefetchScalarGridSpec(
            num_scalar_prefetch=1, grid=(grid,), in_specs=in_specs, out_specs=out_specs
        ),
        out_shape=[jax.ShapeDtypeStruct(s, jnp.float32) for s in out_shapes],
        compiler_params=pltpu.CompilerParams(vmem_limit_bytes=56 * 1024 * 1024),
    )(table, *operands)


def at_least_zero(v):
    return jnp.maximum(v, 0)


def lanes(block):
    return pl.ds(pl.multiple_of(block * BLK, BLK), BLK)


def pack_first(tab, front, za, yb):
    g = pl.program_id(0)
    za[0] = front[:, 0:64, lanes(at_least_zero(tab[Z_OWN + g]))]
    for k in range(4):
        yb[0, k] = front[at_least_zero(tab[R_PICK + g * 4 + k]), 64:128, :]


def pack_second(tab, zin, yin, xa, zb):
    g = pl.program_id(0)
    xa[0] = zin[at_least_zero(tab[X_OWN + g])]
    for c in range(2):
        column = lanes(at_least_zero(tab[Z_PICK + c * 8 + g]))
        for i in range(12):
            source = at_least_zero(tab[ROW_FROM + c * 12 + i])
            zb[0, c * 12 + i] = yin[source, :, column]


def pack_third(tab, xin, zin, ya, xb):
    g = pl.program_id(0)
    for c in range(2):
        source = at_least_zero(tab[X_PICK + c * 8 + g])
        xb[0, c * 12 : c * 12 + 12] = zin[source, c * 12 : c * 12 + 12]
    for k in range(4):
        i = at_least_zero(tab[R_PICK + g * 4 + k])
        for slot in range(6):
            source = at_least_zero(tab[COL_OWN + slot])
            ya[0, k, :, slot * BLK : slot * BLK + BLK] = xin[source, i]


def add_all(tab, root, yin, xin, out):
    i = pl.program_id(0)
    for slot in range(6):
        columns = slice(slot * BLK, slot * BLK + BLK)
        upper, lower = root[0, 0:64, columns], root[0, 64:128, columns]
        for c in range(2):
            row, col = tab[ROW_FROM + c * 12 + i], tab[COL_FROM + c * 6 + slot]
            there = jnp.logical_and(row >= 0, col >= 0)
            upper += jnp.where(there, yin[at_least_zero(row), :, columns], 0.0)
            lower += jnp.where(there, xin[at_least_zero(col), c * 12 + i], 0.0)
        out[0, 0:64, columns] = upper
        out[0, 64:128, columns] = lower


def extend_add(factored, root_front, child_map):
    table = jnp.concatenate([a.reshape(-1) for a in routes(child_map)])
    front = factored.reshape(16, BLK, 512)
    za, yb = local_call(
        pack_first, 8, table, (front,), [whole((16, BLK, 512))],
        [(8, 16, 64, BLK), (8, 4, 64, 512)], [part((16, 64, BLK)), part((4, 64, 512))],
    )
    za, yb = exchange([za.reshape(4, 2, 16, 64, BLK), yb], ["z", ROW], 1)
    xa, zb = local_call(
        pack_second, 8, table, (za.reshape(8, 16, 64, BLK), yb.reshape(32, 64, 512)),
        [whole((8, 16, 64, BLK)), whole((32, 64, 512))],
        [(8, 16, 64, BLK), (8, 24, 64, BLK)], [part((16, 64, BLK)), part((24, 64, BLK))],
    )
    xa, zb = exchange(
        [xa.reshape(4, 2, 16, 64, BLK), zb.reshape(4, 2, 24, 64, BLK)], ["x", "z"], 2
    )
    ya, xb = local_call(
        pack_third, 8, table, (xa.reshape(8, 16, 64, BLK), zb.reshape(8, 24, 64, BLK)),
        [whole((8, 16, 64, BLK)), whole((8, 24, 64, BLK))],
        [(8, 4, 64, 768), (8, 24, 64, BLK)], [part((4, 64, 768)), part((24, 64, BLK))],
    )
    ya, xb = exchange([ya, xb.reshape(4, 2, 24, 64, BLK)], [ROW, "x"], 3)
    (assembled,) = local_call(
        add_all, 12, table,
        (root_front.reshape(12, BLK, 768), ya.reshape(32, 64, 768), xb.reshape(8, 24, 64, BLK)),
        [part((BLK, 768)), whole((32, 64, 768)), whole((8, 24, 64, BLK))],
        [(12, BLK, 768)], [part((BLK, 768))],
    )
    return assembled.reshape(root_front.shape)


def body(child_fronts, root_front, child_map, panel_order):
    row_count = lax.axis_size(ROW)
    col_count = lax.axis_size(COL)
    my_row = lax.axis_index(ROW)
    my_col = lax.axis_index(COL)
    group_size = row_count // 2
    child_index = my_row // group_size
    within = my_row % group_size
    row_len, col_len = child_fronts.shape
    row_index = within * row_len + jnp.arange(row_len)
    col_index = my_col * col_len + jnp.arange(col_len)
    child_plan = []
    for column_step in range(CPAN):
        panel_start = column_step * PANEL
        child_plan.append(
            {
                "row_off": panel_start % row_len,
                "row_mine": within == panel_start // row_len,
                "col_off": panel_start % col_len,
                "col_owner": panel_start // col_len,
                "col_mine": my_col == panel_start // col_len,
                "rest_rows": row_index >= panel_start + PANEL,
                "rest_cols": col_index >= panel_start + PANEL,
            }
        )
    factored = eliminate(child_fronts, child_plan, 2, child_index)
    root_rows, root_cols = root_front.shape
    assembled = extend_add(factored, root_front, child_map)
    root_row_index = my_row * root_rows + jnp.arange(root_rows)
    root_col_index = my_col * root_cols + jnp.arange(root_cols)
    root_plan = []
    for column_step in range(RPAN):
        panel_start = panel_order[column_step] * PANEL
        done_panels = panel_order[: column_step + 1]
        root_plan.append(
            {
                "row_off": panel_start % root_rows,
                "row_mine": my_row == panel_start // root_rows,
                "col_off": panel_start % root_cols,
                "col_owner": panel_start // root_cols,
                "col_mine": my_col == panel_start // root_cols,
                "rest_rows": jnp.all(
                    (root_row_index // PANEL)[:, None] != done_panels[None, :], axis=1
                ),
                "rest_cols": jnp.all(
                    (root_col_index // PANEL)[:, None] != done_panels[None, :], axis=1
                ),
            }
        )
    return (factored, eliminate(assembled, root_plan, 1, 0))


def solution(mesh):
    grid = Mesh(mesh.devices.reshape(4, 2, 4, 4), ("y", "core", "x", "z"))
    return jax.shard_map(
        body,
        mesh=grid,
        in_specs=(P(ROW, COL), P(ROW, COL), P(), P()),
        out_specs=(P(ROW, COL), P(ROW, COL)),
        check_vma=False,
    )
```

```python
import functools

import jax
import jax.numpy as jnp
from jax import lax
from jax.experimental import pallas as pl
from jax.experimental.pallas import tpu as pltpu
from jax.sharding import Mesh
from jax.sharding import PartitionSpec as P

PANEL = 256
BLK = 128
CPAN = 2
RPAN = 3

ROW = ("y", "core")
COL = ("x", "z")
MESH = pl.DeviceIdType.MESH
NEVER = 99

HIGH = lax.Precision.HIGH
HIGHEST = lax.Precision.HIGHEST


def peers_of(axes):
    y, core = lax.axis_index("y"), lax.axis_index("core")
    if axes == ROW:
        return 2 * y + core, 8, lambda p: {"y": p // 2, "core": lax.rem(p, 2)}
    if axes == "child":
        pair = y // 2 * 2
        me = lax.rem(y, 2) * 2 + core
        return me, 4, lambda p: {"y": pair + p // 2, "core": lax.rem(p, 2)}
    return lax.axis_index(axes), 4, lambda p: {axes: p}


def swap(array, axes):
    return (array, axes, lambda ref, p: ref.at[p], lambda ref, p: ref.at[p], array.shape)


def swap_inner(array, axes):
    shape = (array.shape[1], array.shape[0]) + array.shape[2:]
    return (array, axes, lambda ref, p: ref.at[:, p], lambda ref, p: ref.at[p], shape)


def swap_half(array, axes, half):
    return (
        array, axes, lambda ref, p: ref.at[half, p], lambda ref, p: ref.at[p], array.shape[1:]
    )


def share(array, axes, size):
    return (array, axes, lambda ref, p: ref, lambda ref, p: ref.at[p], (size,) + array.shape)


def share_inner(array, axes, size):
    shape = (array.shape[0], size) + array.shape[1:]
    return (array, axes, lambda ref, p: ref, lambda ref, p: ref.at[:, p], shape)


def exchange(moves, collective_id):
    n = len(moves)
    greeted = list(dict.fromkeys(m[1] for m in moves))

    def kernel(*refs):
        ins, outs = refs[:n], refs[n : 2 * n]
        send_sem, recv_sem, own_sem = refs[2 * n :]
        barrier = pltpu.get_barrier_semaphore()
        total = 0
        for ax in greeted:
            me, size, ident = peers_of(ax)
            for d in range(1, size):
                pl.semaphore_signal(
                    barrier, inc=1, device_id=ident(lax.rem(me + d, size)), device_id_type=MESH
                )
            total += size - 1
        own = []
        for i, (_, ax, src, dst, _) in enumerate(moves):
            me = peers_of(ax)[0]
            copy = pltpu.make_async_copy(src(ins[i], me), dst(outs[i], me), own_sem.at[i])
            copy.start()
            own.append(copy)
        pl.semaphore_wait(barrier, total)
        copies = []
        for i, (_, ax, src, dst, _) in enumerate(moves):
            me, size, ident = peers_of(ax)
            for d in sorted(range(1, size), key=lambda d: -min(d, size - d)):
                p = lax.rem(me + d, size)
                copy = pltpu.make_async_remote_copy(
                    src_ref=src(ins[i], p),
                    dst_ref=dst(outs[i], me),
                    send_sem=send_sem.at[i, d],
                    recv_sem=recv_sem.at[i, d],
                    device_id=ident(p),
                    device_id_type=MESH,
                )
                copy.start()
                copies.append(copy)
        for copy in own + copies:
            copy.wait()

    return pl.pallas_call(
        kernel,
        out_shape=[jax.ShapeDtypeStruct(m[4], jnp.float32) for m in moves],
        in_specs=[pl.BlockSpec(memory_space=pl.ANY)] * n,
        out_specs=[pl.BlockSpec(memory_space=pl.ANY)] * n,
        scratch_shapes=[
            pltpu.SemaphoreType.DMA((n, 8)),
            pltpu.SemaphoreType.DMA((n, 8)),
            pltpu.SemaphoreType.DMA((n,)),
        ],
        compiler_params=pltpu.CompilerParams(collective_id=collective_id, has_side_effects=True),
    )(*[m[0] for m in moves])


def rank_in(key, group, valid):
    n = key.shape[1]
    earlier = jnp.arange(n)[None, :] < jnp.arange(n)[:, None]
    same = (key[:, :, None] == key[:, None, :]) & (group[:, None] == group[None, :])[None]
    return jnp.sum((same & valid[:, None, :] & earlier[None]).astype(jnp.int32), axis=2)


def find(match, value):
    return jnp.sum(jnp.where(match, value + 1, 0), axis=-1) - 1


def routes(child_map):
    y, core = lax.axis_index("y"), lax.axis_index("core")
    x, z = lax.axis_index("x"), lax.axis_index("z")
    my_child, within = y // 2, lax.rem(y, 2) * 2 + core
    r, o = 2 * y + core, 4 * x + z
    blocks = jnp.arange(64)
    skip = CPAN * PANEL // BLK
    cyclic = (child_map % 6) * 16 + child_map // 6
    t = jnp.concatenate([jnp.zeros((2, skip), jnp.int32), cyclic], axis=1)
    valid = jnp.broadcast_to(blocks >= skip, (2, 64))
    kz = rank_in(t % 4, blocks // 4, valid)
    kx = rank_in(t % 16, blocks // 16, valid)
    kr = rank_in(t % 16 // 2, blocks // 16, valid)
    four, two = jnp.arange(4), jnp.arange(2)

    mine = valid & (blocks // 4 == o)[None]
    z_pick = find(
        mine[:, None, None]
        & ((t % 4)[:, None, None] == four[None, :, None, None])
        & (kz[:, None, None] == two[None, None, :, None]),
        blocks % 4,
    )
    mine = valid & (blocks // 16 == x)[None] & (t % 4 == z)
    x_pick = find(
        mine[:, None, None]
        & ((t % 16 // 4)[:, None, None] == four[None, :, None, None])
        & (kx[:, None, None] == two[None, None, :, None]),
        ((blocks // 4 % 4)[None] * 2 + kz)[:, None, None],
    )
    slots = jnp.arange(6)
    col_from = find(
        valid[:, None] & (t[:, None] == (slots * 16 + o)[None, :, None]),
        ((blocks // 16)[None] * 2 + kx)[:, None],
    )
    mine = valid & (blocks // 16 == within)[None]
    own = lambda a: lax.dynamic_index_in_dim(a, my_child, 0, keepdims=False)
    r_pick = find(
        own(mine)[None, None]
        & (own(t % 16 // 2)[None, None] == jnp.arange(8)[:, None, None])
        & (own(kr)[None, None] == four[None, :, None]),
        blocks % 16,
    )
    slots = jnp.arange(12)
    row_from = find(
        valid[:, None] & (t[:, None] == (slots % 6 * 16 + 2 * r + slots // 6)[None, :, None]),
        ((jnp.arange(2)[:, None] * 4 + (blocks // 16)[None]) * 4 + kr)[:, None],
    )
    return own(z_pick), z_pick, x_pick, own(x_pick), col_from, own(col_from), r_pick, row_from


Z_OWN, Z_PICK, X_PICK, X_OWN, COL_FROM, COL_OWN, R_PICK, ROW_FROM = 0, 8, 24, 40, 48, 60, 66, 98


def whole(shape):
    return pl.BlockSpec(shape, lambda g, tab: (0,) * len(shape))


def part(shape):
    return pl.BlockSpec((1,) + shape, lambda g, tab: (g,) + (0,) * len(shape))


def local_call(kernel, grid, table, operands, in_specs, out_shapes, out_specs, scratch=()):
    return pl.pallas_call(
        kernel,
        grid_spec=pltpu.PrefetchScalarGridSpec(
            num_scalar_prefetch=1, grid=(grid,), in_specs=in_specs, out_specs=out_specs,
            scratch_shapes=list(scratch),
        ),
        out_shape=[jax.ShapeDtypeStruct(s, jnp.float32) for s in out_shapes],
        compiler_params=pltpu.CompilerParams(vmem_limit_bytes=56 * 1024 * 1024),
    )(table, *operands)


def at_least_zero(v):
    return jnp.maximum(v, 0)


def lanes(block):
    return pl.ds(pl.multiple_of(block * BLK, BLK), BLK)


def pack_first(tab, front, za, yb):
    g = pl.program_id(0)
    za[0] = front[:, 0:64, lanes(at_least_zero(tab[Z_OWN + g]))]
    for k in range(4):
        yb[0, k] = front[at_least_zero(tab[R_PICK + g * 4 + k]), 64:128, :]


def pack_second(tab, zin, yin, xa, zb):
    g = pl.program_id(0)
    xa[0] = zin[at_least_zero(tab[X_OWN + g])]
    for c in range(2):
        column = lanes(at_least_zero(tab[Z_PICK + c * 8 + g]))
        for i in range(12):
            source = at_least_zero(tab[ROW_FROM + c * 12 + i])
            zb[0, c * 12 + i] = yin[source, :, column]


def pack_third(tab, xin, zin, ya, xb):
    g = pl.program_id(0)
    for c in range(2):
        source = at_least_zero(tab[X_PICK + c * 8 + g])
        xb[0, c * 12 : c * 12 + 12] = zin[source, c * 12 : c * 12 + 12]
    for k in range(4):
        i = at_least_zero(tab[R_PICK + g * 4 + k])
        for slot in range(6):
            source = at_least_zero(tab[COL_OWN + slot])
            ya[0, k, :, slot * BLK : slot * BLK + BLK] = xin[source, i]


def add_all(tab, root, yin, xin, out):
    i = pl.program_id(0)
    for slot in range(6):
        columns = slice(slot * BLK, slot * BLK + BLK)
        upper, lower = root[0, 0:64, columns], root[0, 64:128, columns]
        for c in range(2):
            row, col = tab[ROW_FROM + c * 12 + i], tab[COL_FROM + c * 6 + slot]
            there = jnp.logical_and(row >= 0, col >= 0)
            upper += jnp.where(there, yin[at_least_zero(row), :, columns], 0.0)
            lower += jnp.where(there, xin[at_least_zero(col), c * 12 + i], 0.0)
        out[0, 0:64, columns] = upper
        out[0, 64:128, columns] = lower


def extend_add(factored, root_front, child_map):
    table = jnp.concatenate([a.reshape(-1) for a in routes(child_map)])
    front = factored.reshape(16, BLK, 512)
    za, yb = local_call(
        pack_first, 8, table, (front,), [whole((16, BLK, 512))],
        [(8, 16, 64, BLK), (8, 4, 64, 512)], [part((16, 64, BLK)), part((4, 64, 512))],
    )
    za, yb = exchange([swap(za.reshape(4, 2, 16, 64, BLK), "z"), swap(yb, ROW)], 1)
    xa, zb = local_call(
        pack_second, 8, table, (za.reshape(8, 16, 64, BLK), yb.reshape(32, 64, 512)),
        [whole((8, 16, 64, BLK)), whole((32, 64, 512))],
        [(8, 16, 64, BLK), (8, 24, 64, BLK)], [part((16, 64, BLK)), part((24, 64, BLK))],
    )
    xa, zb = exchange(
        [swap(xa.reshape(4, 2, 16, 64, BLK), "x"), swap(zb.reshape(4, 2, 24, 64, BLK), "z")], 2
    )
    ya, xb = local_call(
        pack_third, 8, table, (xa.reshape(8, 16, 64, BLK), zb.reshape(8, 24, 64, BLK)),
        [whole((8, 16, 64, BLK)), whole((8, 24, 64, BLK))],
        [(8, 4, 64, 768), (8, 24, 64, BLK)], [part((4, 64, 768)), part((24, 64, BLK))],
    )
    ya, xb = exchange([swap(ya, ROW), swap(xb.reshape(4, 2, 24, 64, BLK), "x")], 3)
    (assembled,) = local_call(
        add_all, 12, table,
        (root_front.reshape(12, BLK, 768), ya.reshape(32, 64, 768), xb.reshape(8, 24, 64, BLK)),
        [part((BLK, 768)), whole((32, 64, 768)), whole((8, 24, 64, BLK))],
        [(12, BLK, 768)], [part((BLK, 768))],
    )
    return assembled.reshape(root_front.shape)


def pick(arrived, owners):
    parts = [
        lax.dynamic_index_in_dim(arrived[..., q * PANEL : (q + 1) * PANEL], owner, 0, keepdims=False)
        for q, owner in enumerate(owners)
    ]
    return jnp.concatenate(parts, axis=-1)


def gather_bands(cols, rows, col_off, xs, zs, row_owners, axes, size, first_id):
    count, width = cols.shape
    panels, _, span = rows.shape
    piece = PANEL // size
    cols = cols.reshape(2, 4, count // 8, width)
    rows = rows.reshape(panels, size, piece, span)
    first, second, slices = exchange(
        [swap_half(cols, "z", 0), swap_half(cols, "x", 1), swap_inner(rows, axes)], first_id
    )
    first, second = pick(first, zs), pick(second, xs)
    slices = jnp.stack(
        [lax.dynamic_index_in_dim(slices[:, k], owner, 0, keepdims=False) for k, owner in enumerate(row_owners)]
    )
    cross = jnp.concatenate(
        [lax.dynamic_slice_in_dim(slices, off, PANEL, 2) for off in col_off], axis=2
    )
    split = lambda a: a.reshape(4, count // 32, width)
    half = span // 2
    first, second, cross, left = exchange(
        [
            swap(split(first), "x"), swap(split(second), "z"), share(cross, "z", 4),
            share_inner(slices[..., :half], axes, size),
        ],
        first_id + 1,
    )
    first, second, cross = pick(first, xs), pick(second, zs), pick(cross, zs)
    first, second, cross, right = exchange(
        [
            share(first, "x", 4), share(second, "z", 4), share(cross, "x", 4),
            share_inner(slices[..., half:], axes, size),
        ],
        first_id + 2,
    )
    cross = pick(cross, xs)
    join = lambda a: a.reshape(count // 8, width)
    first, second, cross = exchange(
        [share(join(first), "z", 4), share(join(second), "x", 4), share_inner(cross, axes, size)],
        first_id + 3,
    )
    halves = [a.reshape(count // 2, width) for a in (first, second)]
    left, right = (a.reshape(width, half) for a in (left, right))
    return halves, left, right, cross.reshape(width, width)


def dot(a, b, precision=HIGH):
    return jnp.dot(a, b, precision=precision, preferred_element_type=jnp.float32)


def newton(block):
    shape = (PANEL, PANEL)
    eye = lax.broadcasted_iota(jnp.int32, shape, 0) == lax.broadcasted_iota(jnp.int32, shape, 1)
    kept = jnp.where(eye, block, 0.0)
    by_col = 1.0 / jnp.sum(kept, axis=0, keepdims=True)
    by_row = 1.0 / jnp.sum(kept, axis=1, keepdims=True)
    identity = jnp.where(eye, 1.0, 0.0)
    error = identity - block * by_col
    product = identity + error
    for _ in range(3):
        error = dot(error, error, HIGHEST)
        product = product + dot(product, error, HIGHEST)
    return product * by_row


def panel(k):
    return slice(k * PANEL, (k + 1) * PANEL)


def finish_kernel(n, row_panels, col_panels, precision, tab, front, upper, lower, left, right, cross, out,
                  work, inverse, pivots):
    g = pl.program_id(0)

    @pl.when(g == 0)
    def _():
        work[...] = cross[...]
        span = left.shape[1]
        pivots[:, :span] = left[...]
        pivots[:, span:] = right[...]
        for k in range(n):
            inverse[k] = newton(work[panel(k), panel(k)])
            for p in range(k + 1, n):
                factor = dot(work[panel(p), panel(k)], inverse[k], HIGHEST)
                for q in range(k + 1, n):
                    work[panel(p), panel(q)] -= dot(factor, work[panel(k), panel(q)], HIGHEST)
                pivots[panel(p), :] -= dot(factor, pivots[panel(k), :], HIGHEST)
        for j in range(col_panels):
            for k in range(n):
                pivots[panel(k), panel(j)] = jnp.where(
                    tab[row_panels + j] > k, pivots[panel(k), panel(j)], 0.0
                )

    mine = jnp.where(g < row_panels // 2, upper[...], lower[...])
    band = [mine[:, panel(k)] for k in range(n)]
    for k in range(n):
        band[k] = dot(band[k], inverse[k], HIGHEST)
        for q in range(k + 1, n):
            band[q] = band[q] - dot(band[k], work[panel(k), panel(q)], HIGHEST)
    band = [jnp.where(tab[g] > k, band[k], 0.0) for k in range(n)]
    factors = jnp.concatenate(band, axis=1)
    for j in range(col_panels):
        new = front[:, panel(j)] - dot(factors, pivots[:, panel(j)], precision)
        for k in range(n):
            here = jnp.logical_and(tab[row_panels + j] == k, tab[g] > k)
            new = jnp.where(here, band[k], new)
        out[:, panel(j)] = new


def finish(front, halves, left, right, cross, row_step, col_step, precision):
    rows, cols = front.shape
    width = cross.shape[0]
    n, row_panels, col_panels = width // PANEL, rows // PANEL, cols // PANEL
    half = row_panels // 2
    keep = lambda shape: pl.BlockSpec(shape, lambda g, tab: (0, 0))
    (out,) = local_call(
        functools.partial(finish_kernel, n, row_panels, col_panels, precision),
        row_panels,
        jnp.concatenate([row_step, col_step]).astype(jnp.int32),
        (front, *halves, left, right, cross),
        [
            pl.BlockSpec((PANEL, cols), lambda g, tab: (g, 0)),
            pl.BlockSpec((PANEL, width), lambda g, tab: (jnp.minimum(g, half - 1), 0)),
            pl.BlockSpec((PANEL, width), lambda g, tab: (jnp.maximum(g - half, 0), 0)),
            keep(left.shape), keep(right.shape), keep(cross.shape),
        ],
        [front.shape],
        [pl.BlockSpec((PANEL, cols), lambda g, tab: (g, 0))],
        scratch=[
            pltpu.VMEM((width, width), jnp.float32),
            pltpu.VMEM((n, PANEL, PANEL), jnp.float32),
            pltpu.VMEM((width, cols), jnp.float32),
        ],
    )
    return out


def body(child_fronts, root_front, child_map, panel_order):
    y, core = lax.axis_index("y"), lax.axis_index("core")
    r, o = 2 * y + core, 4 * lax.axis_index("x") + lax.axis_index("z")
    within = lax.rem(y, 2) * 2 + core

    zeros = [0] * CPAN
    bands = gather_bands(
        child_fronts, child_fronts[: CPAN * PANEL].reshape(CPAN, PANEL, -1),
        [k * PANEL for k in range(CPAN)], zeros, zeros, zeros, "child", 4, 10,
    )
    row_panel, col_panel = within * 8 + jnp.arange(8), o * 2 + jnp.arange(2)
    row_step = jnp.where(row_panel < CPAN, row_panel, NEVER)
    col_step = jnp.where(col_panel < CPAN, col_panel, NEVER)
    halves, left, right, cross = bands
    factored = finish(child_fronts, halves, left, right, cross, row_step, col_step, HIGHEST)

    assembled = extend_add(factored, root_front, child_map)

    row_panels, col_panels = 6, 3
    order = [panel_order[k] for k in range(RPAN)]
    col_off = [p % col_panels * PANEL for p in order]
    row_off = [p % row_panels * PANEL for p in order]
    owner = [p // col_panels for p in order]
    cols = jnp.concatenate([lax.dynamic_slice_in_dim(assembled, off, PANEL, 1) for off in col_off], 1)
    rows = jnp.stack([lax.dynamic_slice_in_dim(assembled, off, PANEL, 0) for off in row_off])
    halves, left, right, cross = gather_bands(
        cols, rows, col_off, [c // 4 for c in owner], [c % 4 for c in owner],
        [p // row_panels for p in order], ROW, 8, 20,
    )

    def steps(places):
        match = places[:, None] == panel_order[None, :]
        return jnp.min(jnp.where(match, jnp.arange(RPAN)[None, :], NEVER), axis=1)

    row_step = steps(r * row_panels + jnp.arange(row_panels))
    col_step = steps(o * col_panels + jnp.arange(col_panels))
    return factored, finish(assembled, halves, left, right, cross, row_step, col_step, HIGH)


def solution(mesh):
    grid = Mesh(mesh.devices.reshape(4, 2, 4, 4), ("y", "core", "x", "z"))
    return jax.shard_map(
        body,
        mesh=grid,
        in_specs=(P(ROW, COL), P(ROW, COL), P(), P()),
        out_specs=(P(ROW, COL), P(ROW, COL)),
        check_vma=False,
    )
```

```python
import functools

import jax
import jax.numpy as jnp
from jax import lax
from jax.experimental import pallas as pl
from jax.experimental.pallas import tpu as pltpu
from jax.sharding import Mesh
from jax.sharding import PartitionSpec as P

PANEL = 256
BLK = 128
CPAN = 2
RPAN = 3

ROW = ("y", "core")
COL = ("x", "z")
MESH = pl.DeviceIdType.MESH
NEVER = 99

HIGH = lax.Precision.HIGH
HIGHEST = lax.Precision.HIGHEST


def peers_of(axes):
    y, core = lax.axis_index("y"), lax.axis_index("core")
    if axes == ROW:
        return 2 * y + core, 8, lambda p: {"y": p // 2, "core": lax.rem(p, 2)}
    if axes == "child":
        pair = y // 2 * 2
        me = lax.rem(y, 2) * 2 + core
        return me, 4, lambda p: {"y": pair + p // 2, "core": lax.rem(p, 2)}
    return lax.axis_index(axes), 4, lambda p: {axes: p}


def swap(array, axes):
    return (array, axes, lambda ref, p: ref.at[p], lambda ref, p: ref.at[p], array.shape, array.shape[1:])


def swap_inner(array, axes):
    shape = (array.shape[1], array.shape[0]) + array.shape[2:]
    return (array, axes, lambda ref, p: ref.at[:, p], lambda ref, p: ref.at[p], shape, shape[1:])


def swap_half(array, axes, half):
    return (
        array, axes, lambda ref, p: ref.at[half, p], lambda ref, p: ref.at[p], array.shape[1:],
        array.shape[2:],
    )


def share(array, axes, size):
    return (
        array, axes, lambda ref, p: ref, lambda ref, p: ref.at[p], (size,) + array.shape, array.shape
    )


def share_inner(array, axes, size):
    shape = (array.shape[0], size) + array.shape[1:]
    return (array, axes, lambda ref, p: ref, lambda ref, p: ref.at[:, p], shape, array.shape)


def exchange(moves, collective_id):
    n = len(moves)
    greeted = list(dict.fromkeys(m[1] for m in moves))

    def kernel(*refs):
        ins, outs = refs[:n], refs[n : 2 * n]
        send_sem, recv_sem, own_sem = refs[2 * n : 2 * n + 3]
        stages = refs[2 * n + 3 :]
        barrier = pltpu.get_barrier_semaphore()
        total = 0
        for ax in greeted:
            me, size, ident = peers_of(ax)
            for d in range(1, size):
                pl.semaphore_signal(
                    barrier, inc=1, device_id=ident(lax.rem(me + d, size)), device_id_type=MESH
                )
            total += size - 1
        loads, stores = [], []
        for i, (_, ax, src, dst, _, _) in enumerate(moves):
            me = peers_of(ax)[0]
            loads.append(pltpu.make_async_copy(src(ins[i], me), stages[i], own_sem.at[i]))
            stores.append(pltpu.make_async_copy(stages[i], dst(outs[i], me), own_sem.at[i]))
        for copy in loads:
            copy.start()
        pl.semaphore_wait(barrier, total)
        copies = []
        for i, (_, ax, src, dst, _, _) in enumerate(moves):
            me, size, ident = peers_of(ax)
            for d in sorted(range(1, size), key=lambda d: -min(d, size - d)):
                p = lax.rem(me + d, size)
                copy = pltpu.make_async_remote_copy(
                    src_ref=src(ins[i], p),
                    dst_ref=dst(outs[i], me),
                    send_sem=send_sem.at[i, d],
                    recv_sem=recv_sem.at[i, d],
                    device_id=ident(p),
                    device_id_type=MESH,
                )
                copy.start()
                copies.append(copy)
        for load, store in zip(loads, stores):
            load.wait()
            store.start()
        for copy in stores + copies:
            copy.wait()

    return pl.pallas_call(
        kernel,
        out_shape=[jax.ShapeDtypeStruct(m[4], jnp.float32) for m in moves],
        in_specs=[pl.BlockSpec(memory_space=pl.ANY)] * n,
        out_specs=[pl.BlockSpec(memory_space=pl.ANY)] * n,
        scratch_shapes=[
            pltpu.SemaphoreType.DMA((n, 8)),
            pltpu.SemaphoreType.DMA((n, 8)),
            pltpu.SemaphoreType.DMA((n,)),
            *[pltpu.VMEM(m[5], jnp.float32) for m in moves],
        ],
        compiler_params=pltpu.CompilerParams(
            collective_id=collective_id, has_side_effects=True, vmem_limit_bytes=32 * 1024 * 1024
        ),
    )(*[m[0] for m in moves])


def rank_in(key, group, valid):
    n = key.shape[1]
    earlier = jnp.arange(n)[None, :] < jnp.arange(n)[:, None]
    same = (key[:, :, None] == key[:, None, :]) & (group[:, None] == group[None, :])[None]
    return jnp.sum((same & valid[:, None, :] & earlier[None]).astype(jnp.int32), axis=2)


def find(match, value):
    return jnp.sum(jnp.where(match, value + 1, 0), axis=-1) - 1


def routes(child_map):
    y, core = lax.axis_index("y"), lax.axis_index("core")
    x, z = lax.axis_index("x"), lax.axis_index("z")
    my_child, within = y // 2, lax.rem(y, 2) * 2 + core
    r, o = 2 * y + core, 4 * x + z
    blocks = jnp.arange(64)
    skip = CPAN * PANEL // BLK
    cyclic = (child_map % 6) * 16 + child_map // 6
    t = jnp.concatenate([jnp.zeros((2, skip), jnp.int32), cyclic], axis=1)
    valid = jnp.broadcast_to(blocks >= skip, (2, 64))
    kz = rank_in(t % 4, blocks // 4, valid)
    kx = rank_in(t % 16, blocks // 16, valid)
    kr = rank_in(t % 16 // 2, blocks // 16, valid)
    four, two = jnp.arange(4), jnp.arange(2)

    mine = valid & (blocks // 4 == o)[None]
    z_pick = find(
        mine[:, None, None]
        & ((t % 4)[:, None, None] == four[None, :, None, None])
        & (kz[:, None, None] == two[None, None, :, None]),
        blocks % 4,
    )
    mine = valid & (blocks // 16 == x)[None] & (t % 4 == z)
    x_pick = find(
        mine[:, None, None]
        & ((t % 16 // 4)[:, None, None] == four[None, :, None, None])
        & (kx[:, None, None] == two[None, None, :, None]),
        ((blocks // 4 % 4)[None] * 2 + kz)[:, None, None],
    )
    slots = jnp.arange(6)
    col_from = find(
        valid[:, None] & (t[:, None] == (slots * 16 + o)[None, :, None]),
        ((blocks // 16)[None] * 2 + kx)[:, None],
    )
    mine = valid & (blocks // 16 == within)[None]
    own = lambda a: lax.dynamic_index_in_dim(a, my_child, 0, keepdims=False)
    r_pick = find(
        own(mine)[None, None]
        & (own(t % 16 // 2)[None, None] == jnp.arange(8)[:, None, None])
        & (own(kr)[None, None] == four[None, :, None]),
        blocks % 16,
    )
    slots = jnp.arange(12)
    row_from = find(
        valid[:, None] & (t[:, None] == (slots % 6 * 16 + 2 * r + slots // 6)[None, :, None]),
        ((jnp.arange(2)[:, None] * 4 + (blocks // 16)[None]) * 4 + kr)[:, None],
    )
    return own(z_pick), z_pick, x_pick, own(x_pick), col_from, own(col_from), r_pick, row_from


Z_OWN, Z_PICK, X_PICK, X_OWN, COL_FROM, COL_OWN, R_PICK, ROW_FROM = 0, 8, 24, 40, 48, 60, 66, 98


def whole(shape):
    return pl.BlockSpec(shape, lambda g, tab: (0,) * len(shape))


def part(shape):
    return pl.BlockSpec((1,) + shape, lambda g, tab: (g,) + (0,) * len(shape))


def local_call(kernel, grid, table, operands, in_specs, out_shapes, out_specs, scratch=()):
    return pl.pallas_call(
        kernel,
        grid_spec=pltpu.PrefetchScalarGridSpec(
            num_scalar_prefetch=1, grid=(grid,), in_specs=in_specs, out_specs=out_specs,
            scratch_shapes=list(scratch),
        ),
        out_shape=[jax.ShapeDtypeStruct(s, jnp.float32) for s in out_shapes],
        compiler_params=pltpu.CompilerParams(vmem_limit_bytes=56 * 1024 * 1024),
    )(table, *operands)


def at_least_zero(v):
    return jnp.maximum(v, 0)


def lanes(block):
    return pl.ds(pl.multiple_of(block * BLK, BLK), BLK)


def pack_first(tab, front, za, yb):
    g = pl.program_id(0)
    za[0] = front[:, 0:64, lanes(at_least_zero(tab[Z_OWN + g]))]
    for k in range(4):
        yb[0, k] = front[at_least_zero(tab[R_PICK + g * 4 + k]), 64:128, :]


def pack_second(tab, zin, yin, xa, zb):
    g = pl.program_id(0)
    xa[0] = zin[at_least_zero(tab[X_OWN + g])]
    for c in range(2):
        column = lanes(at_least_zero(tab[Z_PICK + c * 8 + g]))
        for i in range(12):
            source = at_least_zero(tab[ROW_FROM + c * 12 + i])
            zb[0, c * 12 + i] = yin[source, :, column]


def pack_third(tab, xin, zin, ya, xb):
    g = pl.program_id(0)
    for c in range(2):
        source = at_least_zero(tab[X_PICK + c * 8 + g])
        xb[0, c * 12 : c * 12 + 12] = zin[source, c * 12 : c * 12 + 12]
    for k in range(4):
        i = at_least_zero(tab[R_PICK + g * 4 + k])
        for slot in range(6):
            source = at_least_zero(tab[COL_OWN + slot])
            ya[0, k, :, slot * BLK : slot * BLK + BLK] = xin[source, i]


def add_all(tab, root, yin, xin, out):
    i = pl.program_id(0)
    for slot in range(6):
        columns = slice(slot * BLK, slot * BLK + BLK)
        upper, lower = root[0, 0:64, columns], root[0, 64:128, columns]
        for c in range(2):
            row, col = tab[ROW_FROM + c * 12 + i], tab[COL_FROM + c * 6 + slot]
            there = jnp.logical_and(row >= 0, col >= 0)
            upper += jnp.where(there, yin[at_least_zero(row), :, columns], 0.0)
            lower += jnp.where(there, xin[at_least_zero(col), c * 12 + i], 0.0)
        out[0, 0:64, columns] = upper
        out[0, 64:128, columns] = lower


def extend_add(factored, root_front, child_map):
    table = jnp.concatenate([a.reshape(-1) for a in routes(child_map)])
    front = factored.reshape(16, BLK, 512)
    za, yb = local_call(
        pack_first, 8, table, (front,), [whole((16, BLK, 512))],
        [(8, 16, 64, BLK), (8, 4, 64, 512)], [part((16, 64, BLK)), part((4, 64, 512))],
    )
    za, yb = exchange([swap(za.reshape(4, 2, 16, 64, BLK), "z"), swap(yb, ROW)], 1)
    xa, zb = local_call(
        pack_second, 8, table, (za.reshape(8, 16, 64, BLK), yb.reshape(32, 64, 512)),
        [whole((8, 16, 64, BLK)), whole((32, 64, 512))],
        [(8, 16, 64, BLK), (8, 24, 64, BLK)], [part((16, 64, BLK)), part((24, 64, BLK))],
    )
    xa, zb = exchange(
        [swap(xa.reshape(4, 2, 16, 64, BLK), "x"), swap(zb.reshape(4, 2, 24, 64, BLK), "z")], 2
    )
    ya, xb = local_call(
        pack_third, 8, table, (xa.reshape(8, 16, 64, BLK), zb.reshape(8, 24, 64, BLK)),
        [whole((8, 16, 64, BLK)), whole((8, 24, 64, BLK))],
        [(8, 4, 64, 768), (8, 24, 64, BLK)], [part((4, 64, 768)), part((24, 64, BLK))],
    )
    ya, xb = exchange([swap(ya, ROW), swap(xb.reshape(4, 2, 24, 64, BLK), "x")], 3)
    (assembled,) = local_call(
        add_all, 12, table,
        (root_front.reshape(12, BLK, 768), ya.reshape(32, 64, 768), xb.reshape(8, 24, 64, BLK)),
        [part((BLK, 768)), whole((32, 64, 768)), whole((8, 24, 64, BLK))],
        [(12, BLK, 768)], [part((BLK, 768))],
    )
    return assembled.reshape(root_front.shape)


def pick(arrived, owners):
    parts = [
        lax.dynamic_index_in_dim(arrived[..., q * PANEL : (q + 1) * PANEL], owner, 0, keepdims=False)
        for q, owner in enumerate(owners)
    ]
    return jnp.concatenate(parts, axis=-1)


def gather_bands(cols, rows, col_off, xs, zs, row_owners, axes, size, first_id):
    count, width = cols.shape
    panels, _, span = rows.shape
    piece = PANEL // size
    cols = cols.reshape(2, 4, count // 8, width)
    rows = rows.reshape(panels, size, piece, span)
    first, second, slices = exchange(
        [swap_half(cols, "z", 0), swap_half(cols, "x", 1), swap_inner(rows, axes)], first_id
    )
    first, second = pick(first, zs), pick(second, xs)
    slices = jnp.stack(
        [lax.dynamic_index_in_dim(slices[:, k], owner, 0, keepdims=False) for k, owner in enumerate(row_owners)]
    )
    cross = jnp.concatenate(
        [lax.dynamic_slice_in_dim(slices, off, PANEL, 2) for off in col_off], axis=2
    )
    split = lambda a: a.reshape(4, count // 32, width)
    half = span // 2
    first, second, cross, left = exchange(
        [
            swap(split(first), "x"), swap(split(second), "z"), share(cross, "z", 4),
            share_inner(slices[..., :half], axes, size),
        ],
        first_id + 1,
    )
    first, second, cross = pick(first, xs), pick(second, zs), pick(cross, zs)
    first, second, cross, right = exchange(
        [
            share(first, "x", 4), share(second, "z", 4), share(cross, "x", 4),
            share_inner(slices[..., half:], axes, size),
        ],
        first_id + 2,
    )
    cross = pick(cross, xs)
    join = lambda a: a.reshape(count // 8, width)
    first, second, cross = exchange(
        [share(join(first), "z", 4), share(join(second), "x", 4), share_inner(cross, axes, size)],
        first_id + 3,
    )
    halves = [a.reshape(count // 2, width) for a in (first, second)]
    left, right = (a.reshape(width, half) for a in (left, right))
    return halves, left, right, cross.reshape(width, width)


PARENT = {
    (3, 0): (0, 0), (3, 3): (3, 0), (3, 1): (3, 0), (2, 0): (3, 0), (2, 3): (2, 0),
    (3, 2): (3, 1), (0, 1): (3, 1), (0, 3): (3, 3), (2, 1): (3, 1), (1, 0): (2, 0),
    (2, 2): (3, 2), (1, 1): (2, 1), (0, 2): (3, 2), (1, 3): (2, 3), (1, 2): (2, 2),
}


def turned(place, quarter_turns):
    for _ in range(quarter_turns):
        place = (-place[1] % 4, place[0])
    return place


def tree_children(turn):
    children = [[] for _ in range(16)]
    for child, parent in PARENT.items():
        child, parent = turned(child, turn), turned(parent, turn)
        children[4 * parent[0] + parent[1]].append(4 * child[0] + child[1])
    return children


def tree_depth(turn):
    depth = [0] * 16
    for place in PARENT:
        node, hops = place, 0
        while node != (0, 0):
            node, hops = PARENT[node], hops + 1
        place = turned(place, turn)
        depth[4 * place[0] + place[1]] = hops
    return depth


def lookup(values, index):
    result = jnp.int32(values[0])
    for k in range(1, len(values)):
        result = jnp.where(index == k, jnp.int32(values[k]), result)
    return result


CHUNK = 32
CHUNKS = 2048 // (4 * CHUNK)
CROSS = CPAN * PANEL // (4 * CHUNK)
U_PARTS = 4
DEPTH = 5
SLACK = 2


def spread_kernel(front, cols, rows, cross, recv, send, cross_recv, cross_send, rows_recv,
                  rows_send, own_sem, stage):
    y, core = lax.axis_index("y"), lax.axis_index("core")
    x, z = lax.axis_index("x"), lax.axis_index("z")
    place, within = 4 * x + z, lax.rem(y, 2) * 2 + core
    is_root = place == 0
    tables = [tree_children(turn) for turn in range(4)]
    target = [
        [lookup([(t[k] + [-1, -1, -1])[s] for k in range(16)], place) for s in range(3)]
        for t in tables
    ]
    depth = [lookup(tree_depth(turn), place) for turn in range(4)]
    sibling = {"core": 1 - core}
    above = {"y": y // 2 * 2 + 1 - lax.rem(y, 2)}

    barrier = pltpu.get_barrier_semaphore()
    for ident in (
        {"x": lax.rem(x + 1, 4)}, {"x": lax.rem(x + 3, 4)},
        {"z": lax.rem(z + 1, 4)}, {"z": lax.rem(z + 3, 4)}, sibling, above,
    ):
        pl.semaphore_signal(barrier, inc=1, device_id=ident, device_id_type=MESH)

    part = CPAN * PANEL // U_PARTS
    whole_band = pl.ds(0, CPAN * PANEL)
    load_own = pltpu.make_async_copy(front, stage, own_sem.at[0])
    own_cols = pltpu.make_async_copy(stage, cols, own_sem.at[0])
    own_rows = pltpu.make_async_copy(stage.at[whole_band], rows, own_sem.at[1])
    load_own.start()
    pl.semaphore_wait(barrier, 6)

    def rows_copy(src, k, way, ident):
        span = pl.ds(k * part, part)
        return pltpu.make_async_remote_copy(
            src_ref=src.at[span], dst_ref=rows.at[span], send_sem=rows_send.at[way, k],
            recv_sem=rows_recv.at[k], device_id=ident, device_id_type=MESH,
        )

    def band(c, q):
        return pl.ds(pl.multiple_of((c * 4 + q) * CHUNK, CHUNK), CHUNK)

    def cols_copy(src, c, q, s):
        span = band(c, q)
        there = jnp.maximum(target[q][s], 0)
        return pltpu.make_async_remote_copy(
            src_ref=src.at[span], dst_ref=cols.at[span], send_sem=send.at[q, s, c],
            recv_sem=recv.at[q, c], device_id={"x": there // 4, "z": lax.rem(there, 4)},
            device_id_type=MESH,
        )

    def cross_copy(src, c, q, way, ident):
        span = band(c, q)
        return pltpu.make_async_remote_copy(
            src_ref=src.at[span], dst_ref=cross.at[span], send_sem=cross_send.at[way, q, c],
            recv_sem=cross_recv.at[q, c], device_id=ident, device_id_type=MESH,
        )

    @pl.when(within == 0)
    def _():
        for k in range(U_PARTS):
            rows_copy(front, k, 0, above).start()
            rows_copy(front, k, 1, sibling).start()

    load_own.wait()

    @pl.when(is_root)
    def _():
        own_cols.start()

    @pl.when(within == 0)
    def _():
        own_rows.start()

    def both(first, second):
        return jnp.logical_and(first, second)

    def pass_cols(c, q):
        @pl.when(is_root)
        def _():
            cols_copy(front, c, q, 0).start()

            @pl.when(both(within == 0, c < CROSS))
            def _():
                cross_copy(front, c, q, 0, above).start()
                cross_copy(front, c, q, 1, sibling).start()

        @pl.when(jnp.logical_not(is_root))
        def _():
            cols_copy(cols, c, q, 0).wait_recv()
            for s in range(3):

                @pl.when(target[q][s] >= 0)
                def _():
                    cols_copy(cols, c, q, s).start()

            @pl.when(both(within == 0, c < CROSS))
            def _():
                cross_copy(cols, c, q, 0, above).start()
                cross_copy(cols, c, q, 1, sibling).start()

    def loop(lo, hi, body):
        lax.fori_loop(lo, hi, lambda c, _: (body(c), 0)[1], 0)

    def step(turn):
        for q in range(4):
            c = turn - SLACK * depth[q]

            @pl.when(both(c >= 0, c < CHUNKS))
            def _():
                pass_cols(c, q)

        for q in range(4):
            late = turn - SLACK * (depth[q] + 1)

            @pl.when(both(within == 2, both(late >= 0, late < CROSS)))
            def _():
                cross_copy(cross, late, q, 0, above).wait_recv()
                cross_copy(cross, late, q, 1, sibling).start()

    loop(0, CHUNKS + SLACK * DEPTH, step)

    @pl.when(within == 2)
    def _():
        for k in range(U_PARTS):
            rows_copy(rows, k, 0, above).wait_recv()
            rows_copy(rows, k, 1, sibling).start()

    @pl.when(within == 0)
    def _():
        own_rows.wait()
        for k in range(U_PARTS):
            rows_copy(front, k, 0, above).wait_send()
            rows_copy(front, k, 1, sibling).wait_send()

        def send_done(c):
            for q in range(4):
                cross_copy(front, c, q, 0, above).wait_send()
                cross_copy(front, c, q, 1, sibling).wait_send()

        loop(0, CROSS, send_done)

    @pl.when(within == 2)
    def _():
        for k in range(U_PARTS):
            rows_copy(rows, k, 1, sibling).wait_send()

        def send_done(c):
            for q in range(4):
                cross_copy(cross, c, q, 1, sibling).wait_send()

        loop(0, CROSS, send_done)

    @pl.when(lax.rem(within, 2) == 1)
    def _():
        for k in range(U_PARTS):
            rows_copy(rows, k, 0, sibling).wait_recv()

        def arrived(c):
            for q in range(4):
                cross_copy(cross, c, q, 0, sibling).wait_recv()

        loop(0, CROSS, arrived)

    def cols_done(c):
        for q in range(4):
            for s in range(3):

                @pl.when(target[q][s] >= 0)
                def _():
                    cols_copy(front, c, q, s).wait_send()

    loop(0, CHUNKS, cols_done)

    @pl.when(is_root)
    def _():
        own_cols.wait()

    @pl.when(within == 0)
    def _():
        load = pltpu.make_async_copy(cols.at[whole_band], stage.at[whole_band], own_sem.at[0])
        load.start()
        load.wait()
        store = pltpu.make_async_copy(stage.at[whole_band], cross, own_sem.at[0])
        store.start()
        store.wait()


def spread(front, collective_id):
    rows, cols = front.shape
    width = CPAN * PANEL
    shapes = [(rows, width), (width, cols), (width, width)]
    dma = pltpu.SemaphoreType.DMA
    return pl.pallas_call(
        spread_kernel,
        out_shape=[jax.ShapeDtypeStruct(s, jnp.float32) for s in shapes],
        in_specs=[pl.BlockSpec(memory_space=pl.ANY)],
        out_specs=[pl.BlockSpec(memory_space=pl.ANY)] * 3,
        scratch_shapes=[
            dma((4, CHUNKS)), dma((4, 3, CHUNKS)), dma((4, CROSS)), dma((2, 4, CROSS)),
            dma((U_PARTS,)), dma((2, U_PARTS)), dma((2,)), pltpu.VMEM(front.shape, jnp.float32),
        ],
        compiler_params=pltpu.CompilerParams(
            collective_id=collective_id, has_side_effects=True, vmem_limit_bytes=32 * 1024 * 1024
        ),
    )(front)


def dot(a, b, precision=HIGH):
    return jnp.dot(a, b, precision=precision, preferred_element_type=jnp.float32)


def newton(block):
    shape = (PANEL, PANEL)
    eye = lax.broadcasted_iota(jnp.int32, shape, 0) == lax.broadcasted_iota(jnp.int32, shape, 1)
    kept = jnp.where(eye, block, 0.0)
    by_col = 1.0 / jnp.sum(kept, axis=0, keepdims=True)
    by_row = 1.0 / jnp.sum(kept, axis=1, keepdims=True)
    identity = jnp.where(eye, 1.0, 0.0)
    error = identity - block * by_col
    product = identity + error
    for _ in range(3):
        error = dot(error, error, HIGHEST)
        product = product + dot(product, error, HIGHEST)
    return product * by_row


def panel(k):
    return slice(k * PANEL, (k + 1) * PANEL)


def finish_kernel(n, row_panels, col_panels, precision, bands, tab, front, *refs):
    cols, rows, cross, out, work, inverse, pivots = (
        refs[:bands], refs[bands:-5], refs[-5], *refs[-4:]
    )
    g = pl.program_id(0)

    @pl.when(g == 0)
    def _():
        work[...] = cross[...]
        for i, part in enumerate(rows):
            span = part.shape[1]
            pivots[:, i * span : (i + 1) * span] = part[...]
        for k in range(n):
            inverse[k] = newton(work[panel(k), panel(k)])
            for p in range(k + 1, n):
                factor = dot(work[panel(p), panel(k)], inverse[k], HIGHEST)
                for q in range(k + 1, n):
                    work[panel(p), panel(q)] -= dot(factor, work[panel(k), panel(q)], HIGHEST)
                pivots[panel(p), :] -= dot(factor, pivots[panel(k), :], HIGHEST)
        for j in range(col_panels):
            for k in range(n):
                pivots[panel(k), panel(j)] = jnp.where(
                    tab[row_panels + j] > k, pivots[panel(k), panel(j)], 0.0
                )

    mine = cols[0][...]
    if bands == 2:
        mine = jnp.where(g < row_panels // 2, mine, cols[1][...])
    band = [mine[:, panel(k)] for k in range(n)]
    for k in range(n):
        band[k] = dot(band[k], inverse[k], HIGHEST)
        for q in range(k + 1, n):
            band[q] = band[q] - dot(band[k], work[panel(k), panel(q)], HIGHEST)
    band = [jnp.where(tab[g] > k, band[k], 0.0) for k in range(n)]
    factors = jnp.concatenate(band, axis=1)
    for j in range(col_panels):
        new = front[:, panel(j)] - dot(factors, pivots[:, panel(j)], precision)
        for k in range(n):
            here = jnp.logical_and(tab[row_panels + j] == k, tab[g] > k)
            new = jnp.where(here, band[k], new)
        out[:, panel(j)] = new


def finish(front, bands, pivot_rows, cross, row_step, col_step, precision):
    rows, cols = front.shape
    width = cross.shape[0]
    n, row_panels, col_panels = width // PANEL, rows // PANEL, cols // PANEL
    half = row_panels // 2
    keep = lambda shape: pl.BlockSpec(shape, lambda g, tab: (0, 0))
    if len(bands) == 1:
        band_specs = [pl.BlockSpec((PANEL, width), lambda g, tab: (g, 0))]
    else:
        band_specs = [
            pl.BlockSpec((PANEL, width), lambda g, tab: (jnp.minimum(g, half - 1), 0)),
            pl.BlockSpec((PANEL, width), lambda g, tab: (jnp.maximum(g - half, 0), 0)),
        ]
    (out,) = local_call(
        functools.partial(finish_kernel, n, row_panels, col_panels, precision, len(bands)),
        row_panels,
        jnp.concatenate([row_step, col_step]).astype(jnp.int32),
        (front, *bands, *pivot_rows, cross),
        [
            pl.BlockSpec((PANEL, cols), lambda g, tab: (g, 0)),
            *band_specs,
            *[keep(p.shape) for p in pivot_rows],
            keep(cross.shape),
        ],
        [front.shape],
        [pl.BlockSpec((PANEL, cols), lambda g, tab: (g, 0))],
        scratch=[
            pltpu.VMEM((width, width), jnp.float32),
            pltpu.VMEM((n, PANEL, PANEL), jnp.float32),
            pltpu.VMEM((width, cols), jnp.float32),
        ],
    )
    return out


def body(child_fronts, root_front, child_map, panel_order):
    y, core = lax.axis_index("y"), lax.axis_index("core")
    r, o = 2 * y + core, 4 * lax.axis_index("x") + lax.axis_index("z")
    within = lax.rem(y, 2) * 2 + core

    pivot_cols, pivot_rows, cross = spread(child_fronts, 10)
    row_panel, col_panel = within * 8 + jnp.arange(8), o * 2 + jnp.arange(2)
    row_step = jnp.where(row_panel < CPAN, row_panel, NEVER)
    col_step = jnp.where(col_panel < CPAN, col_panel, NEVER)
    factored = finish(
        child_fronts, [pivot_cols], [pivot_rows], cross, row_step, col_step, HIGHEST
    )

    assembled = extend_add(factored, root_front, child_map)

    row_panels, col_panels = 6, 3
    order = [panel_order[k] for k in range(RPAN)]
    col_off = [p % col_panels * PANEL for p in order]
    row_off = [p % row_panels * PANEL for p in order]
    owner = [p // col_panels for p in order]
    cols = jnp.concatenate([lax.dynamic_slice_in_dim(assembled, off, PANEL, 1) for off in col_off], 1)
    rows = jnp.stack([lax.dynamic_slice_in_dim(assembled, off, PANEL, 0) for off in row_off])
    halves, left, right, cross = gather_bands(
        cols, rows, col_off, [c // 4 for c in owner], [c % 4 for c in owner],
        [p // row_panels for p in order], ROW, 8, 20,
    )

    def steps(places):
        match = places[:, None] == panel_order[None, :]
        return jnp.min(jnp.where(match, jnp.arange(RPAN)[None, :], NEVER), axis=1)

    row_step = steps(r * row_panels + jnp.arange(row_panels))
    col_step = steps(o * col_panels + jnp.arange(col_panels))
    return factored, finish(assembled, halves, [left, right], cross, row_step, col_step, HIGH)


def solution(mesh):
    grid = Mesh(mesh.devices.reshape(4, 2, 4, 4), ("y", "core", "x", "z"))
    return jax.shard_map(
        body,
        mesh=grid,
        in_specs=(P(ROW, COL), P(ROW, COL), P(), P()),
        out_specs=(P(ROW, COL), P(ROW, COL)),
        check_vma=False,
    )
```

```python
import functools

import jax
import jax.numpy as jnp
from jax import lax
from jax.experimental import pallas as pl
from jax.experimental.pallas import tpu as pltpu
from jax.sharding import Mesh
from jax.sharding import PartitionSpec as P

PANEL = 256
BLK = 128
CPAN = 2
RPAN = 3

ROW = ("y", "core")
COL = ("x", "z")
MESH = pl.DeviceIdType.MESH
NEVER = 99

HIGH = lax.Precision.HIGH
HIGHEST = lax.Precision.HIGHEST


def peers_of(axes):
    y, core = lax.axis_index("y"), lax.axis_index("core")
    if axes == ROW:
        return 2 * y + core, 8, lambda p: {"y": p // 2, "core": lax.rem(p, 2)}
    if axes == "child":
        pair = y // 2 * 2
        me = lax.rem(y, 2) * 2 + core
        return me, 4, lambda p: {"y": pair + p // 2, "core": lax.rem(p, 2)}
    return lax.axis_index(axes), 4, lambda p: {axes: p}


def swap(array, axes):
    return (array, axes, lambda ref, p: ref.at[p], lambda ref, p: ref.at[p], array.shape, array.shape[1:])


def swap_inner(array, axes):
    shape = (array.shape[1], array.shape[0]) + array.shape[2:]
    return (array, axes, lambda ref, p: ref.at[:, p], lambda ref, p: ref.at[p], shape, shape[1:])


def swap_half(array, axes, half):
    return (
        array, axes, lambda ref, p: ref.at[half, p], lambda ref, p: ref.at[p], array.shape[1:],
        array.shape[2:],
    )


def share(array, axes, size):
    return (
        array, axes, lambda ref, p: ref, lambda ref, p: ref.at[p], (size,) + array.shape, array.shape
    )


def share_inner(array, axes, size):
    shape = (array.shape[0], size) + array.shape[1:]
    return (array, axes, lambda ref, p: ref, lambda ref, p: ref.at[:, p], shape, array.shape)


def exchange(moves, collective_id):
    n = len(moves)
    greeted = list(dict.fromkeys(m[1] for m in moves))

    def kernel(*refs):
        ins, outs = refs[:n], refs[n : 2 * n]
        send_sem, recv_sem, own_sem = refs[2 * n : 2 * n + 3]
        stages = refs[2 * n + 3 :]
        barrier = pltpu.get_barrier_semaphore()
        total = 0
        for ax in greeted:
            me, size, ident = peers_of(ax)
            for d in range(1, size):
                pl.semaphore_signal(
                    barrier, inc=1, device_id=ident(lax.rem(me + d, size)), device_id_type=MESH
                )
            total += size - 1
        loads, stores = [], []
        for i, (_, ax, src, dst, _, _) in enumerate(moves):
            me = peers_of(ax)[0]
            loads.append(pltpu.make_async_copy(src(ins[i], me), stages[i], own_sem.at[i]))
            stores.append(pltpu.make_async_copy(stages[i], dst(outs[i], me), own_sem.at[i]))
        for copy in loads:
            copy.start()
        pl.semaphore_wait(barrier, total)
        copies = []
        for i, (_, ax, src, dst, _, _) in enumerate(moves):
            me, size, ident = peers_of(ax)
            for d in sorted(range(1, size), key=lambda d: -min(d, size - d)):
                p = lax.rem(me + d, size)
                copy = pltpu.make_async_remote_copy(
                    src_ref=src(ins[i], p),
                    dst_ref=dst(outs[i], me),
                    send_sem=send_sem.at[i, d],
                    recv_sem=recv_sem.at[i, d],
                    device_id=ident(p),
                    device_id_type=MESH,
                )
                copy.start()
                copies.append(copy)
        for load, store in zip(loads, stores):
            load.wait()
            store.start()
        for copy in stores + copies:
            copy.wait()

    return pl.pallas_call(
        kernel,
        out_shape=[jax.ShapeDtypeStruct(m[4], jnp.float32) for m in moves],
        in_specs=[pl.BlockSpec(memory_space=pl.ANY)] * n,
        out_specs=[pl.BlockSpec(memory_space=pl.ANY)] * n,
        scratch_shapes=[
            pltpu.SemaphoreType.DMA((n, 8)),
            pltpu.SemaphoreType.DMA((n, 8)),
            pltpu.SemaphoreType.DMA((n,)),
            *[pltpu.VMEM(m[5], jnp.float32) for m in moves],
        ],
        compiler_params=pltpu.CompilerParams(
            collective_id=collective_id, has_side_effects=True, vmem_limit_bytes=32 * 1024 * 1024
        ),
    )(*[m[0] for m in moves])


def rank_in(key, group, valid):
    n = key.shape[1]
    earlier = jnp.arange(n)[None, :] < jnp.arange(n)[:, None]
    same = (key[:, :, None] == key[:, None, :]) & (group[:, None] == group[None, :])[None]
    return jnp.sum((same & valid[:, None, :] & earlier[None]).astype(jnp.int32), axis=2)


def routes(child_map):
    y, core = lax.axis_index("y"), lax.axis_index("core")
    x, z = lax.axis_index("x"), lax.axis_index("z")
    within, r, o = lax.rem(y, 2) * 2 + core, 2 * y + core, 4 * x + z
    blocks = jnp.arange(64)
    skip = CPAN * PANEL // BLK
    cyclic = (child_map % 6) * 16 + child_map // 6
    t = jnp.concatenate([jnp.zeros((2, skip), jnp.int32), cyclic], axis=1)
    valid = jnp.broadcast_to(blocks >= skip, (2, 64))
    kz = rank_in(t % 4, blocks // 4, valid)
    kx = rank_in(t % 16, blocks // 16, valid)
    kr = rank_in(t % 16 // 2, blocks // 16, valid)
    child = jnp.arange(2)[:, None]
    device, group = (blocks // 4)[None], (blocks // 16)[None]
    kinds = [
        (device == o, t % 4 * 2 + kz, blocks[None] % 4),
        ((group == x) & (t % 4 == z), t % 16 // 4 * 2 + kx, device % 4 * 2 + kz),
        (t % 16 == o, t // 16, group * 2 + kx),
        (group == within, t % 16 // 2 * 4 + kr, blocks[None] % 16),
        (t % 16 // 2 == r, t % 2 * 6 + t // 16, (child * 4 + group) * 4 + kr),
    ]
    lists = lambda k: jnp.stack([jnp.broadcast_to(a, (2, 64)) for a in k])
    place = jnp.where(lists([valid & k[0] for k in kinds]), lists([k[1] for k in kinds]), -1)
    says = lists([k[2] for k in kinds]) + 1
    match = place[:, :, None, :] == jnp.arange(32)[None, None, :, None]
    return (jnp.sum(jnp.where(match, says[:, :, None, :], 0), axis=3) - 1).reshape(-1)


Z_PICK, X_PICK, COL_FROM, R_PICK, ROW_FROM = (64 * k for k in range(5))


def whole(shape):
    return pl.BlockSpec(shape, lambda g, tab: (0,) * len(shape))


def part(shape):
    return pl.BlockSpec((1,) + shape, lambda g, tab: (g,) + (0,) * len(shape))


def local_call(kernel, grid, table, operands, in_specs, out_shapes, out_specs, scratch=()):
    return pl.pallas_call(
        kernel,
        grid_spec=pltpu.PrefetchScalarGridSpec(
            num_scalar_prefetch=1, grid=(grid,), in_specs=in_specs, out_specs=out_specs,
            scratch_shapes=list(scratch),
        ),
        out_shape=[jax.ShapeDtypeStruct(s, jnp.float32) for s in out_shapes],
        compiler_params=pltpu.CompilerParams(vmem_limit_bytes=56 * 1024 * 1024),
    )(table, *operands)


def at_least_zero(v):
    return jnp.maximum(v, 0)


def lanes(block):
    return pl.ds(pl.multiple_of(block * BLK, BLK), BLK)


QUARTER = BLK // 4


def extend_kernel(tab, front, *refs):
    ya_in, xb_in = refs[0:2], refs[2:4]
    send_sem, recv_sem, own_sem = refs[-3:]
    za_out, za_in, xa_out, xa_in, ya_out, yb_out, yb_in, zb_out, zb_in, xb_out = (
        refs[4 + 2 * i : 6 + 2 * i] for i in range(10)
    )
    barrier = pltpu.get_barrier_semaphore()
    total = 0
    for ax in ("z", "x", ROW):
        me, size, ident = peers_of(ax)
        for d in range(1, size):
            pl.semaphore_signal(
                barrier, inc=1, device_id=ident(lax.rem(me + d, size)), device_id_type=MESH
            )
        total += size - 1

    started = []

    def send(number, src, dst, axes, count):
        me, size, ident = peers_of(axes)
        slot = lambda p: pl.ds(p * count, count)
        own = pltpu.make_async_copy(src.at[slot(me)], dst.at[slot(me)], own_sem.at[number])
        own.start()
        copies = []
        for d in sorted(range(1, size), key=lambda d: -min(d, size - d)):
            p = lax.rem(me + d, size)
            copy = pltpu.make_async_remote_copy(
                src_ref=src.at[slot(p)],
                dst_ref=dst.at[slot(me)],
                send_sem=send_sem.at[number, d],
                recv_sem=recv_sem.at[number, d],
                device_id=ident(p),
                device_id_type=MESH,
            )
            copy.start()
            copies.append(copy)
        started.extend(copies)
        return own, copies

    def arrive(transfer):
        own, copies = transfer
        own.wait()
        for copy in copies:
            copy.wait_recv()

    def each(count, body):
        lax.fori_loop(0, count, lambda g, _: (body(g), 0)[1], 0)

    own = 32 * (lax.axis_index("y") // 2)

    def entry(at):
        return tab[at]

    def pack_za(ch):
        rows = slice(ch * QUARTER, (ch + 1) * QUARTER)

        def body(g):
            za_out[ch][g] = front[entry(Z_PICK + own + g), :, rows, :]

        each(8, body)

    def pack_yb(ch):
        rows = slice((2 + ch) * QUARTER, (3 + ch) * QUARTER)

        def body(g):
            yb_out[ch][g] = front[:, entry(R_PICK + own + g), rows, :]

        each(32, body)

    def pack_xa(ch):
        def body(g):
            xa_out[ch][g] = za_in[ch][entry(X_PICK + own + g)]

        each(8, body)

    def pack_zb(ch):
        def body(g):
            for c in range(2):
                column = entry(Z_PICK + c * 32 + g)
                for i in range(12):
                    source = entry(ROW_FROM + c * 32 + i)
                    zb_out[ch][g, c * 12 + i] = yb_in[ch][source, column]

        each(8, body)

    def pack_ya(ch):
        def body(g):
            i = entry(R_PICK + own + g)
            for slot in range(6):
                columns = slice(slot * BLK, slot * BLK + BLK)
                ya_out[ch][g, :, columns] = xa_in[ch][entry(COL_FROM + own + slot), i]

        each(32, body)

    def pack_xb(ch):
        def body(g):
            for c in range(2):
                rows = slice(c * 12, c * 12 + 12)
                xb_out[ch][g, rows] = zb_in[ch][entry(X_PICK + c * 32 + g), rows]

        each(8, body)

    za = lambda ch: send(0 + ch, za_out[ch], za_in[ch], "z", 2)
    xa = lambda ch: send(2 + ch, xa_out[ch], xa_in[ch], "x", 2)
    ya = lambda ch: send(4 + ch, ya_out[ch], ya_in[ch], ROW, 4)
    yb = lambda ch: send(6 + ch, yb_out[ch], yb_in[ch], ROW, 4)
    zb = lambda ch: send(8 + ch, zb_out[ch], zb_in[ch], "z", 2)
    xb = lambda ch: send(10 + ch, xb_out[ch], xb_in[ch], "x", 2)

    pack_za(0)
    pl.semaphore_wait(barrier, total)
    za0 = za(0)
    pack_yb(0)
    yb0 = yb(0)
    pack_za(1)
    pack_yb(1)
    arrive(za0)
    za1 = za(1)
    pack_xa(0)
    xa0 = xa(0)
    arrive(yb0)
    yb1 = yb(1)
    pack_zb(0)
    zb0 = zb(0)
    arrive(xa0)
    pack_ya(0)
    ya0 = ya(0)
    arrive(za1)
    pack_xa(1)
    xa1 = xa(1)
    arrive(yb1)
    pack_zb(1)
    zb1 = zb(1)
    arrive(xa1)
    pack_ya(1)
    ya1 = ya(1)
    arrive(zb0)
    pack_xb(0)
    xb0 = xb(0)
    arrive(zb1)
    pack_xb(1)
    xb1 = xb(1)
    for last in (ya0, ya1, xb0, xb1):
        arrive(last)
    for copy in started:
        copy.wait_send()


def add_all(tab, root, ya0, ya1, xb0, xb1, out):
    i = pl.program_id(0)
    for slot in range(6):
        columns = slice(slot * BLK, slot * BLK + BLK)
        sums = [root[0, q * QUARTER : (q + 1) * QUARTER, columns] for q in range(4)]
        for c in range(2):
            row, col = tab[ROW_FROM + c * 32 + i], tab[COL_FROM + c * 32 + slot]
            there = jnp.logical_and(row >= 0, col >= 0)
            row, col = at_least_zero(row), at_least_zero(col)
            arrived = [
                ya0[row, :, columns], ya1[row, :, columns], xb0[col, c * 12 + i], xb1[col, c * 12 + i]
            ]
            sums = [s + jnp.where(there, a, 0.0) for s, a in zip(sums, arrived)]
        for q in range(4):
            out[0, q * QUARTER : (q + 1) * QUARTER, columns] = sums[q]


def extend_add(front, root_front, child_map):
    table = routes(child_map)
    blocks, rows, wide = (8, 16, QUARTER, BLK), (32, QUARTER, 768), (8, 24, QUARTER, BLK)
    band = (32, 4, QUARTER, BLK)
    buffers = [blocks] * 8 + [rows] * 2 + [band] * 4 + [wide] * 6
    arrived = pl.pallas_call(
        extend_kernel,
        out_shape=[jax.ShapeDtypeStruct(s, jnp.float32) for s in (rows, rows, wide, wide)],
        in_specs=[
            pl.BlockSpec(memory_space=pltpu.SMEM), pl.BlockSpec(memory_space=pltpu.VMEM),
        ],
        out_specs=[pl.BlockSpec(memory_space=pl.ANY)] * 4,
        scratch_shapes=[
            *[pltpu.VMEM(s, jnp.float32) for s in buffers],
            pltpu.SemaphoreType.DMA((12, 8)),
            pltpu.SemaphoreType.DMA((12, 8)),
            pltpu.SemaphoreType.DMA((12,)),
        ],
        compiler_params=pltpu.CompilerParams(
            collective_id=1, has_side_effects=True, vmem_limit_bytes=58 * 1024 * 1024
        ),
    )(jnp.maximum(table, 0), front.reshape(4, 16, BLK, BLK))
    (assembled,) = local_call(
        add_all, 12, table, (root_front.reshape(12, BLK, 768), *arrived),
        [part((BLK, 768)), whole(rows), whole(rows), whole(wide), whole(wide)],
        [(12, BLK, 768)], [part((BLK, 768))],
    )
    return assembled.reshape(root_front.shape)


def pick(arrived, owners):
    parts = [
        lax.dynamic_index_in_dim(arrived[..., q * PANEL : (q + 1) * PANEL], owner, 0, keepdims=False)
        for q, owner in enumerate(owners)
    ]
    return jnp.concatenate(parts, axis=-1)


def gather_bands(cols, rows, col_off, xs, zs, row_owners, axes, size, first_id):
    count, width = cols.shape
    panels, _, span = rows.shape
    piece = PANEL // size
    cols = cols.reshape(2, 4, count // 8, width)
    rows = rows.reshape(panels, size, piece, span)
    first, second, slices = exchange(
        [swap_half(cols, "z", 0), swap_half(cols, "x", 1), swap_inner(rows, axes)], first_id
    )
    first, second = pick(first, zs), pick(second, xs)
    slices = jnp.stack(
        [lax.dynamic_index_in_dim(slices[:, k], owner, 0, keepdims=False) for k, owner in enumerate(row_owners)]
    )
    cross = jnp.concatenate(
        [lax.dynamic_slice_in_dim(slices, off, PANEL, 2) for off in col_off], axis=2
    )
    split = lambda a: a.reshape(4, count // 32, width)
    half = span // 2
    first, second, upper, lower, left = exchange(
        [
            swap(split(first), "x"), swap(split(second), "z"),
            share(cross[:, : piece // 2], "z", 4), share(cross[:, piece // 2 :], "x", 4),
            share_inner(slices[..., :half], axes, size),
        ],
        first_id + 1,
    )
    first, second = pick(first, xs), pick(second, zs)
    upper, lower = pick(upper, zs), pick(lower, xs)
    first, second, upper, lower, right = exchange(
        [
            share(first, "x", 4), share(second, "z", 4),
            share(upper, "x", 4), share(lower, "z", 4),
            share_inner(slices[..., half:], axes, size),
        ],
        first_id + 2,
    )
    cross = jnp.concatenate([pick(upper, xs), pick(lower, zs)], axis=1)
    join = lambda a: a.reshape(count // 8, width)
    first, second, cross = exchange(
        [share(join(first), "z", 4), share(join(second), "x", 4), share_inner(cross, axes, size)],
        first_id + 3,
    )
    halves = [a.reshape(count // 2, width) for a in (first, second)]
    left, right = (a.reshape(width, half) for a in (left, right))
    return halves, left, right, cross.reshape(width, width)


PARENT = {
    (3, 0): (0, 0), (3, 3): (3, 0), (3, 1): (3, 0), (2, 0): (3, 0), (2, 3): (2, 0),
    (3, 2): (3, 1), (0, 1): (3, 1), (0, 3): (3, 3), (2, 1): (3, 1), (1, 0): (2, 0),
    (2, 2): (3, 2), (1, 1): (2, 1), (0, 2): (3, 2), (1, 3): (2, 3), (1, 2): (2, 2),
}


def turned(place, quarter_turns):
    for _ in range(quarter_turns):
        place = (-place[1] % 4, place[0])
    return place


def tree_children(turn):
    children = [[] for _ in range(16)]
    for child, parent in PARENT.items():
        child, parent = turned(child, turn), turned(parent, turn)
        children[4 * parent[0] + parent[1]].append(4 * child[0] + child[1])
    return children


def tree_depth(turn):
    depth = [0] * 16
    for place in PARENT:
        node, hops = place, 0
        while node != (0, 0):
            node, hops = PARENT[node], hops + 1
        place = turned(place, turn)
        depth[4 * place[0] + place[1]] = hops
    return depth


def lookup(values, index):
    result = jnp.int32(values[0])
    for k in range(1, len(values)):
        result = jnp.where(index == k, jnp.int32(values[k]), result)
    return result


CHUNK = 32
CHUNKS = 2048 // (4 * CHUNK)
CROSS = CPAN * PANEL // (4 * CHUNK)
U_PARTS = 4
DEPTH = 5
SLACK = 2


def spread_kernel(front, cols, rows, cross, recv, send, cross_recv, cross_send, rows_recv,
                  rows_send, own_sem, stage):
    y, core = lax.axis_index("y"), lax.axis_index("core")
    x, z = lax.axis_index("x"), lax.axis_index("z")
    place, within = 4 * x + z, lax.rem(y, 2) * 2 + core
    is_root = place == 0
    tables = [tree_children(turn) for turn in range(4)]
    target = [
        [lookup([(t[k] + [-1, -1, -1])[s] for k in range(16)], place) for s in range(3)]
        for t in tables
    ]
    depth = [lookup(tree_depth(turn), place) for turn in range(4)]
    sibling = {"core": 1 - core}
    above = {"y": y // 2 * 2 + 1 - lax.rem(y, 2)}

    barrier = pltpu.get_barrier_semaphore()
    for ident in (
        {"x": lax.rem(x + 1, 4)}, {"x": lax.rem(x + 3, 4)},
        {"z": lax.rem(z + 1, 4)}, {"z": lax.rem(z + 3, 4)}, sibling, above,
    ):
        pl.semaphore_signal(barrier, inc=1, device_id=ident, device_id_type=MESH)

    part = CPAN * PANEL // U_PARTS
    whole_band = pl.ds(0, CPAN * PANEL)
    load_own = pltpu.make_async_copy(front, stage, own_sem.at[0])
    own_cols = pltpu.make_async_copy(stage, cols, own_sem.at[0])
    own_rows = pltpu.make_async_copy(stage.at[whole_band], rows, own_sem.at[1])
    load_own.start()
    pl.semaphore_wait(barrier, 6)

    def rows_copy(src, k, way, ident):
        span = pl.ds(k * part, part)
        return pltpu.make_async_remote_copy(
            src_ref=src.at[span], dst_ref=rows.at[span], send_sem=rows_send.at[way, k],
            recv_sem=rows_recv.at[k], device_id=ident, device_id_type=MESH,
        )

    def band(c, q):
        return pl.ds(pl.multiple_of((c * 4 + q) * CHUNK, CHUNK), CHUNK)

    def cols_copy(src, c, q, s):
        span = band(c, q)
        there = jnp.maximum(target[q][s], 0)
        return pltpu.make_async_remote_copy(
            src_ref=src.at[span], dst_ref=cols.at[span], send_sem=send.at[q, s, c],
            recv_sem=recv.at[q, c], device_id={"x": there // 4, "z": lax.rem(there, 4)},
            device_id_type=MESH,
        )

    def cross_copy(src, c, q, way, ident):
        span = band(c, q)
        return pltpu.make_async_remote_copy(
            src_ref=src.at[span], dst_ref=cross.at[span], send_sem=cross_send.at[way, q, c],
            recv_sem=cross_recv.at[q, c], device_id=ident, device_id_type=MESH,
        )

    @pl.when(within == 0)
    def _():
        for k in range(U_PARTS):
            rows_copy(front, k, 0, above).start()
            rows_copy(front, k, 1, sibling).start()

    load_own.wait()

    @pl.when(is_root)
    def _():
        own_cols.start()

    @pl.when(within == 0)
    def _():
        own_rows.start()

    def both(first, second):
        return jnp.logical_and(first, second)

    def pass_cols(c, q):
        @pl.when(is_root)
        def _():
            cols_copy(front, c, q, 0).start()

            @pl.when(both(within == 0, c < CROSS))
            def _():
                cross_copy(front, c, q, 0, above).start()
                cross_copy(front, c, q, 1, sibling).start()

        @pl.when(jnp.logical_not(is_root))
        def _():
            cols_copy(cols, c, q, 0).wait_recv()
            for s in range(3):

                @pl.when(target[q][s] >= 0)
                def _():
                    cols_copy(cols, c, q, s).start()

            @pl.when(both(within == 0, c < CROSS))
            def _():
                cross_copy(cols, c, q, 0, above).start()
                cross_copy(cols, c, q, 1, sibling).start()

    def loop(lo, hi, body):
        lax.fori_loop(lo, hi, lambda c, _: (body(c), 0)[1], 0)

    def step(turn):
        for q in range(4):
            c = turn - SLACK * depth[q]

            @pl.when(both(c >= 0, c < CHUNKS))
            def _():
                pass_cols(c, q)

        for q in range(4):
            late = turn - SLACK * (depth[q] + 1)

            @pl.when(both(within == 2, both(late >= 0, late < CROSS)))
            def _():
                cross_copy(cross, late, q, 0, above).wait_recv()
                cross_copy(cross, late, q, 1, sibling).start()

    loop(0, CHUNKS + SLACK * DEPTH, step)

    @pl.when(within == 2)
    def _():
        for k in range(U_PARTS):
            rows_copy(rows, k, 0, above).wait_recv()
            rows_copy(rows, k, 1, sibling).start()

    @pl.when(within == 0)
    def _():
        own_rows.wait()
        for k in range(U_PARTS):
            rows_copy(front, k, 0, above).wait_send()
            rows_copy(front, k, 1, sibling).wait_send()

        def send_done(c):
            for q in range(4):
                cross_copy(front, c, q, 0, above).wait_send()
                cross_copy(front, c, q, 1, sibling).wait_send()

        loop(0, CROSS, send_done)

    @pl.when(within == 2)
    def _():
        for k in range(U_PARTS):
            rows_copy(rows, k, 1, sibling).wait_send()

        def send_done(c):
            for q in range(4):
                cross_copy(cross, c, q, 1, sibling).wait_send()

        loop(0, CROSS, send_done)

    @pl.when(lax.rem(within, 2) == 1)
    def _():
        for k in range(U_PARTS):
            rows_copy(rows, k, 0, sibling).wait_recv()

        def arrived(c):
            for q in range(4):
                cross_copy(cross, c, q, 0, sibling).wait_recv()

        loop(0, CROSS, arrived)

    def cols_done(c):
        for q in range(4):
            for s in range(3):

                @pl.when(target[q][s] >= 0)
                def _():
                    cols_copy(front, c, q, s).wait_send()

    loop(0, CHUNKS, cols_done)

    @pl.when(is_root)
    def _():
        own_cols.wait()

    @pl.when(within == 0)
    def _():
        load = pltpu.make_async_copy(cols.at[whole_band], stage.at[whole_band], own_sem.at[0])
        load.start()
        load.wait()
        store = pltpu.make_async_copy(stage.at[whole_band], cross, own_sem.at[0])
        store.start()
        store.wait()


def spread(front, collective_id):
    rows, cols = front.shape
    width = CPAN * PANEL
    shapes = [(rows, width), (width, cols), (width, width)]
    dma = pltpu.SemaphoreType.DMA
    return pl.pallas_call(
        spread_kernel,
        out_shape=[jax.ShapeDtypeStruct(s, jnp.float32) for s in shapes],
        in_specs=[pl.BlockSpec(memory_space=pl.ANY)],
        out_specs=[pl.BlockSpec(memory_space=pl.ANY)] * 3,
        scratch_shapes=[
            dma((4, CHUNKS)), dma((4, 3, CHUNKS)), dma((4, CROSS)), dma((2, 4, CROSS)),
            dma((U_PARTS,)), dma((2, U_PARTS)), dma((2,)), pltpu.VMEM(front.shape, jnp.float32),
        ],
        compiler_params=pltpu.CompilerParams(
            collective_id=collective_id, has_side_effects=True, vmem_limit_bytes=32 * 1024 * 1024
        ),
    )(front)


def dot(a, b, precision=HIGH):
    return jnp.dot(a, b, precision=precision, preferred_element_type=jnp.float32)


def newton(block):
    shape = (PANEL, PANEL)
    eye = lax.broadcasted_iota(jnp.int32, shape, 0) == lax.broadcasted_iota(jnp.int32, shape, 1)
    kept = jnp.where(eye, block, 0.0)
    by_col = 1.0 / jnp.sum(kept, axis=0, keepdims=True)
    by_row = 1.0 / jnp.sum(kept, axis=1, keepdims=True)
    identity = jnp.where(eye, 1.0, 0.0)
    error = identity - block * by_col
    product = identity + error
    error = dot(error, error, HIGHEST)
    for _ in range(2):
        both = dot(jnp.concatenate([error, product], axis=0), error, HIGHEST)
        error, product = both[:PANEL], product + both[PANEL:]
    return (product + dot(product, error, HIGHEST)) * by_row


def panel(k):
    return slice(k * PANEL, (k + 1) * PANEL)


def finish_kernel(n, row_panels, col_panels, precision, bands, tail, tab, front, *refs):
    cols, rows, cross, outs = refs[:bands], refs[bands:tail], refs[tail], refs[tail + 1 : -3]
    work, inverse, pivots = refs[-3:]
    g = pl.program_id(0)

    @pl.when(g == 0)
    def _():
        work[...] = cross[...]
        for i, part in enumerate(rows):
            span = part.shape[1]
            pivots[:, i * span : (i + 1) * span] = part[...]
        for k in range(n):
            inverse[k] = newton(work[panel(k), panel(k)])
            for p in range(k + 1, n):
                factor = dot(work[panel(p), panel(k)], inverse[k], HIGHEST)
                for q in range(k + 1, n):
                    work[panel(p), panel(q)] -= dot(factor, work[panel(k), panel(q)], HIGHEST)
                pivots[panel(p), :] -= dot(factor, pivots[panel(k), :], HIGHEST)
        for j in range(col_panels):
            for k in range(n):
                pivots[panel(k), panel(j)] = jnp.where(
                    tab[row_panels + j] > k, pivots[panel(k), panel(j)], 0.0
                )

    mine = cols[0][...]
    if bands == 2:
        mine = jnp.where(g < row_panels // 2, mine, cols[1][...])
    band = [mine[:, panel(k)] for k in range(n)]
    for k in range(n):
        band[k] = dot(band[k], inverse[k], HIGHEST)
        for q in range(k + 1, n):
            band[q] = band[q] - dot(band[k], work[panel(k), panel(q)], HIGHEST)
    band = [jnp.where(tab[g] > k, band[k], 0.0) for k in range(n)]
    factors = jnp.concatenate(band, axis=1)
    for j in range(col_panels):
        new = front[:, panel(j)] - dot(factors, pivots[:, panel(j)], precision)
        for k in range(n):
            here = jnp.logical_and(tab[row_panels + j] == k, tab[g] > k)
            new = jnp.where(here, band[k], new)
        outs[0][:, panel(j)] = new
        if len(outs) == 2:
            outs[1][2 * j] = new[:, :BLK]
            outs[1][2 * j + 1] = new[:, BLK:]


def finish(front, bands, pivot_rows, cross, row_step, col_step, precision, blocked=False):
    rows, cols = front.shape
    width = cross.shape[0]
    n, row_panels, col_panels = width // PANEL, rows // PANEL, cols // PANEL
    half = row_panels // 2
    keep = lambda shape: pl.BlockSpec(shape, lambda g, tab: (0, 0))
    if len(bands) == 1:
        band_specs = [pl.BlockSpec((PANEL, width), lambda g, tab: (g, 0))]
    else:
        band_specs = [
            pl.BlockSpec((PANEL, width), lambda g, tab: (jnp.minimum(g, half - 1), 0)),
            pl.BlockSpec((PANEL, width), lambda g, tab: (jnp.maximum(g - half, 0), 0)),
        ]
    return local_call(
        functools.partial(finish_kernel, n, row_panels, col_panels, precision, len(bands), len(bands) + len(pivot_rows)),
        row_panels,
        jnp.concatenate([row_step, col_step]).astype(jnp.int32),
        (front, *bands, *pivot_rows, cross),
        [
            pl.BlockSpec((PANEL, cols), lambda g, tab: (g, 0)),
            *band_specs,
            *[keep(p.shape) for p in pivot_rows],
            keep(cross.shape),
        ],
        [front.shape] + [(cols // BLK, rows, BLK)] * blocked,
        [pl.BlockSpec((PANEL, cols), lambda g, tab: (g, 0))]
        + [pl.BlockSpec((cols // BLK, PANEL, BLK), lambda g, tab: (0, g, 0))] * blocked,
        scratch=[
            pltpu.VMEM((width, width), jnp.float32),
            pltpu.VMEM((n, PANEL, PANEL), jnp.float32),
            pltpu.VMEM((width, cols), jnp.float32),
        ],
    )


def body(child_fronts, root_front, child_map, panel_order):
    y, core = lax.axis_index("y"), lax.axis_index("core")
    r, o = 2 * y + core, 4 * lax.axis_index("x") + lax.axis_index("z")
    within = lax.rem(y, 2) * 2 + core

    pivot_cols, pivot_rows, cross = spread(child_fronts, 10)
    row_panel, col_panel = within * 8 + jnp.arange(8), o * 2 + jnp.arange(2)
    row_step = jnp.where(row_panel < CPAN, row_panel, NEVER)
    col_step = jnp.where(col_panel < CPAN, col_panel, NEVER)
    factored, blocks = finish(
        child_fronts, [pivot_cols], [pivot_rows], cross, row_step, col_step, HIGHEST, True
    )

    assembled = extend_add(blocks, root_front, child_map)

    row_panels, col_panels = 6, 3
    order = [panel_order[k] for k in range(RPAN)]
    col_off = [p % col_panels * PANEL for p in order]
    row_off = [p % row_panels * PANEL for p in order]
    owner = [p // col_panels for p in order]
    cols = jnp.concatenate([lax.dynamic_slice_in_dim(assembled, off, PANEL, 1) for off in col_off], 1)
    rows = jnp.stack([lax.dynamic_slice_in_dim(assembled, off, PANEL, 0) for off in row_off])
    halves, left, right, cross = gather_bands(
        cols, rows, col_off, [c // 4 for c in owner], [c % 4 for c in owner],
        [p // row_panels for p in order], ROW, 8, 20,
    )

    def steps(places):
        match = places[:, None] == panel_order[None, :]
        return jnp.min(jnp.where(match, jnp.arange(RPAN)[None, :], NEVER), axis=1)

    row_step = steps(r * row_panels + jnp.arange(row_panels))
    col_step = steps(o * col_panels + jnp.arange(col_panels))
    return factored, finish(assembled, halves, [left, right], cross, row_step, col_step, HIGH)[0]


def solution(mesh):
    grid = Mesh(mesh.devices.reshape(4, 2, 4, 4), ("y", "core", "x", "z"))
    return jax.shard_map(
        body,
        mesh=grid,
        in_specs=(P(ROW, COL), P(ROW, COL), P(), P()),
        out_specs=(P(ROW, COL), P(ROW, COL)),
        check_vma=False,
    )
```

```python
import functools

import jax
import jax.numpy as jnp
from jax import lax
from jax.experimental import pallas as pl
from jax.experimental.pallas import tpu as pltpu
from jax.sharding import Mesh
from jax.sharding import PartitionSpec as P

PANEL = 256
BLK = 128
CPAN = 2
RPAN = 3

ROW = ("y", "core")
COL = ("x", "z")
MESH = pl.DeviceIdType.MESH
NEVER = 99

HIGH = lax.Precision.HIGH
HIGHEST = lax.Precision.HIGHEST


def peers_of(axes):
    y, core = lax.axis_index("y"), lax.axis_index("core")
    if axes == ROW:
        return 2 * y + core, 8, lambda p: {"y": p // 2, "core": lax.rem(p, 2)}
    if axes == "child":
        pair = y // 2 * 2
        me = lax.rem(y, 2) * 2 + core
        return me, 4, lambda p: {"y": pair + p // 2, "core": lax.rem(p, 2)}
    return lax.axis_index(axes), 4, lambda p: {axes: p}


def swap(array, axes):
    return (array, axes, lambda ref, p: ref.at[p], lambda ref, p: ref.at[p], array.shape, array.shape[1:])


def swap_inner(array, axes):
    shape = (array.shape[1], array.shape[0]) + array.shape[2:]
    return (array, axes, lambda ref, p: ref.at[:, p], lambda ref, p: ref.at[p], shape, shape[1:])


def swap_half(array, axes, half):
    return (
        array, axes, lambda ref, p: ref.at[half, p], lambda ref, p: ref.at[p], array.shape[1:],
        array.shape[2:],
    )


def share(array, axes, size):
    return (
        array, axes, lambda ref, p: ref, lambda ref, p: ref.at[p], (size,) + array.shape, array.shape
    )


def share_inner(array, axes, size):
    shape = (array.shape[0], size) + array.shape[1:]
    return (array, axes, lambda ref, p: ref, lambda ref, p: ref.at[:, p], shape, array.shape)


def exchange(moves, collective_id):
    n = len(moves)
    greeted = list(dict.fromkeys(m[1] for m in moves))

    def kernel(*refs):
        ins, outs = refs[:n], refs[n : 2 * n]
        send_sem, recv_sem, own_sem = refs[2 * n : 2 * n + 3]
        stages = refs[2 * n + 3 :]
        barrier = pltpu.get_barrier_semaphore()
        total = 0
        for ax in greeted:
            me, size, ident = peers_of(ax)
            for d in range(1, size):
                pl.semaphore_signal(
                    barrier, inc=1, device_id=ident(lax.rem(me + d, size)), device_id_type=MESH
                )
            total += size - 1
        loads, stores = [], []
        for i, (_, ax, src, dst, _, _) in enumerate(moves):
            me = peers_of(ax)[0]
            loads.append(pltpu.make_async_copy(src(ins[i], me), stages[i], own_sem.at[i]))
            stores.append(pltpu.make_async_copy(stages[i], dst(outs[i], me), own_sem.at[i]))
        for copy in loads:
            copy.start()
        pl.semaphore_wait(barrier, total)
        copies = []
        for i, (_, ax, src, dst, _, _) in enumerate(moves):
            me, size, ident = peers_of(ax)
            for d in sorted(range(1, size), key=lambda d: -min(d, size - d)):
                p = lax.rem(me + d, size)
                copy = pltpu.make_async_remote_copy(
                    src_ref=src(ins[i], p),
                    dst_ref=dst(outs[i], me),
                    send_sem=send_sem.at[i, d],
                    recv_sem=recv_sem.at[i, d],
                    device_id=ident(p),
                    device_id_type=MESH,
                )
                copy.start()
                copies.append(copy)
        for load, store in zip(loads, stores):
            load.wait()
            store.start()
        for copy in stores + copies:
            copy.wait()

    return pl.pallas_call(
        kernel,
        out_shape=[jax.ShapeDtypeStruct(m[4], jnp.float32) for m in moves],
        in_specs=[pl.BlockSpec(memory_space=pl.ANY)] * n,
        out_specs=[pl.BlockSpec(memory_space=pl.ANY)] * n,
        scratch_shapes=[
            pltpu.SemaphoreType.DMA((n, 8)),
            pltpu.SemaphoreType.DMA((n, 8)),
            pltpu.SemaphoreType.DMA((n,)),
            *[pltpu.VMEM(m[5], jnp.float32) for m in moves],
        ],
        compiler_params=pltpu.CompilerParams(
            collective_id=collective_id, has_side_effects=True, vmem_limit_bytes=32 * 1024 * 1024
        ),
    )(*[m[0] for m in moves])


def rank_in(key, group, valid):
    n = key.shape[1]
    earlier = jnp.arange(n)[None, :] < jnp.arange(n)[:, None]
    same = (key[:, :, None] == key[:, None, :]) & (group[:, None] == group[None, :])[None]
    return jnp.sum((same & valid[:, None, :] & earlier[None]).astype(jnp.int32), axis=2)


def routes(child_map):
    y, core = lax.axis_index("y"), lax.axis_index("core")
    x, z = lax.axis_index("x"), lax.axis_index("z")
    within, r, o = lax.rem(y, 2) * 2 + core, 2 * y + core, 4 * x + z
    blocks = jnp.arange(64)
    skip = CPAN * PANEL // BLK
    cyclic = (child_map % 6) * 16 + child_map // 6
    t = jnp.concatenate([jnp.zeros((2, skip), jnp.int32), cyclic], axis=1)
    valid = jnp.broadcast_to(blocks >= skip, (2, 64))
    kz = rank_in(t % 4, blocks // 4, valid)
    kx = rank_in(t % 16, blocks // 16, valid)
    kr = rank_in(t % 16 // 2, blocks // 16, valid)
    child = jnp.arange(2)[:, None]
    device, group = (blocks // 4)[None], (blocks // 16)[None]
    kinds = [
        (device == o, t % 4 * 2 + kz, blocks[None] % 4),
        ((group == x) & (t % 4 == z), t % 16 // 4 * 2 + kx, device % 4 * 2 + kz),
        (t % 16 == o, t // 16, group * 2 + kx),
        (group == within, t % 16 // 2 * 4 + kr, blocks[None] % 16),
        (t % 16 // 2 == r, t % 2 * 6 + t // 16, (child * 4 + group) * 4 + kr),
    ]
    lists = lambda k: jnp.stack([jnp.broadcast_to(a, (2, 64)) for a in k])
    place = jnp.where(lists([valid & k[0] for k in kinds]), lists([k[1] for k in kinds]), -1)
    says = lists([k[2] for k in kinds]) + 1
    match = place[:, :, None, :] == jnp.arange(32)[None, None, :, None]
    return (jnp.sum(jnp.where(match, says[:, :, None, :], 0), axis=3) - 1).reshape(-1)


Z_PICK, X_PICK, COL_FROM, R_PICK, ROW_FROM = (64 * k for k in range(5))


def whole(shape):
    return pl.BlockSpec(shape, lambda g, tab: (0,) * len(shape))


def part(shape):
    return pl.BlockSpec((1,) + shape, lambda g, tab: (g,) + (0,) * len(shape))


def local_call(kernel, grid, table, operands, in_specs, out_shapes, out_specs, scratch=()):
    return pl.pallas_call(
        kernel,
        grid_spec=pltpu.PrefetchScalarGridSpec(
            num_scalar_prefetch=1, grid=(grid,), in_specs=in_specs, out_specs=out_specs,
            scratch_shapes=list(scratch),
        ),
        out_shape=[jax.ShapeDtypeStruct(s, jnp.float32) for s in out_shapes],
        compiler_params=pltpu.CompilerParams(vmem_limit_bytes=56 * 1024 * 1024),
    )(table, *operands)


def at_least_zero(v):
    return jnp.maximum(v, 0)


def lanes(block):
    return pl.ds(pl.multiple_of(block * BLK, BLK), BLK)


PARTS = 4
SLICE = BLK // (2 * PARTS)


def extend_kernel(tab, front, *refs):
    ya_in, xb_in = refs[:PARTS], refs[PARTS : 2 * PARTS]
    send_sem, recv_sem, own_sem = refs[-3:]
    za_out, za_in, xa_out, xa_in, ya_out, yb_out, yb_in, zb_out, zb_in, xb_out = (
        refs[(2 + i) * PARTS : (3 + i) * PARTS] for i in range(10)
    )
    barrier = pltpu.get_barrier_semaphore()
    total = 0
    for ax in ("z", "x", ROW):
        me, size, ident = peers_of(ax)
        for d in range(1, size):
            pl.semaphore_signal(
                barrier, inc=1, device_id=ident(lax.rem(me + d, size)), device_id_type=MESH
            )
        total += size - 1

    started = []

    def send(number, src, dst, axes, count):
        me, size, ident = peers_of(axes)
        slot = lambda p: pl.ds(p * count, count)
        own = pltpu.make_async_copy(src.at[slot(me)], dst.at[slot(me)], own_sem.at[number])
        own.start()
        copies = []
        for d in sorted(range(1, size), key=lambda d: -min(d, size - d)):
            p = lax.rem(me + d, size)
            copy = pltpu.make_async_remote_copy(
                src_ref=src.at[slot(p)],
                dst_ref=dst.at[slot(me)],
                send_sem=send_sem.at[number, d],
                recv_sem=recv_sem.at[number, d],
                device_id=ident(p),
                device_id_type=MESH,
            )
            copy.start()
            copies.append(copy)
        started.extend(copies)
        return own, copies

    def arrive(transfer):
        own, copies = transfer
        own.wait()
        for copy in copies:
            copy.wait_recv()

    def each(count, body):
        lax.fori_loop(0, count, lambda g, _: (body(g), 0)[1], 0)

    own = 32 * (lax.axis_index("y") // 2)

    def entry(at):
        return tab[at]

    def pack_za(ch):
        rows = slice(ch * SLICE, (ch + 1) * SLICE)

        def body(g):
            za_out[ch][g] = front[entry(Z_PICK + own + g), :, rows, :]

        each(8, body)

    def pack_yb(ch):
        rows = slice((PARTS + ch) * SLICE, (PARTS + ch + 1) * SLICE)

        def body(g):
            yb_out[ch][g] = front[:, entry(R_PICK + own + g), rows, :]

        each(32, body)

    def pack_xa(ch):
        def body(g):
            xa_out[ch][g] = za_in[ch][entry(X_PICK + own + g)]

        each(8, body)

    def pack_zb(ch):
        def body(g):
            for c in range(2):
                column = entry(Z_PICK + c * 32 + g)
                for i in range(12):
                    source = entry(ROW_FROM + c * 32 + i)
                    zb_out[ch][g, c * 12 + i] = yb_in[ch][source, column]

        each(8, body)

    def pack_ya(ch):
        def body(g):
            i = entry(R_PICK + own + g)
            for slot in range(6):
                columns = slice(slot * BLK, slot * BLK + BLK)
                ya_out[ch][g, :, columns] = xa_in[ch][entry(COL_FROM + own + slot), i]

        each(32, body)

    def pack_xb(ch):
        def body(g):
            for c in range(2):
                rows = slice(c * 12, c * 12 + 12)
                xb_out[ch][g, rows] = zb_in[ch][entry(X_PICK + c * 32 + g), rows]

        each(8, body)

    stages = {
        "A": [
            (pack_za, "z", za_out, za_in, 2, 2), (pack_xa, "x", xa_out, xa_in, 2, 2),
            (pack_ya, ROW, ya_out, ya_in, 4, 3),
        ],
        "B": [
            (pack_yb, ROW, yb_out, yb_in, 4, 2), (pack_zb, "z", zb_out, zb_in, 2, 3),
            (pack_xb, "x", xb_out, xb_in, 2, 3),
        ],
    }
    free, pending, number = {"z": 0, "x": 0, ROW: 0}, [], 0

    def begin(time, half, ch, stage, packed=False):
        nonlocal number
        pack, axes, out, arriving, count, cost = stages[half][stage]
        if not packed:
            pack(ch)
        free[axes] = max(time, free[axes]) + cost
        pending.append((free[axes], number, half, ch, stage, send(number, out[ch], arriving[ch], axes, count)))
        number += 1

    pack_za(0)
    pl.semaphore_wait(barrier, total)
    begin(0, "A", 0, 0, packed=True)
    begin(0, "B", 0, 0)
    for ch in range(1, PARTS):
        pack_za(ch)
        pack_yb(ch)
    while pending:
        pending.sort(key=lambda p: p[:2])
        time, _, half, ch, stage, transfer = pending.pop(0)
        arrive(transfer)
        if stage == 0 and ch + 1 < PARTS:
            begin(time, half, ch + 1, 0, packed=True)
        if stage < 2:
            begin(time, half, ch, stage + 1)
    for copy in started:
        copy.wait_send()


def add_all(tab, root, *refs):
    i = pl.program_id(0)
    out = refs[-1]
    for slot in range(6):
        columns = slice(slot * BLK, slot * BLK + BLK)
        sums = [root[0, q * SLICE : (q + 1) * SLICE, columns] for q in range(2 * PARTS)]
        for c in range(2):
            mine = refs[c * 2 * PARTS : (c + 1) * 2 * PARTS]
            row, col = tab[ROW_FROM + c * 32 + i], tab[COL_FROM + c * 32 + slot]
            there = jnp.logical_and(row >= 0, col >= 0)
            col = at_least_zero(col)
            arrived = [m[0, :, columns] for m in mine[:PARTS]] + [m[col, 0] for m in mine[PARTS:]]
            sums = [s + jnp.where(there, a, 0.0) for s, a in zip(sums, arrived)]
        for q in range(2 * PARTS):
            out[0, q * SLICE : (q + 1) * SLICE, columns] = sums[q]


def extend_add(front, root_front, child_map):
    table = routes(child_map)
    blocks, rows, wide = (8, 16, SLICE, BLK), (32, SLICE, 768), (8, 24, SLICE, BLK)
    band = (32, 4, SLICE, BLK)
    buffers = [blocks] * (4 * PARTS) + [rows] * PARTS + [band] * (2 * PARTS) + [wide] * (3 * PARTS)
    arrived = pl.pallas_call(
        extend_kernel,
        out_shape=[jax.ShapeDtypeStruct(s, jnp.float32) for s in [rows] * PARTS + [wide] * PARTS],
        in_specs=[
            pl.BlockSpec(memory_space=pltpu.SMEM), pl.BlockSpec(memory_space=pltpu.VMEM),
        ],
        out_specs=[pl.BlockSpec(memory_space=pl.ANY)] * (2 * PARTS),
        scratch_shapes=[
            *[pltpu.VMEM(s, jnp.float32) for s in buffers],
            pltpu.SemaphoreType.DMA((6 * PARTS, 8)),
            pltpu.SemaphoreType.DMA((6 * PARTS, 8)),
            pltpu.SemaphoreType.DMA((6 * PARTS,)),
        ],
        compiler_params=pltpu.CompilerParams(
            collective_id=1, has_side_effects=True, vmem_limit_bytes=58 * 1024 * 1024
        ),
    )(jnp.maximum(table, 0), front.reshape(4, 16, BLK, BLK))
    operands, specs = [], []
    for c in range(2):
        from_rows = lambda g, tab, c=c: (at_least_zero(tab[ROW_FROM + c * 32 + g]), 0, 0)
        from_wide = lambda g, tab, c=c: (0, c * 12 + g, 0, 0)
        operands += arrived
        specs += [pl.BlockSpec((1,) + rows[1:], from_rows)] * PARTS
        specs += [pl.BlockSpec((8, 1, SLICE, BLK), from_wide)] * PARTS
    (assembled,) = local_call(
        add_all, 12, table, (root_front.reshape(12, BLK, 768), *operands),
        [part((BLK, 768)), *specs], [(12, BLK, 768)], [part((BLK, 768))],
    )
    return assembled.reshape(root_front.shape)


def pick(arrived, owners):
    parts = [
        lax.dynamic_index_in_dim(arrived[..., q * PANEL : (q + 1) * PANEL], owner, 0, keepdims=False)
        for q, owner in enumerate(owners)
    ]
    return jnp.concatenate(parts, axis=-1)


def gather_bands(cols, rows, col_off, xs, zs, row_owners, axes, size, first_id):
    count, width = cols.shape
    panels, _, span = rows.shape
    piece = PANEL // size
    cols = cols.reshape(2, 4, count // 8, width)
    rows = rows.reshape(panels, size, piece, span)
    first, second, slices = exchange(
        [swap_half(cols, "z", 0), swap_half(cols, "x", 1), swap_inner(rows, axes)], first_id
    )
    first, second = pick(first, zs), pick(second, xs)
    slices = jnp.stack(
        [lax.dynamic_index_in_dim(slices[:, k], owner, 0, keepdims=False) for k, owner in enumerate(row_owners)]
    )
    cross = jnp.concatenate(
        [lax.dynamic_slice_in_dim(slices, off, PANEL, 2) for off in col_off], axis=2
    )
    split = lambda a: a.reshape(4, count // 32, width)
    half = span // 2
    first, second, upper, lower, left = exchange(
        [
            swap(split(first), "x"), swap(split(second), "z"),
            share(cross[:, : piece // 2], "z", 4), share(cross[:, piece // 2 :], "x", 4),
            share_inner(slices[..., :half], axes, size),
        ],
        first_id + 1,
    )
    first, second = pick(first, xs), pick(second, zs)
    upper, lower = pick(upper, zs), pick(lower, xs)
    first, second, upper, lower, right = exchange(
        [
            share(first, "x", 4), share(second, "z", 4),
            share(upper, "x", 4), share(lower, "z", 4),
            share_inner(slices[..., half:], axes, size),
        ],
        first_id + 2,
    )
    cross = jnp.concatenate([pick(upper, xs), pick(lower, zs)], axis=1)
    join = lambda a: a.reshape(count // 8, width)
    first, second, cross = exchange(
        [share(join(first), "z", 4), share(join(second), "x", 4), share_inner(cross, axes, size)],
        first_id + 3,
    )
    halves = [a.reshape(count // 2, width) for a in (first, second)]
    left, right = (a.reshape(width, half) for a in (left, right))
    return halves, left, right, cross.reshape(width, width)


PARENT = {
    (3, 0): (0, 0), (3, 3): (3, 0), (3, 1): (3, 0), (2, 0): (3, 0), (2, 3): (2, 0),
    (3, 2): (3, 1), (0, 1): (3, 1), (0, 3): (3, 3), (2, 1): (3, 1), (1, 0): (2, 0),
    (2, 2): (3, 2), (1, 1): (2, 1), (0, 2): (3, 2), (1, 3): (2, 3), (1, 2): (2, 2),
}


def turned(place, quarter_turns):
    for _ in range(quarter_turns):
        place = (-place[1] % 4, place[0])
    return place


def tree_children(turn):
    children = [[] for _ in range(16)]
    for child, parent in PARENT.items():
        child, parent = turned(child, turn), turned(parent, turn)
        children[4 * parent[0] + parent[1]].append(4 * child[0] + child[1])
    return children


def tree_depth(turn):
    depth = [0] * 16
    for place in PARENT:
        node, hops = place, 0
        while node != (0, 0):
            node, hops = PARENT[node], hops + 1
        place = turned(place, turn)
        depth[4 * place[0] + place[1]] = hops
    return depth


def lookup(values, index):
    result = jnp.int32(values[0])
    for k in range(1, len(values)):
        result = jnp.where(index == k, jnp.int32(values[k]), result)
    return result


CHUNK = 32
CHUNKS = 2048 // (4 * CHUNK)
CROSS = CPAN * PANEL // (4 * CHUNK)
U_PARTS = 4
DEPTH = 5
SLACK = 2
U_TURN = 8


def spread_kernel(front, cols, rows, cross, recv, send, cross_recv, cross_send, rows_recv,
                  rows_send, own_sem, stage):
    y, core = lax.axis_index("y"), lax.axis_index("core")
    x, z = lax.axis_index("x"), lax.axis_index("z")
    place, within = 4 * x + z, lax.rem(y, 2) * 2 + core
    is_root = place == 0
    tables = [tree_children(turn) for turn in range(4)]
    target = [
        [lookup([(t[k] + [-1, -1, -1])[s] for k in range(16)], place) for s in range(3)]
        for t in tables
    ]
    depth = [lookup(tree_depth(turn), place) for turn in range(4)]
    sibling = {"core": 1 - core}
    above = {"y": y // 2 * 2 + 1 - lax.rem(y, 2)}

    barrier = pltpu.get_barrier_semaphore()
    for ident in (
        {"x": lax.rem(x + 1, 4)}, {"x": lax.rem(x + 3, 4)},
        {"z": lax.rem(z + 1, 4)}, {"z": lax.rem(z + 3, 4)}, sibling, above,
    ):
        pl.semaphore_signal(barrier, inc=1, device_id=ident, device_id_type=MESH)

    part = CPAN * PANEL // U_PARTS
    whole_band = pl.ds(0, CPAN * PANEL)
    load_own = pltpu.make_async_copy(front, stage, own_sem.at[0])
    own_cols = pltpu.make_async_copy(stage, cols, own_sem.at[0])
    own_rows = pltpu.make_async_copy(stage.at[whole_band], rows, own_sem.at[1])
    load_own.start()
    load_cross = pltpu.make_async_copy(
        cols.at[whole_band], stage.at[whole_band], own_sem.at[2]
    )
    store_cross = pltpu.make_async_copy(stage.at[whole_band], cross, own_sem.at[2])
    pl.semaphore_wait(barrier, 6)

    def rows_copy(src, k, way, ident):
        span = pl.ds(k * part, part)
        return pltpu.make_async_remote_copy(
            src_ref=src.at[span], dst_ref=rows.at[span], send_sem=rows_send.at[way, k],
            recv_sem=rows_recv.at[k], device_id=ident, device_id_type=MESH,
        )

    def band(c, q):
        return pl.ds(pl.multiple_of((c * 4 + q) * CHUNK, CHUNK), CHUNK)

    def cols_copy(src, c, q, s):
        span = band(c, q)
        there = jnp.maximum(target[q][s], 0)
        return pltpu.make_async_remote_copy(
            src_ref=src.at[span], dst_ref=cols.at[span], send_sem=send.at[q, s, c],
            recv_sem=recv.at[q, c], device_id={"x": there // 4, "z": lax.rem(there, 4)},
            device_id_type=MESH,
        )

    def cross_copy(src, c, q, way, ident):
        span = band(c, q)
        return pltpu.make_async_remote_copy(
            src_ref=src.at[span], dst_ref=cross.at[span], send_sem=cross_send.at[way, q, c],
            recv_sem=cross_recv.at[q, c], device_id=ident, device_id_type=MESH,
        )

    @pl.when(within == 0)
    def _():
        for k in range(U_PARTS):
            rows_copy(front, k, 0, above).start()
            rows_copy(front, k, 1, sibling).start()

    load_own.wait()

    @pl.when(is_root)
    def _():
        own_cols.start()

    @pl.when(within == 0)
    def _():
        own_rows.start()
        own_rows.wait()

    @pl.when(is_root)
    def _():
        own_cols.wait()

    def both(first, second):
        return jnp.logical_and(first, second)

    def pass_cols(c, q):
        @pl.when(is_root)
        def _():
            cols_copy(front, c, q, 0).start()

            @pl.when(both(within == 0, c < CROSS))
            def _():
                cross_copy(front, c, q, 0, above).start()
                cross_copy(front, c, q, 1, sibling).start()

        @pl.when(jnp.logical_not(is_root))
        def _():
            cols_copy(cols, c, q, 0).wait_recv()
            for s in range(3):

                @pl.when(target[q][s] >= 0)
                def _():
                    cols_copy(cols, c, q, s).start()

            @pl.when(both(within == 0, c < CROSS))
            def _():
                cross_copy(cols, c, q, 0, above).start()
                cross_copy(cols, c, q, 1, sibling).start()

    def loop(lo, hi, body):
        lax.fori_loop(lo, hi, lambda c, _: (body(c), 0)[1], 0)

    def step(turn):
        for q in range(4):
            c = turn - SLACK * depth[q]

            @pl.when(both(c >= 0, c < CHUNKS))
            def _():
                pass_cols(c, q)

        for q in range(4):
            late = turn - SLACK * (depth[q] + 1)

            @pl.when(both(within == 2, both(late >= 0, late < CROSS)))
            def _():
                cross_copy(cross, late, q, 0, above).wait_recv()
                cross_copy(cross, late, q, 1, sibling).start()

        for k in range(U_PARTS):

            @pl.when(both(within == 2, turn == U_TURN + k))
            def _():
                rows_copy(rows, k, 0, above).wait_recv()
                rows_copy(rows, k, 1, sibling).start()

        @pl.when(both(within == 0, turn == CROSS + SLACK * DEPTH))
        def _():
            load_cross.start()

        @pl.when(both(within == 0, turn == CROSS + SLACK * DEPTH + 3))
        def _():
            load_cross.wait()
            store_cross.start()

    loop(0, CHUNKS + SLACK * DEPTH, step)

    @pl.when(within == 0)
    def _():
        for k in range(U_PARTS):
            rows_copy(front, k, 0, above).wait_send()
            rows_copy(front, k, 1, sibling).wait_send()

        def send_done(c):
            for q in range(4):
                cross_copy(front, c, q, 0, above).wait_send()
                cross_copy(front, c, q, 1, sibling).wait_send()

        loop(0, CROSS, send_done)

    @pl.when(within == 2)
    def _():
        for k in range(U_PARTS):
            rows_copy(rows, k, 1, sibling).wait_send()

        def send_done(c):
            for q in range(4):
                cross_copy(cross, c, q, 1, sibling).wait_send()

        loop(0, CROSS, send_done)

    @pl.when(lax.rem(within, 2) == 1)
    def _():
        for k in range(U_PARTS):
            rows_copy(rows, k, 0, sibling).wait_recv()

        def arrived(c):
            for q in range(4):
                cross_copy(cross, c, q, 0, sibling).wait_recv()

        loop(0, CROSS, arrived)

    def cols_done(c):
        for q in range(4):
            for s in range(3):

                @pl.when(target[q][s] >= 0)
                def _():
                    cols_copy(front, c, q, s).wait_send()

    loop(0, CHUNKS, cols_done)

    @pl.when(within == 0)
    def _():
        store_cross.wait()


def spread(front, collective_id):
    rows, cols = front.shape
    width = CPAN * PANEL
    shapes = [(rows, width), (width, cols), (width, width)]
    dma = pltpu.SemaphoreType.DMA
    return pl.pallas_call(
        spread_kernel,
        out_shape=[jax.ShapeDtypeStruct(s, jnp.float32) for s in shapes],
        in_specs=[pl.BlockSpec(memory_space=pl.ANY)],
        out_specs=[pl.BlockSpec(memory_space=pl.ANY)] * 3,
        scratch_shapes=[
            dma((4, CHUNKS)), dma((4, 3, CHUNKS)), dma((4, CROSS)), dma((2, 4, CROSS)),
            dma((U_PARTS,)), dma((2, U_PARTS)), dma((3,)), pltpu.VMEM(front.shape, jnp.float32),
        ],
        compiler_params=pltpu.CompilerParams(
            collective_id=collective_id, has_side_effects=True, vmem_limit_bytes=32 * 1024 * 1024
        ),
    )(front)


def dot(a, b, precision=HIGH):
    return jnp.dot(a, b, precision=precision, preferred_element_type=jnp.float32)


def newton(block):
    shape = (PANEL, PANEL)
    eye = lax.broadcasted_iota(jnp.int32, shape, 0) == lax.broadcasted_iota(jnp.int32, shape, 1)
    kept = jnp.where(eye, block, 0.0)
    by_col = 1.0 / jnp.sum(kept, axis=0, keepdims=True)
    by_row = 1.0 / jnp.sum(kept, axis=1, keepdims=True)
    identity = jnp.where(eye, 1.0, 0.0)
    error = identity - block * by_col
    product = identity + error
    for _ in range(3):
        error = dot(error, error, HIGHEST)
        product = product + dot(product, error, HIGHEST)
    return product * by_row


def panel(k):
    return slice(k * PANEL, (k + 1) * PANEL)


def finish_kernel(n, row_panels, col_panels, precision, bands, tail, tab, front, *refs):
    cols, rows, cross, outs = refs[:bands], refs[bands:tail], refs[tail], refs[tail + 1 : -3]
    work, inverse, pivots = refs[-3:]
    g = pl.program_id(0)

    @pl.when(g == 0)
    def _():
        work[...] = cross[...]
        for i, part in enumerate(rows):
            span = part.shape[1]
            pivots[:, i * span : (i + 1) * span] = part[...]
        for k in range(n):
            inverse[k] = newton(work[panel(k), panel(k)])
            for p in range(k + 1, n):
                factor = dot(work[panel(p), panel(k)], inverse[k], HIGHEST)
                for q in range(k + 1, n):
                    work[panel(p), panel(q)] -= dot(factor, work[panel(k), panel(q)], HIGHEST)
                pivots[panel(p), :] -= dot(factor, pivots[panel(k), :], HIGHEST)
        for j in range(col_panels):
            for k in range(n):
                pivots[panel(k), panel(j)] = jnp.where(
                    tab[row_panels + j] > k, pivots[panel(k), panel(j)], 0.0
                )

    mine = cols[0][...]
    if bands == 2:
        mine = jnp.where(g < row_panels // 2, mine, cols[1][...])
    band = [mine[:, panel(k)] for k in range(n)]
    for k in range(n):
        band[k] = dot(band[k], inverse[k], HIGHEST)
        for q in range(k + 1, n):
            band[q] = band[q] - dot(band[k], work[panel(k), panel(q)], HIGHEST)
    band = [jnp.where(tab[g] > k, band[k], 0.0) for k in range(n)]
    factors = jnp.concatenate(band, axis=1)
    for j in range(col_panels):
        new = front[:, panel(j)] - dot(factors, pivots[:, panel(j)], precision)
        for k in range(n):
            here = jnp.logical_and(tab[row_panels + j] == k, tab[g] > k)
            new = jnp.where(here, band[k], new)
        outs[0][:, panel(j)] = new
        if len(outs) == 2:
            outs[1][2 * j] = new[:, :BLK]
            outs[1][2 * j + 1] = new[:, BLK:]


def finish(front, bands, pivot_rows, cross, row_step, col_step, precision, blocked=False):
    rows, cols = front.shape
    width = cross.shape[0]
    n, row_panels, col_panels = width // PANEL, rows // PANEL, cols // PANEL
    half = row_panels // 2
    keep = lambda shape: pl.BlockSpec(shape, lambda g, tab: (0, 0))
    if len(bands) == 1:
        band_specs = [pl.BlockSpec((PANEL, width), lambda g, tab: (g, 0))]
    else:
        band_specs = [
            pl.BlockSpec((PANEL, width), lambda g, tab: (jnp.minimum(g, half - 1), 0)),
            pl.BlockSpec((PANEL, width), lambda g, tab: (jnp.maximum(g - half, 0), 0)),
        ]
    return local_call(
        functools.partial(finish_kernel, n, row_panels, col_panels, precision, len(bands), len(bands) + len(pivot_rows)),
        row_panels,
        jnp.concatenate([row_step, col_step]).astype(jnp.int32),
        (front, *bands, *pivot_rows, cross),
        [
            pl.BlockSpec((PANEL, cols), lambda g, tab: (g, 0)),
            *band_specs,
            *[keep(p.shape) for p in pivot_rows],
            keep(cross.shape),
        ],
        [front.shape] + [(cols // BLK, rows, BLK)] * blocked,
        [pl.BlockSpec((PANEL, cols), lambda g, tab: (g, 0))]
        + [pl.BlockSpec((cols // BLK, PANEL, BLK), lambda g, tab: (0, g, 0))] * blocked,
        scratch=[
            pltpu.VMEM((width, width), jnp.float32),
            pltpu.VMEM((n, PANEL, PANEL), jnp.float32),
            pltpu.VMEM((width, cols), jnp.float32),
        ],
    )


def body(child_fronts, root_front, child_map, panel_order):
    y, core = lax.axis_index("y"), lax.axis_index("core")
    r, o = 2 * y + core, 4 * lax.axis_index("x") + lax.axis_index("z")
    within = lax.rem(y, 2) * 2 + core

    pivot_cols, pivot_rows, cross = spread(child_fronts, 10)
    row_panel, col_panel = within * 8 + jnp.arange(8), o * 2 + jnp.arange(2)
    row_step = jnp.where(row_panel < CPAN, row_panel, NEVER)
    col_step = jnp.where(col_panel < CPAN, col_panel, NEVER)
    factored, blocks = finish(
        child_fronts, [pivot_cols], [pivot_rows], cross, row_step, col_step, HIGHEST, True
    )

    assembled = extend_add(blocks, root_front, child_map)

    row_panels, col_panels = 6, 3
    order = panel_order.astype(jnp.uint32)
    each = lambda a: [a[k] for k in range(RPAN)]
    col_off = each(order % col_panels * PANEL)
    row_off = each(order % row_panels * PANEL)
    owner_x, owner_z = each(order // (4 * col_panels)), each(order // col_panels % 4)
    owner_row = each(order // row_panels)
    cols = jnp.concatenate([lax.dynamic_slice_in_dim(assembled, off, PANEL, 1) for off in col_off], 1)
    rows = jnp.stack([lax.dynamic_slice_in_dim(assembled, off, PANEL, 0) for off in row_off])
    halves, left, right, cross = gather_bands(
        cols, rows, col_off, owner_x, owner_z, owner_row, ROW, 8, 20,
    )

    def steps(places):
        match = places[:, None] == panel_order[None, :]
        return jnp.min(jnp.where(match, jnp.arange(RPAN)[None, :], NEVER), axis=1)

    row_step = steps(r * row_panels + jnp.arange(row_panels))
    col_step = steps(o * col_panels + jnp.arange(col_panels))
    return factored, finish(assembled, halves, [left, right], cross, row_step, col_step, HIGH)[0]


def solution(mesh):
    grid = Mesh(mesh.devices.reshape(4, 2, 4, 4), ("y", "core", "x", "z"))
    return jax.shard_map(
        body,
        mesh=grid,
        in_specs=(P(ROW, COL), P(ROW, COL), P(), P()),
        out_specs=(P(ROW, COL), P(ROW, COL)),
        check_vma=False,
    )
```

```python
import functools

import jax
import jax.numpy as jnp
from jax import lax
from jax.experimental import pallas as pl
from jax.experimental.pallas import tpu as pltpu
from jax.sharding import Mesh
from jax.sharding import PartitionSpec as P

PANEL = 256
BLK = 128
CPAN = 2
RPAN = 3

ROW = ("y", "core")
COL = ("x", "z")
MESH = pl.DeviceIdType.MESH
NEVER = 99

HIGH = lax.Precision.HIGH
HIGHEST = lax.Precision.HIGHEST


def peers_of(axes):
    y, core = lax.axis_index("y"), lax.axis_index("core")
    if axes == ROW:
        return 2 * y + core, 8, lambda p: {"y": p // 2, "core": lax.rem(p, 2)}
    if axes == "child":
        pair = y // 2 * 2
        me = lax.rem(y, 2) * 2 + core
        return me, 4, lambda p: {"y": pair + p // 2, "core": lax.rem(p, 2)}
    return lax.axis_index(axes), 4, lambda p: {axes: p}


def rank_in(key, group, valid):
    n = key.shape[1]
    earlier = jnp.arange(n)[None, :] < jnp.arange(n)[:, None]
    same = (key[:, :, None] == key[:, None, :]) & (group[:, None] == group[None, :])[None]
    return jnp.sum((same & valid[:, None, :] & earlier[None]).astype(jnp.int32), axis=2)


def routes(child_map):
    y, core = lax.axis_index("y"), lax.axis_index("core")
    x, z = lax.axis_index("x"), lax.axis_index("z")
    within, r, o = lax.rem(y, 2) * 2 + core, 2 * y + core, 4 * x + z
    blocks = jnp.arange(64)
    skip = CPAN * PANEL // BLK
    cyclic = (child_map % 6) * 16 + child_map // 6
    t = jnp.concatenate([jnp.zeros((2, skip), jnp.int32), cyclic], axis=1)
    valid = jnp.broadcast_to(blocks >= skip, (2, 64))
    kz = rank_in(t % 4, blocks // 4, valid)
    kx = rank_in(t % 16, blocks // 16, valid)
    kr = rank_in(t % 16 // 2, blocks // 16, valid)
    child = jnp.arange(2)[:, None]
    device, group = (blocks // 4)[None], (blocks // 16)[None]
    kinds = [
        (device == o, t % 4 * 2 + kz, blocks[None] % 4),
        ((group == x) & (t % 4 == z), t % 16 // 4 * 2 + kx, device % 4 * 2 + kz),
        (t % 16 == o, t // 16, group * 2 + kx),
        (group == within, t % 16 // 2 * 4 + kr, blocks[None] % 16),
        (t % 16 // 2 == r, t % 2 * 6 + t // 16, (child * 4 + group) * 4 + kr),
    ]
    lists = lambda k: jnp.stack([jnp.broadcast_to(a, (2, 64)) for a in k])
    place = jnp.where(lists([valid & k[0] for k in kinds]), lists([k[1] for k in kinds]), -1)
    says = lists([k[2] for k in kinds]) + 1
    match = place[:, :, None, :] == jnp.arange(32)[None, None, :, None]
    return (jnp.sum(jnp.where(match, says[:, :, None, :], 0), axis=3) - 1).reshape(-1)


Z_PICK, X_PICK, COL_FROM, R_PICK, ROW_FROM = (64 * k for k in range(5))


def whole(shape):
    return pl.BlockSpec(shape, lambda g, tab: (0,) * len(shape))


def part(shape):
    return pl.BlockSpec((1,) + shape, lambda g, tab: (g,) + (0,) * len(shape))


def local_call(kernel, grid, table, operands, in_specs, out_shapes, out_specs, scratch=()):
    return pl.pallas_call(
        kernel,
        grid_spec=pltpu.PrefetchScalarGridSpec(
            num_scalar_prefetch=1, grid=(grid,), in_specs=in_specs, out_specs=out_specs,
            scratch_shapes=list(scratch),
        ),
        out_shape=[jax.ShapeDtypeStruct(s, jnp.float32) for s in out_shapes],
        compiler_params=pltpu.CompilerParams(vmem_limit_bytes=56 * 1024 * 1024),
    )(table, *operands)


def at_least_zero(v):
    return jnp.maximum(v, 0)


def lanes(block):
    return pl.ds(pl.multiple_of(block * BLK, BLK), BLK)


PARTS = 4
SLICE = BLK // (2 * PARTS)


def extend_kernel(tab, front, *refs):
    ya_in, xb_in = refs[:PARTS], refs[PARTS : 2 * PARTS]
    send_sem, recv_sem, own_sem = refs[-3:]
    za_out, za_in, xa_out, xa_in, ya_out, yb_out, yb_in, zb_out, zb_in, xb_out = (
        refs[(2 + i) * PARTS : (3 + i) * PARTS] for i in range(10)
    )
    barrier = pltpu.get_barrier_semaphore()
    total = 0
    for ax in ("z", "x", ROW):
        me, size, ident = peers_of(ax)
        for d in range(1, size):
            pl.semaphore_signal(
                barrier, inc=1, device_id=ident(lax.rem(me + d, size)), device_id_type=MESH
            )
        total += size - 1

    started = []

    def send(number, src, dst, axes, count):
        me, size, ident = peers_of(axes)
        slot = lambda p: pl.ds(p * count, count)
        own = pltpu.make_async_copy(src.at[slot(me)], dst.at[slot(me)], own_sem.at[number])
        own.start()
        copies = []
        for d in sorted(range(1, size), key=lambda d: -min(d, size - d)):
            p = lax.rem(me + d, size)
            copy = pltpu.make_async_remote_copy(
                src_ref=src.at[slot(p)],
                dst_ref=dst.at[slot(me)],
                send_sem=send_sem.at[number, d],
                recv_sem=recv_sem.at[number, d],
                device_id=ident(p),
                device_id_type=MESH,
            )
            copy.start()
            copies.append(copy)
        started.extend(copies)
        return own, copies

    def arrive(transfer):
        own, copies = transfer
        own.wait()
        for copy in copies:
            copy.wait_recv()

    def each(count, body):
        lax.fori_loop(0, count, lambda g, _: (body(g), 0)[1], 0)

    own = 32 * (lax.axis_index("y") // 2)

    def entry(at):
        return tab[at]

    def pack_za(ch):
        rows = slice(ch * SLICE, (ch + 1) * SLICE)

        def body(g):
            za_out[ch][g] = front[entry(Z_PICK + own + g), :, rows, :]

        each(8, body)

    def pack_yb(ch):
        rows = slice((PARTS + ch) * SLICE, (PARTS + ch + 1) * SLICE)

        def body(g):
            yb_out[ch][g] = front[:, entry(R_PICK + own + g), rows, :]

        each(32, body)

    def pack_xa(ch):
        def body(g):
            xa_out[ch][g] = za_in[ch][entry(X_PICK + own + g)]

        each(8, body)

    def pack_zb(ch):
        def body(g):
            for c in range(2):
                column = entry(Z_PICK + c * 32 + g)
                for i in range(12):
                    source = entry(ROW_FROM + c * 32 + i)
                    zb_out[ch][g, c * 12 + i] = yb_in[ch][source, column]

        each(8, body)

    def pack_ya(ch):
        def body(g):
            i = entry(R_PICK + own + g)
            for slot in range(6):
                columns = slice(slot * BLK, slot * BLK + BLK)
                ya_out[ch][g, :, columns] = xa_in[ch][entry(COL_FROM + own + slot), i]

        each(32, body)

    def pack_xb(ch):
        def body(g):
            for c in range(2):
                rows = slice(c * 12, c * 12 + 12)
                xb_out[ch][g, rows] = zb_in[ch][entry(X_PICK + c * 32 + g), rows]

        each(8, body)

    stages = {
        "A": [
            (pack_za, "z", za_out, za_in, 2, 2), (pack_xa, "x", xa_out, xa_in, 2, 2),
            (pack_ya, ROW, ya_out, ya_in, 4, 3),
        ],
        "B": [
            (pack_yb, ROW, yb_out, yb_in, 4, 2), (pack_zb, "z", zb_out, zb_in, 2, 3),
            (pack_xb, "x", xb_out, xb_in, 2, 3),
        ],
    }
    free, pending, number = {"z": 0, "x": 0, ROW: 0}, [], 0

    def begin(time, half, ch, stage, packed=False):
        nonlocal number
        pack, axes, out, arriving, count, cost = stages[half][stage]
        if not packed:
            pack(ch)
        free[axes] = max(time, free[axes]) + cost
        pending.append((free[axes], number, half, ch, stage, send(number, out[ch], arriving[ch], axes, count)))
        number += 1

    pack_za(0)
    pl.semaphore_wait(barrier, total)
    begin(0, "A", 0, 0, packed=True)
    begin(0, "B", 0, 0)
    for ch in range(1, PARTS):
        pack_za(ch)
        pack_yb(ch)
    while pending:
        pending.sort(key=lambda p: p[:2])
        time, _, half, ch, stage, transfer = pending.pop(0)
        arrive(transfer)
        if stage == 0 and ch + 1 < PARTS:
            begin(time, half, ch + 1, 0, packed=True)
        if stage < 2:
            begin(time, half, ch, stage + 1)
    for copy in started:
        copy.wait_send()


def add_all(tab, root, *refs):
    i = pl.program_id(0)
    out = refs[-1]
    for slot in range(6):
        columns = slice(slot * BLK, slot * BLK + BLK)
        sums = [root[0, q * SLICE : (q + 1) * SLICE, columns] for q in range(2 * PARTS)]
        for c in range(2):
            mine = refs[c * 2 * PARTS : (c + 1) * 2 * PARTS]
            row, col = tab[ROW_FROM + c * 32 + i], tab[COL_FROM + c * 32 + slot]
            there = jnp.logical_and(row >= 0, col >= 0)
            col = at_least_zero(col)
            arrived = [m[0, :, columns] for m in mine[:PARTS]] + [m[col, 0] for m in mine[PARTS:]]
            sums = [s + jnp.where(there, a, 0.0) for s, a in zip(sums, arrived)]
        for q in range(2 * PARTS):
            out[0, q * SLICE : (q + 1) * SLICE, columns] = sums[q]


def extend_add(front, root_front, child_map):
    table = routes(child_map)
    blocks, rows, wide = (8, 16, SLICE, BLK), (32, SLICE, 768), (8, 24, SLICE, BLK)
    band = (32, 4, SLICE, BLK)
    buffers = [blocks] * (4 * PARTS) + [rows] * PARTS + [band] * (2 * PARTS) + [wide] * (3 * PARTS)
    arrived = pl.pallas_call(
        extend_kernel,
        out_shape=[jax.ShapeDtypeStruct(s, jnp.float32) for s in [rows] * PARTS + [wide] * PARTS],
        in_specs=[
            pl.BlockSpec(memory_space=pltpu.SMEM), pl.BlockSpec(memory_space=pltpu.VMEM),
        ],
        out_specs=[pl.BlockSpec(memory_space=pl.ANY)] * (2 * PARTS),
        scratch_shapes=[
            *[pltpu.VMEM(s, jnp.float32) for s in buffers],
            pltpu.SemaphoreType.DMA((6 * PARTS, 8)),
            pltpu.SemaphoreType.DMA((6 * PARTS, 8)),
            pltpu.SemaphoreType.DMA((6 * PARTS,)),
        ],
        compiler_params=pltpu.CompilerParams(
            collective_id=1, has_side_effects=True, vmem_limit_bytes=58 * 1024 * 1024
        ),
    )(jnp.maximum(table, 0), front.reshape(4, 16, BLK, BLK))
    operands, specs = [], []
    for c in range(2):
        from_rows = lambda g, tab, c=c: (at_least_zero(tab[ROW_FROM + c * 32 + g]), 0, 0)
        from_wide = lambda g, tab, c=c: (0, c * 12 + g, 0, 0)
        operands += arrived
        specs += [pl.BlockSpec((1,) + rows[1:], from_rows)] * PARTS
        specs += [pl.BlockSpec((8, 1, SLICE, BLK), from_wide)] * PARTS
    (assembled,) = local_call(
        add_all, 12, table, (root_front.reshape(12, BLK, 768), *operands),
        [part((BLK, 768)), *specs], [(12, BLK, 768)], [part((BLK, 768))],
    )
    return assembled.reshape(root_front.shape)


def gather_kernel(tab, cols, rows, upper, lower, rows_out, cross_out, *refs):
    (arrived_a, arrived_b, arrived_rows, mine, mine_blocks, cross_a, cross_b, cross_a1, cross_b1,
     cross_a2, cross_b2, cross_a3, cross_b3, cross_all, a1, b1, a2, b2, a3, b3, a4, b4) = refs[:-3]
    send_sem, recv_sem, own_sem = refs[-3:]
    barrier = pltpu.get_barrier_semaphore()
    total = 0
    for ax in ("z", "x", ROW):
        me, size, ident = peers_of(ax)
        for d in range(1, size):
            pl.semaphore_signal(
                barrier, inc=1, device_id=ident(lax.rem(me + d, size)), device_id_type=MESH
            )
        total += size - 1
    started = []

    def send(number, src, dst, axes):
        me, size, ident = peers_of(axes)
        own = pltpu.make_async_copy(src(me), dst(me), own_sem.at[number])
        own.start()
        copies = []
        for d in sorted(range(1, size), key=lambda d: -min(d, size - d)):
            p = lax.rem(me + d, size)
            copy = pltpu.make_async_remote_copy(
                src_ref=src(p),
                dst_ref=dst(me),
                send_sem=send_sem.at[number, d],
                recv_sem=recv_sem.at[number, d],
                device_id=ident(p),
                device_id_type=MESH,
            )
            copy.start()
            copies.append(copy)
        started.extend(copies)
        return own, copies

    def arrive(*transfers):
        for own, copies in transfers:
            own.wait()
            for copy in copies:
                copy.wait_recv()

    def slot(ref):
        return lambda p: ref.at[p]

    def inner(ref):
        return lambda p: ref.at[:, p]

    def same(ref):
        return lambda p: ref

    owner_x = [tab[k] for k in range(RPAN)]
    owner_z = [tab[RPAN + k] for k in range(RPAN)]
    owner_row = [tab[2 * RPAN + k] for k in range(RPAN)]
    owned = [tab[3 * RPAN + k] for k in range(RPAN)]

    pl.semaphore_wait(barrier, total)
    t_rows = send(0, inner(rows), slot(arrived_rows), ROW)
    t_a = send(1, lambda p: cols.at[0, p], slot(arrived_a), "z")
    t_b = send(2, lambda p: cols.at[1, p], slot(arrived_b), "x")

    arrive(t_rows)
    for k in range(RPAN):
        mine[k] = arrived_rows[owner_row[k], k]
        for j in range(3):
            mine_blocks[j, k] = arrived_rows[owner_row[k], k, :, panel(j)]
    half = mine.shape[1] // 2
    for q in range(RPAN):
        block = mine_blocks[owned[q]]
        cross_a[:, :, panel(q)] = block[:, :half]
        cross_b[:, :, panel(q)] = block[:, half:]
    t_cross_a = send(3, same(cross_a), slot(cross_a1), "z")
    t_cross_b = send(4, same(cross_b), slot(cross_b1), "x")
    t_mine = send(5, same(mine), inner(rows_out), ROW)

    piece = a1.shape[1]

    def split(transfer, arrived, owners, out):
        arrive(transfer)
        for q in range(RPAN):
            for p in range(4):
                out[p, :, panel(q)] = arrived[owners[q], p * piece : (p + 1) * piece, panel(q)]

    def select(transfer, arrived, owners, out):
        arrive(transfer)
        for q in range(RPAN):
            out[..., panel(q)] = arrived[owners[q], ..., panel(q)]

    split(t_a, arrived_a, owner_z, a1)
    t_a = send(6, slot(a1), slot(a2), "x")
    split(t_b, arrived_b, owner_x, b1)
    t_b = send(7, slot(b1), slot(b2), "z")
    select(t_cross_a, cross_a1, owner_z, cross_a2)
    t_cross_a = send(8, same(cross_a2), slot(cross_a3), "x")
    select(t_cross_b, cross_b1, owner_x, cross_b2)
    t_cross_b = send(9, same(cross_b2), slot(cross_b3), "z")
    select(t_a, a2, owner_x, a3)
    t_a = send(10, same(a3), slot(a4), "x")
    select(t_b, b2, owner_z, b3)
    t_b = send(11, same(b3), slot(b4), "z")
    arrive(t_cross_a, t_cross_b)
    for q in range(RPAN):
        cross_all[:, :half, panel(q)] = cross_a3[owner_x[q], :, :, panel(q)]
        cross_all[:, half:, panel(q)] = cross_b3[owner_z[q], :, :, panel(q)]
    t_cross = send(12, same(cross_all), inner(cross_out), ROW)
    arrive(t_a)
    t_a = send(13, same(a4), slot(upper), "z")
    arrive(t_b)
    t_b = send(14, same(b4), slot(lower), "x")
    arrive(t_mine, t_cross, t_a, t_b)
    for copy in started:
        copy.wait_send()


def gather_bands(cols, rows, table, collective_id):
    count, width = cols.shape
    piece, span = PANEL // 8, rows.shape[2]
    band, ring = (RPAN, 8, piece, span), (4, count // 8, width)
    small, cross = (4, count // 32, width), (RPAN, piece // 2, width)
    full = (4,) + small
    buffers = [
        ring, ring, (8, RPAN, piece, span), (RPAN, piece, span), (3, RPAN, piece, PANEL),
        cross, cross, (4,) + cross, (4,) + cross, cross, cross, (4,) + cross, (4,) + cross,
        (RPAN, piece, width), small, small, small, small, small[1:], small[1:], small, small,
    ]
    upper, lower, pivot_rows, cross = pl.pallas_call(
        gather_kernel,
        out_shape=[jax.ShapeDtypeStruct(s, jnp.float32) for s in (full, full, band, band)],
        in_specs=[pl.BlockSpec(memory_space=pltpu.SMEM)] + [pl.BlockSpec(memory_space=pl.ANY)] * 2,
        out_specs=[pl.BlockSpec(memory_space=pl.ANY)] * 4,
        scratch_shapes=[
            *[pltpu.VMEM(s, jnp.float32) for s in buffers],
            pltpu.SemaphoreType.DMA((15, 8)),
            pltpu.SemaphoreType.DMA((15, 8)),
            pltpu.SemaphoreType.DMA((15,)),
        ],
        compiler_params=pltpu.CompilerParams(
            collective_id=collective_id, has_side_effects=True, vmem_limit_bytes=40 * 1024 * 1024
        ),
    )(table, cols.reshape(2, 4, count // 8, width), rows.reshape(band))
    halves = [a.reshape(count // 2, width) for a in (upper, lower)]
    return halves, pivot_rows.reshape(width, span), cross.reshape(width, width)


PARENT = {
    (3, 0): (0, 0), (3, 3): (3, 0), (3, 1): (3, 0), (2, 0): (3, 0), (2, 3): (2, 0),
    (3, 2): (3, 1), (0, 1): (3, 1), (0, 3): (3, 3), (2, 1): (3, 1), (1, 0): (2, 0),
    (2, 2): (3, 2), (1, 1): (2, 1), (0, 2): (3, 2), (1, 3): (2, 3), (1, 2): (2, 2),
}


def turned(place, quarter_turns):
    for _ in range(quarter_turns):
        place = (-place[1] % 4, place[0])
    return place


def tree_children(turn):
    children = [[] for _ in range(16)]
    for child, parent in PARENT.items():
        child, parent = turned(child, turn), turned(parent, turn)
        children[4 * parent[0] + parent[1]].append(4 * child[0] + child[1])
    return children


def tree_depth(turn):
    depth = [0] * 16
    for place in PARENT:
        node, hops = place, 0
        while node != (0, 0):
            node, hops = PARENT[node], hops + 1
        place = turned(place, turn)
        depth[4 * place[0] + place[1]] = hops
    return depth


def lookup(values, index):
    result = jnp.int32(values[0])
    for k in range(1, len(values)):
        result = jnp.where(index == k, jnp.int32(values[k]), result)
    return result


CHUNK = 32
CHUNKS = 2048 // (4 * CHUNK)
CROSS = CPAN * PANEL // (4 * CHUNK)
U_PARTS = 4
DEPTH = 5
SLACK = 2
U_TURN = 8


def spread_kernel(front, cols, rows, cross, recv, send, cross_recv, cross_send, rows_recv,
                  rows_send, own_sem, stage):
    y, core = lax.axis_index("y"), lax.axis_index("core")
    x, z = lax.axis_index("x"), lax.axis_index("z")
    place, within = 4 * x + z, lax.rem(y, 2) * 2 + core
    is_root = place == 0
    tables = [tree_children(turn) for turn in range(4)]
    target = [
        [lookup([(t[k] + [-1, -1, -1])[s] for k in range(16)], place) for s in range(3)]
        for t in tables
    ]
    depth = [lookup(tree_depth(turn), place) for turn in range(4)]
    sibling = {"core": 1 - core}
    above = {"y": y // 2 * 2 + 1 - lax.rem(y, 2)}

    barrier = pltpu.get_barrier_semaphore()
    for ident in (
        {"x": lax.rem(x + 1, 4)}, {"x": lax.rem(x + 3, 4)},
        {"z": lax.rem(z + 1, 4)}, {"z": lax.rem(z + 3, 4)}, sibling, above,
    ):
        pl.semaphore_signal(barrier, inc=1, device_id=ident, device_id_type=MESH)

    part = CPAN * PANEL // U_PARTS
    whole_band = pl.ds(0, CPAN * PANEL)
    load_own = pltpu.make_async_copy(front, stage, own_sem.at[0])
    own_cols = pltpu.make_async_copy(stage, cols, own_sem.at[0])
    own_rows = pltpu.make_async_copy(stage.at[whole_band], rows, own_sem.at[1])
    load_own.start()
    load_cross = pltpu.make_async_copy(
        cols.at[whole_band], stage.at[whole_band], own_sem.at[2]
    )
    store_cross = pltpu.make_async_copy(stage.at[whole_band], cross, own_sem.at[2])
    pl.semaphore_wait(barrier, 6)

    def rows_copy(src, k, way, ident):
        span = pl.ds(k * part, part)
        return pltpu.make_async_remote_copy(
            src_ref=src.at[span], dst_ref=rows.at[span], send_sem=rows_send.at[way, k],
            recv_sem=rows_recv.at[k], device_id=ident, device_id_type=MESH,
        )

    def band(c, q):
        return pl.ds(pl.multiple_of((c * 4 + q) * CHUNK, CHUNK), CHUNK)

    def cols_copy(src, c, q, s):
        span = band(c, q)
        there = jnp.maximum(target[q][s], 0)
        return pltpu.make_async_remote_copy(
            src_ref=src.at[span], dst_ref=cols.at[span], send_sem=send.at[q, s, c],
            recv_sem=recv.at[q, c], device_id={"x": there // 4, "z": lax.rem(there, 4)},
            device_id_type=MESH,
        )

    def cross_copy(src, c, q, way, ident):
        span = band(c, q)
        return pltpu.make_async_remote_copy(
            src_ref=src.at[span], dst_ref=cross.at[span], send_sem=cross_send.at[way, q, c],
            recv_sem=cross_recv.at[q, c], device_id=ident, device_id_type=MESH,
        )

    @pl.when(within == 0)
    def _():
        for k in range(U_PARTS):
            rows_copy(front, k, 0, above).start()
            rows_copy(front, k, 1, sibling).start()

    load_own.wait()

    @pl.when(is_root)
    def _():
        own_cols.start()

    @pl.when(within == 0)
    def _():
        own_rows.start()
        own_rows.wait()

    @pl.when(is_root)
    def _():
        own_cols.wait()

    def both(first, second):
        return jnp.logical_and(first, second)

    def pass_cols(c, q):
        @pl.when(is_root)
        def _():
            cols_copy(front, c, q, 0).start()

            @pl.when(both(within == 0, c < CROSS))
            def _():
                cross_copy(front, c, q, 0, above).start()
                cross_copy(front, c, q, 1, sibling).start()

        @pl.when(jnp.logical_not(is_root))
        def _():
            cols_copy(cols, c, q, 0).wait_recv()
            for s in range(3):

                @pl.when(target[q][s] >= 0)
                def _():
                    cols_copy(cols, c, q, s).start()

            @pl.when(both(within == 0, c < CROSS))
            def _():
                cross_copy(cols, c, q, 0, above).start()
                cross_copy(cols, c, q, 1, sibling).start()

    def loop(lo, hi, body):
        lax.fori_loop(lo, hi, lambda c, _: (body(c), 0)[1], 0)

    def step(turn):
        for q in range(4):
            c = turn - SLACK * depth[q]

            @pl.when(both(c >= 0, c < CHUNKS))
            def _():
                pass_cols(c, q)

        for q in range(4):
            late = turn - SLACK * (depth[q] + 1)

            @pl.when(both(within == 2, both(late >= 0, late < CROSS)))
            def _():
                cross_copy(cross, late, q, 0, above).wait_recv()
                cross_copy(cross, late, q, 1, sibling).start()

        for k in range(U_PARTS):

            @pl.when(both(within == 2, turn == U_TURN + k))
            def _():
                rows_copy(rows, k, 0, above).wait_recv()
                rows_copy(rows, k, 1, sibling).start()

        @pl.when(both(within == 0, turn == CROSS + SLACK * DEPTH))
        def _():
            load_cross.start()

        @pl.when(both(within == 0, turn == CROSS + SLACK * DEPTH + 3))
        def _():
            load_cross.wait()
            store_cross.start()

    loop(0, CHUNKS + SLACK * DEPTH, step)

    @pl.when(within == 0)
    def _():
        for k in range(U_PARTS):
            rows_copy(front, k, 0, above).wait_send()
            rows_copy(front, k, 1, sibling).wait_send()

        def send_done(c):
            for q in range(4):
                cross_copy(front, c, q, 0, above).wait_send()
                cross_copy(front, c, q, 1, sibling).wait_send()

        loop(0, CROSS, send_done)

    @pl.when(within == 2)
    def _():
        for k in range(U_PARTS):
            rows_copy(rows, k, 1, sibling).wait_send()

        def send_done(c):
            for q in range(4):
                cross_copy(cross, c, q, 1, sibling).wait_send()

        loop(0, CROSS, send_done)

    @pl.when(lax.rem(within, 2) == 1)
    def _():
        for k in range(U_PARTS):
            rows_copy(rows, k, 0, sibling).wait_recv()

        def arrived(c):
            for q in range(4):
                cross_copy(cross, c, q, 0, sibling).wait_recv()

        loop(0, CROSS, arrived)

    def cols_done(c):
        for q in range(4):
            for s in range(3):

                @pl.when(target[q][s] >= 0)
                def _():
                    cols_copy(front, c, q, s).wait_send()

    loop(0, CHUNKS, cols_done)

    @pl.when(within == 0)
    def _():
        store_cross.wait()


def spread(front, collective_id):
    rows, cols = front.shape
    width = CPAN * PANEL
    shapes = [(rows, width), (width, cols), (width, width)]
    dma = pltpu.SemaphoreType.DMA
    return pl.pallas_call(
        spread_kernel,
        out_shape=[jax.ShapeDtypeStruct(s, jnp.float32) for s in shapes],
        in_specs=[pl.BlockSpec(memory_space=pl.ANY)],
        out_specs=[pl.BlockSpec(memory_space=pl.ANY)] * 3,
        scratch_shapes=[
            dma((4, CHUNKS)), dma((4, 3, CHUNKS)), dma((4, CROSS)), dma((2, 4, CROSS)),
            dma((U_PARTS,)), dma((2, U_PARTS)), dma((3,)), pltpu.VMEM(front.shape, jnp.float32),
        ],
        compiler_params=pltpu.CompilerParams(
            collective_id=collective_id, has_side_effects=True, vmem_limit_bytes=32 * 1024 * 1024
        ),
    )(front)


def dot(a, b, precision=HIGH):
    return jnp.dot(a, b, precision=precision, preferred_element_type=jnp.float32)


def newton(block):
    shape = (PANEL, PANEL)
    eye = lax.broadcasted_iota(jnp.int32, shape, 0) == lax.broadcasted_iota(jnp.int32, shape, 1)
    kept = jnp.where(eye, block, 0.0)
    by_col = 1.0 / jnp.sum(kept, axis=0, keepdims=True)
    by_row = 1.0 / jnp.sum(kept, axis=1, keepdims=True)
    identity = jnp.where(eye, 1.0, 0.0)
    error = identity - block * by_col
    product = identity + error
    for _ in range(3):
        error = dot(error, error, HIGHEST)
        product = product + dot(product, error, HIGHEST)
    return product * by_row


def panel(k):
    return slice(k * PANEL, (k + 1) * PANEL)


def finish_kernel(n, row_panels, col_panels, precision, bands, tail, tab, front, *refs):
    cols, rows, cross, outs = refs[:bands], refs[bands:tail], refs[tail], refs[tail + 1 : -3]
    work, inverse, pivots = refs[-3:]
    g = pl.program_id(0)

    @pl.when(g == 0)
    def _():
        work[...] = cross[...]
        for i, part in enumerate(rows):
            span = part.shape[1]
            pivots[:, i * span : (i + 1) * span] = part[...]
        for k in range(n):
            inverse[k] = newton(work[panel(k), panel(k)])
            for p in range(k + 1, n):
                factor = dot(work[panel(p), panel(k)], inverse[k], HIGHEST)
                for q in range(k + 1, n):
                    work[panel(p), panel(q)] -= dot(factor, work[panel(k), panel(q)], HIGHEST)
                pivots[panel(p), :] -= dot(factor, pivots[panel(k), :], HIGHEST)
        for j in range(col_panels):
            for k in range(n):
                pivots[panel(k), panel(j)] = jnp.where(
                    tab[row_panels + j] > k, pivots[panel(k), panel(j)], 0.0
                )

    mine = cols[0][...]
    if bands == 2:
        mine = jnp.where(g < row_panels // 2, mine, cols[1][...])
    band = [mine[:, panel(k)] for k in range(n)]
    for k in range(n):
        band[k] = dot(band[k], inverse[k], HIGHEST)
        for q in range(k + 1, n):
            band[q] = band[q] - dot(band[k], work[panel(k), panel(q)], HIGHEST)
    band = [jnp.where(tab[g] > k, band[k], 0.0) for k in range(n)]
    factors = jnp.concatenate(band, axis=1)
    for j in range(col_panels):
        new = front[:, panel(j)] - dot(factors, pivots[:, panel(j)], precision)
        for k in range(n):
            here = jnp.logical_and(tab[row_panels + j] == k, tab[g] > k)
            new = jnp.where(here, band[k], new)
        outs[0][:, panel(j)] = new
        if len(outs) == 2:
            outs[1][2 * j] = new[:, :BLK]
            outs[1][2 * j + 1] = new[:, BLK:]


def finish(front, bands, pivot_rows, cross, row_step, col_step, precision, blocked=False):
    rows, cols = front.shape
    width = cross.shape[0]
    n, row_panels, col_panels = width // PANEL, rows // PANEL, cols // PANEL
    half = row_panels // 2
    keep = lambda shape: pl.BlockSpec(shape, lambda g, tab: (0, 0))
    if len(bands) == 1:
        band_specs = [pl.BlockSpec((PANEL, width), lambda g, tab: (g, 0))]
    else:
        band_specs = [
            pl.BlockSpec((PANEL, width), lambda g, tab: (jnp.minimum(g, half - 1), 0)),
            pl.BlockSpec((PANEL, width), lambda g, tab: (jnp.maximum(g - half, 0), 0)),
        ]
    return local_call(
        functools.partial(finish_kernel, n, row_panels, col_panels, precision, len(bands), len(bands) + len(pivot_rows)),
        row_panels,
        jnp.concatenate([row_step, col_step]).astype(jnp.int32),
        (front, *bands, *pivot_rows, cross),
        [
            pl.BlockSpec((PANEL, cols), lambda g, tab: (g, 0)),
            *band_specs,
            *[keep(p.shape) for p in pivot_rows],
            keep(cross.shape),
        ],
        [front.shape] + [(cols // BLK, rows, BLK)] * blocked,
        [pl.BlockSpec((PANEL, cols), lambda g, tab: (g, 0))]
        + [pl.BlockSpec((cols // BLK, PANEL, BLK), lambda g, tab: (0, g, 0))] * blocked,
        scratch=[
            pltpu.VMEM((width, width), jnp.float32),
            pltpu.VMEM((n, PANEL, PANEL), jnp.float32),
            pltpu.VMEM((width, cols), jnp.float32),
        ],
    )


def body(child_fronts, root_front, child_map, panel_order):
    y, core = lax.axis_index("y"), lax.axis_index("core")
    r, o = 2 * y + core, 4 * lax.axis_index("x") + lax.axis_index("z")
    within = lax.rem(y, 2) * 2 + core

    pivot_cols, pivot_rows, cross = spread(child_fronts, 10)
    row_panel, col_panel = within * 8 + jnp.arange(8), o * 2 + jnp.arange(2)
    row_step = jnp.where(row_panel < CPAN, row_panel, NEVER)
    col_step = jnp.where(col_panel < CPAN, col_panel, NEVER)
    factored, blocks = finish(
        child_fronts, [pivot_cols], [pivot_rows], cross, row_step, col_step, HIGHEST, True
    )

    assembled = extend_add(blocks, root_front, child_map)

    row_panels, col_panels = 6, 3
    order = panel_order.astype(jnp.uint32)
    each = lambda a: [a[k] for k in range(RPAN)]
    col_off = each(order % col_panels * PANEL)
    row_off = each(order % row_panels * PANEL)
    table = jnp.concatenate(
        [
            order // (4 * col_panels), order // col_panels % 4, order // row_panels,
            order % col_panels,
        ]
    ).astype(jnp.int32)
    cols = jnp.concatenate([lax.dynamic_slice_in_dim(assembled, off, PANEL, 1) for off in col_off], 1)
    rows = jnp.stack([lax.dynamic_slice_in_dim(assembled, off, PANEL, 0) for off in row_off])
    halves, pivot_rows, cross = gather_bands(cols, rows, table, 20)

    def steps(places):
        match = places[:, None] == panel_order[None, :]
        return jnp.min(jnp.where(match, jnp.arange(RPAN)[None, :], NEVER), axis=1)

    row_step = steps(r * row_panels + jnp.arange(row_panels))
    col_step = steps(o * col_panels + jnp.arange(col_panels))
    return factored, finish(assembled, halves, [pivot_rows], cross, row_step, col_step, HIGH)[0]


def solution(mesh):
    grid = Mesh(mesh.devices.reshape(4, 2, 4, 4), ("y", "core", "x", "z"))
    return jax.shard_map(
        body,
        mesh=grid,
        in_specs=(P(ROW, COL), P(ROW, COL), P(), P()),
        out_specs=(P(ROW, COL), P(ROW, COL)),
        check_vma=False,
    )
```

```python
import functools

import jax
import jax.numpy as jnp
from jax import lax
from jax.experimental import pallas as pl
from jax.experimental.pallas import tpu as pltpu
from jax.sharding import Mesh
from jax.sharding import PartitionSpec as P

PANEL = 256
BLK = 128
CPAN = 2
RPAN = 3

ROW = ("y", "core")
COL = ("x", "z")
MESH = pl.DeviceIdType.MESH
NEVER = 99

HIGH = lax.Precision.HIGH
HIGHEST = lax.Precision.HIGHEST


def peers_of(axes):
    y, core = lax.axis_index("y"), lax.axis_index("core")
    if axes == ROW:
        return 2 * y + core, 8, lambda p: {"y": p // 2, "core": lax.rem(p, 2)}
    if axes == "child":
        pair = y // 2 * 2
        me = lax.rem(y, 2) * 2 + core
        return me, 4, lambda p: {"y": pair + p // 2, "core": lax.rem(p, 2)}
    return lax.axis_index(axes), 4, lambda p: {axes: p}


def rank_in(key, group, valid):
    n = key.shape[1]
    earlier = jnp.arange(n)[None, :] < jnp.arange(n)[:, None]
    same = (key[:, :, None] == key[:, None, :]) & (group[:, None] == group[None, :])[None]
    return jnp.sum((same & valid[:, None, :] & earlier[None]).astype(jnp.int32), axis=2)


def routes(child_map):
    y, core = lax.axis_index("y"), lax.axis_index("core")
    x, z = lax.axis_index("x"), lax.axis_index("z")
    within, r, o = lax.rem(y, 2) * 2 + core, 2 * y + core, 4 * x + z
    blocks = jnp.arange(64)
    skip = CPAN * PANEL // BLK
    cyclic = (child_map % 6) * 16 + child_map // 6
    t = jnp.concatenate([jnp.zeros((2, skip), jnp.int32), cyclic], axis=1)
    valid = jnp.broadcast_to(blocks >= skip, (2, 64))
    kz = rank_in(t % 4, blocks // 4, valid)
    kx = rank_in(t % 16, blocks // 16, valid)
    kr = rank_in(t % 16 // 2, blocks // 16, valid)
    child = jnp.arange(2)[:, None]
    device, group = (blocks // 4)[None], (blocks // 16)[None]
    kinds = [
        (device == o, t % 4 * 2 + kz, blocks[None] % 4),
        ((group == x) & (t % 4 == z), t % 16 // 4 * 2 + kx, device % 4 * 2 + kz),
        (t % 16 == o, t // 16, group * 2 + kx),
        (group == within, t % 16 // 2 * 4 + kr, blocks[None] % 16),
        (t % 16 // 2 == r, t % 2 * 6 + t // 16, (child * 4 + group) * 4 + kr),
    ]
    lists = lambda k: jnp.stack([jnp.broadcast_to(a, (2, 64)) for a in k])
    place = jnp.where(lists([valid & k[0] for k in kinds]), lists([k[1] for k in kinds]), -1)
    says = lists([k[2] for k in kinds]) + 1
    match = place[:, :, None, :] == jnp.arange(32)[None, None, :, None]
    return (jnp.sum(jnp.where(match, says[:, :, None, :], 0), axis=3) - 1).reshape(-1)


Z_PICK, X_PICK, COL_FROM, R_PICK, ROW_FROM = (64 * k for k in range(5))


def whole(shape):
    return pl.BlockSpec(shape, lambda g, tab: (0,) * len(shape))


def part(shape):
    return pl.BlockSpec((1,) + shape, lambda g, tab: (g,) + (0,) * len(shape))


def local_call(kernel, grid, table, operands, in_specs, out_shapes, out_specs, scratch=()):
    return pl.pallas_call(
        kernel,
        grid_spec=pltpu.PrefetchScalarGridSpec(
            num_scalar_prefetch=1, grid=(grid,), in_specs=in_specs, out_specs=out_specs,
            scratch_shapes=list(scratch),
        ),
        out_shape=[jax.ShapeDtypeStruct(s, jnp.float32) for s in out_shapes],
        compiler_params=pltpu.CompilerParams(vmem_limit_bytes=62 * 1024 * 1024),
    )(table, *operands)


def at_least_zero(v):
    return jnp.maximum(v, 0)


def lanes(block):
    return pl.ds(pl.multiple_of(block * BLK, BLK), BLK)


PARTS = 4
SLICE = BLK // (2 * PARTS)


def extend_kernel(tab, front, *refs):
    ya_in, xb_in = refs[:PARTS], refs[PARTS : 2 * PARTS]
    send_sem, recv_sem, own_sem = refs[-3:]
    za_out, za_in, xa_out, xa_in, ya_out, yb_out, yb_in, zb_out, zb_in, xb_out = (
        refs[(2 + i) * PARTS : (3 + i) * PARTS] for i in range(10)
    )
    barrier = pltpu.get_barrier_semaphore()
    total = 0
    for ax in ("z", "x", ROW):
        me, size, ident = peers_of(ax)
        for d in range(1, size):
            pl.semaphore_signal(
                barrier, inc=1, device_id=ident(lax.rem(me + d, size)), device_id_type=MESH
            )
        total += size - 1

    started = []

    def send(number, src, dst, axes, count):
        me, size, ident = peers_of(axes)
        slot = lambda p: pl.ds(p * count, count)
        own = pltpu.make_async_copy(src.at[slot(me)], dst.at[slot(me)], own_sem.at[number])
        own.start()
        copies = []
        for d in sorted(range(1, size), key=lambda d: -min(d, size - d)):
            p = lax.rem(me + d, size)
            copy = pltpu.make_async_remote_copy(
                src_ref=src.at[slot(p)],
                dst_ref=dst.at[slot(me)],
                send_sem=send_sem.at[number, d],
                recv_sem=recv_sem.at[number, d],
                device_id=ident(p),
                device_id_type=MESH,
            )
            copy.start()
            copies.append(copy)
        started.extend(copies)
        return own, copies

    def arrive(transfer):
        own, copies = transfer
        own.wait()
        for copy in copies:
            copy.wait_recv()

    def each(count, body):
        lax.fori_loop(0, count, lambda g, _: (body(g), 0)[1], 0)

    own = 32 * (lax.axis_index("y") // 2)

    def entry(at):
        return tab[at]

    def pack_za(ch):
        rows = slice(ch * SLICE, (ch + 1) * SLICE)

        def body(g):
            za_out[ch][g] = front[entry(Z_PICK + own + g), :, rows, :]

        each(8, body)

    def pack_yb(ch):
        rows = slice((PARTS + ch) * SLICE, (PARTS + ch + 1) * SLICE)

        def body(g):
            yb_out[ch][g] = front[:, entry(R_PICK + own + g), rows, :]

        each(32, body)

    def pack_xa(ch):
        def body(g):
            xa_out[ch][g] = za_in[ch][entry(X_PICK + own + g)]

        each(8, body)

    def pack_zb(ch):
        def body(g):
            for c in range(2):
                column = entry(Z_PICK + c * 32 + g)
                for i in range(12):
                    source = entry(ROW_FROM + c * 32 + i)
                    zb_out[ch][g, c * 12 + i] = yb_in[ch][source, column]

        each(8, body)

    def pack_ya(ch):
        def body(g):
            i = entry(R_PICK + own + g)
            for slot in range(6):
                columns = slice(slot * BLK, slot * BLK + BLK)
                ya_out[ch][g, :, columns] = xa_in[ch][entry(COL_FROM + own + slot), i]

        each(32, body)

    def pack_xb(ch):
        def body(g):
            for c in range(2):
                rows = slice(c * 12, c * 12 + 12)
                xb_out[ch][g, rows] = zb_in[ch][entry(X_PICK + c * 32 + g), rows]

        each(8, body)

    stages = {
        "A": [
            (pack_za, "z", za_out, za_in, 2, 2), (pack_xa, "x", xa_out, xa_in, 2, 2),
            (pack_ya, ROW, ya_out, ya_in, 4, 3),
        ],
        "B": [
            (pack_yb, ROW, yb_out, yb_in, 4, 2), (pack_zb, "z", zb_out, zb_in, 2, 3),
            (pack_xb, "x", xb_out, xb_in, 2, 3),
        ],
    }
    free, pending, number = {"z": 0, "x": 0, ROW: 0}, [], 0

    def begin(time, half, ch, stage, packed=False):
        nonlocal number
        pack, axes, out, arriving, count, cost = stages[half][stage]
        if not packed:
            pack(ch)
        free[axes] = max(time, free[axes]) + cost
        pending.append((free[axes], number, half, ch, stage, send(number, out[ch], arriving[ch], axes, count)))
        number += 1

    pack_za(0)
    pl.semaphore_wait(barrier, total)
    begin(0, "A", 0, 0, packed=True)
    begin(0, "B", 0, 0)
    for ch in range(1, PARTS):
        pack_za(ch)
        pack_yb(ch)
    while pending:
        pending.sort(key=lambda p: p[:2])
        time, _, half, ch, stage, transfer = pending.pop(0)
        arrive(transfer)
        if stage == 0 and ch + 1 < PARTS:
            begin(time, half, ch + 1, 0, packed=True)
        if stage < 2:
            begin(time, half, ch, stage + 1)
    for copy in started:
        copy.wait_send()


def add_all(tab, root, *refs):
    i = pl.program_id(0)
    out = refs[-1]
    for slot in range(6):
        columns = slice(slot * BLK, slot * BLK + BLK)
        sums = [root[0, q * SLICE : (q + 1) * SLICE, columns] for q in range(2 * PARTS)]
        for c in range(2):
            mine = refs[c * 2 * PARTS : (c + 1) * 2 * PARTS]
            row, col = tab[ROW_FROM + c * 32 + i], tab[COL_FROM + c * 32 + slot]
            there = jnp.logical_and(row >= 0, col >= 0)
            col = at_least_zero(col)
            arrived = [m[0, :, columns] for m in mine[:PARTS]] + [m[col, 0] for m in mine[PARTS:]]
            sums = [s + jnp.where(there, a, 0.0) for s, a in zip(sums, arrived)]
        for q in range(2 * PARTS):
            out[0, q * SLICE : (q + 1) * SLICE, columns] = sums[q]


def extend_add(front, root_front, child_map):
    table = routes(child_map)
    blocks, rows, wide = (8, 16, SLICE, BLK), (32, SLICE, 768), (8, 24, SLICE, BLK)
    band = (32, 4, SLICE, BLK)
    buffers = [blocks] * (4 * PARTS) + [rows] * PARTS + [band] * (2 * PARTS) + [wide] * (3 * PARTS)
    arrived = pl.pallas_call(
        extend_kernel,
        out_shape=[jax.ShapeDtypeStruct(s, jnp.float32) for s in [rows] * PARTS + [wide] * PARTS],
        in_specs=[
            pl.BlockSpec(memory_space=pltpu.SMEM), pl.BlockSpec(memory_space=pltpu.VMEM),
        ],
        out_specs=[pl.BlockSpec(memory_space=pl.ANY)] * (2 * PARTS),
        scratch_shapes=[
            *[pltpu.VMEM(s, jnp.float32) for s in buffers],
            pltpu.SemaphoreType.DMA((6 * PARTS, 8)),
            pltpu.SemaphoreType.DMA((6 * PARTS, 8)),
            pltpu.SemaphoreType.DMA((6 * PARTS,)),
        ],
        compiler_params=pltpu.CompilerParams(
            collective_id=1, has_side_effects=True, vmem_limit_bytes=62 * 1024 * 1024
        ),
    )(jnp.maximum(table, 0), front.reshape(4, 16, BLK, BLK))
    operands, specs = [], []
    for c in range(2):
        from_rows = lambda g, tab, c=c: (at_least_zero(tab[ROW_FROM + c * 32 + g]), 0, 0)
        from_wide = lambda g, tab, c=c: (0, c * 12 + g, 0, 0)
        operands += arrived
        specs += [pl.BlockSpec((1,) + rows[1:], from_rows)] * PARTS
        specs += [pl.BlockSpec((8, 1, SLICE, BLK), from_wide)] * PARTS
    (assembled,) = local_call(
        add_all, 12, table, (root_front.reshape(12, BLK, 768), *operands),
        [part((BLK, 768)), *specs], [(12, BLK, 768)], [part((BLK, 768))],
    )
    return assembled.reshape(root_front.shape)


def gather_kernel(tab, cols, rows, upper, lower, rows_out, cross_out, *refs):
    (arrived_a, arrived_b, arrived_rows, mine, mine_blocks, cross_a, cross_b, cross_a1, cross_b1,
     cross_a2, cross_b2, cross_a3, cross_b3, cross_all, a1, b1, a2, b2, a3, b3, a4, b4) = refs[:-3]
    send_sem, recv_sem, own_sem = refs[-3:]
    barrier = pltpu.get_barrier_semaphore()
    total = 0
    for ax in ("z", "x", ROW):
        me, size, ident = peers_of(ax)
        for d in range(1, size):
            pl.semaphore_signal(
                barrier, inc=1, device_id=ident(lax.rem(me + d, size)), device_id_type=MESH
            )
        total += size - 1
    started = []

    def send(number, src, dst, axes):
        me, size, ident = peers_of(axes)
        own = pltpu.make_async_copy(src(me), dst(me), own_sem.at[number])
        own.start()
        copies = []
        for d in sorted(range(1, size), key=lambda d: -min(d, size - d)):
            p = lax.rem(me + d, size)
            copy = pltpu.make_async_remote_copy(
                src_ref=src(p),
                dst_ref=dst(me),
                send_sem=send_sem.at[number, d],
                recv_sem=recv_sem.at[number, d],
                device_id=ident(p),
                device_id_type=MESH,
            )
            copy.start()
            copies.append(copy)
        started.extend(copies)
        return own, copies

    def arrive(*transfers):
        for own, copies in transfers:
            own.wait()
            for copy in copies:
                copy.wait_recv()

    def slot(ref):
        return lambda p: ref.at[p]

    def inner(ref):
        return lambda p: ref.at[:, p]

    def same(ref):
        return lambda p: ref

    owner_x = [tab[k] for k in range(RPAN)]
    owner_z = [tab[RPAN + k] for k in range(RPAN)]
    owner_row = [tab[2 * RPAN + k] for k in range(RPAN)]
    owned = [tab[3 * RPAN + k] for k in range(RPAN)]

    pl.semaphore_wait(barrier, total)
    t_rows = send(0, inner(rows), slot(arrived_rows), ROW)
    t_a = send(1, lambda p: cols.at[0, p], slot(arrived_a), "z")
    t_b = send(2, lambda p: cols.at[1, p], slot(arrived_b), "x")

    arrive(t_rows)
    for k in range(RPAN):
        mine[k] = arrived_rows[owner_row[k], k]
        for j in range(3):
            mine_blocks[j, k] = arrived_rows[owner_row[k], k, :, panel(j)]
    half = mine.shape[1] // 2
    for q in range(RPAN):
        block = mine_blocks[owned[q]]
        cross_a[:, :, panel(q)] = block[:, :half]
        cross_b[:, :, panel(q)] = block[:, half:]
    t_cross_a = send(3, same(cross_a), slot(cross_a1), "z")
    t_cross_b = send(4, same(cross_b), slot(cross_b1), "x")
    t_mine = send(5, same(mine), inner(rows_out), ROW)

    piece = a1.shape[1]

    def split(transfer, arrived, owners, out):
        arrive(transfer)
        for q in range(RPAN):
            for p in range(4):
                out[p, :, panel(q)] = arrived[owners[q], p * piece : (p + 1) * piece, panel(q)]

    def select(transfer, arrived, owners, out):
        arrive(transfer)
        for q in range(RPAN):
            out[..., panel(q)] = arrived[owners[q], ..., panel(q)]

    split(t_a, arrived_a, owner_z, a1)
    t_a = send(6, slot(a1), slot(a2), "x")
    split(t_b, arrived_b, owner_x, b1)
    t_b = send(7, slot(b1), slot(b2), "z")
    select(t_cross_a, cross_a1, owner_z, cross_a2)
    t_cross_a = send(8, same(cross_a2), slot(cross_a3), "x")
    select(t_cross_b, cross_b1, owner_x, cross_b2)
    t_cross_b = send(9, same(cross_b2), slot(cross_b3), "z")
    select(t_a, a2, owner_x, a3)
    t_a = send(10, same(a3), slot(a4), "x")
    select(t_b, b2, owner_z, b3)
    t_b = send(11, same(b3), slot(b4), "z")
    arrive(t_cross_a, t_cross_b)
    for q in range(RPAN):
        cross_all[:, :half, panel(q)] = cross_a3[owner_x[q], :, :, panel(q)]
        cross_all[:, half:, panel(q)] = cross_b3[owner_z[q], :, :, panel(q)]
    t_cross = send(12, same(cross_all), inner(cross_out), ROW)
    arrive(t_a)
    t_a = send(13, same(a4), slot(upper), "z")
    arrive(t_b)
    t_b = send(14, same(b4), slot(lower), "x")
    arrive(t_mine, t_cross, t_a, t_b)
    for copy in started:
        copy.wait_send()


def gather_bands(cols, rows, table, collective_id):
    count, width = cols.shape
    piece, span = PANEL // 8, rows.shape[2]
    band, ring = (RPAN, 8, piece, span), (4, count // 8, width)
    small, cross = (4, count // 32, width), (RPAN, piece // 2, width)
    full = (4,) + small
    buffers = [
        ring, ring, (8, RPAN, piece, span), (RPAN, piece, span), (3, RPAN, piece, PANEL),
        cross, cross, (4,) + cross, (4,) + cross, cross, cross, (4,) + cross, (4,) + cross,
        (RPAN, piece, width), small, small, small, small, small[1:], small[1:], small, small,
    ]
    upper, lower, pivot_rows, cross = pl.pallas_call(
        gather_kernel,
        out_shape=[jax.ShapeDtypeStruct(s, jnp.float32) for s in (full, full, band, band)],
        in_specs=[pl.BlockSpec(memory_space=pltpu.SMEM)] + [pl.BlockSpec(memory_space=pl.ANY)] * 2,
        out_specs=[pl.BlockSpec(memory_space=pl.ANY)] * 4,
        scratch_shapes=[
            *[pltpu.VMEM(s, jnp.float32) for s in buffers],
            pltpu.SemaphoreType.DMA((15, 8)),
            pltpu.SemaphoreType.DMA((15, 8)),
            pltpu.SemaphoreType.DMA((15,)),
        ],
        compiler_params=pltpu.CompilerParams(
            collective_id=collective_id, has_side_effects=True, vmem_limit_bytes=62 * 1024 * 1024
        ),
    )(table, cols.reshape(2, 4, count // 8, width), rows.reshape(band))
    halves = [a.reshape(count // 2, width) for a in (upper, lower)]
    return halves, pivot_rows.reshape(width, span), cross.reshape(width, width)


PARENT = {
    (3, 0): (0, 0), (3, 3): (3, 0), (3, 1): (3, 0), (2, 0): (3, 0), (2, 3): (2, 0),
    (3, 2): (3, 1), (0, 1): (3, 1), (0, 3): (3, 3), (2, 1): (3, 1), (1, 0): (2, 0),
    (2, 2): (3, 2), (1, 1): (2, 1), (0, 2): (3, 2), (1, 3): (2, 3), (1, 2): (2, 2),
}


def turned(place, quarter_turns):
    for _ in range(quarter_turns):
        place = (-place[1] % 4, place[0])
    return place


def tree_children(turn):
    children = [[] for _ in range(16)]
    for child, parent in PARENT.items():
        child, parent = turned(child, turn), turned(parent, turn)
        children[4 * parent[0] + parent[1]].append(4 * child[0] + child[1])
    return children


def tree_depth(turn):
    depth = [0] * 16
    for place in PARENT:
        node, hops = place, 0
        while node != (0, 0):
            node, hops = PARENT[node], hops + 1
        place = turned(place, turn)
        depth[4 * place[0] + place[1]] = hops
    return depth


def lookup(values, index):
    result = jnp.int32(values[0])
    for k in range(1, len(values)):
        result = jnp.where(index == k, jnp.int32(values[k]), result)
    return result


CHUNK = 32
CHUNKS = 2048 // (4 * CHUNK)
CROSS = CPAN * PANEL // (4 * CHUNK)
U_PARTS = 4
DEPTH = 5
SLACK = 2
U_TURN = 8


def spread_kernel(front, cols, rows, cross, recv, send, cross_recv, cross_send, rows_recv,
                  rows_send, own_sem, stage):
    y, core = lax.axis_index("y"), lax.axis_index("core")
    x, z = lax.axis_index("x"), lax.axis_index("z")
    place, within = 4 * x + z, lax.rem(y, 2) * 2 + core
    is_root = place == 0
    tables = [tree_children(turn) for turn in range(4)]
    target = [
        [lookup([(t[k] + [-1, -1, -1])[s] for k in range(16)], place) for s in range(3)]
        for t in tables
    ]
    depth = [lookup(tree_depth(turn), place) for turn in range(4)]
    sibling = {"core": 1 - core}
    above = {"y": y // 2 * 2 + 1 - lax.rem(y, 2)}

    barrier = pltpu.get_barrier_semaphore()
    for ident in (
        {"x": lax.rem(x + 1, 4)}, {"x": lax.rem(x + 3, 4)},
        {"z": lax.rem(z + 1, 4)}, {"z": lax.rem(z + 3, 4)}, sibling, above,
    ):
        pl.semaphore_signal(barrier, inc=1, device_id=ident, device_id_type=MESH)

    part = CPAN * PANEL // U_PARTS
    whole_band = pl.ds(0, CPAN * PANEL)
    load_own = pltpu.make_async_copy(front, stage, own_sem.at[0])
    own_cols = pltpu.make_async_copy(stage, cols, own_sem.at[0])
    own_rows = pltpu.make_async_copy(stage.at[whole_band], rows, own_sem.at[1])
    load_own.start()
    load_cross = pltpu.make_async_copy(
        cols.at[whole_band], stage.at[whole_band], own_sem.at[2]
    )
    store_cross = pltpu.make_async_copy(stage.at[whole_band], cross, own_sem.at[2])
    pl.semaphore_wait(barrier, 6)

    def rows_copy(src, k, way, ident):
        span = pl.ds(k * part, part)
        return pltpu.make_async_remote_copy(
            src_ref=src.at[span], dst_ref=rows.at[span], send_sem=rows_send.at[way, k],
            recv_sem=rows_recv.at[k], device_id=ident, device_id_type=MESH,
        )

    def band(c, q):
        return pl.ds(pl.multiple_of((c * 4 + q) * CHUNK, CHUNK), CHUNK)

    def cols_copy(src, c, q, s):
        span = band(c, q)
        there = jnp.maximum(target[q][s], 0)
        return pltpu.make_async_remote_copy(
            src_ref=src.at[span], dst_ref=cols.at[span], send_sem=send.at[q, s, c],
            recv_sem=recv.at[q, c], device_id={"x": there // 4, "z": lax.rem(there, 4)},
            device_id_type=MESH,
        )

    def cross_copy(src, c, q, way, ident):
        span = band(c, q)
        return pltpu.make_async_remote_copy(
            src_ref=src.at[span], dst_ref=cross.at[span], send_sem=cross_send.at[way, q, c],
            recv_sem=cross_recv.at[q, c], device_id=ident, device_id_type=MESH,
        )

    @pl.when(within == 0)
    def _():
        for k in range(U_PARTS):
            rows_copy(front, k, 0, above).start()
            rows_copy(front, k, 1, sibling).start()

    load_own.wait()

    @pl.when(is_root)
    def _():
        own_cols.start()

    @pl.when(within == 0)
    def _():
        own_rows.start()
        own_rows.wait()

    @pl.when(is_root)
    def _():
        own_cols.wait()

    def both(first, second):
        return jnp.logical_and(first, second)

    def pass_cols(c, q):
        @pl.when(is_root)
        def _():
            cols_copy(front, c, q, 0).start()

            @pl.when(both(within == 0, c < CROSS))
            def _():
                cross_copy(front, c, q, 0, above).start()
                cross_copy(front, c, q, 1, sibling).start()

        @pl.when(jnp.logical_not(is_root))
        def _():
            cols_copy(cols, c, q, 0).wait_recv()
            for s in range(3):

                @pl.when(target[q][s] >= 0)
                def _():
                    cols_copy(cols, c, q, s).start()

            @pl.when(both(within == 0, c < CROSS))
            def _():
                cross_copy(cols, c, q, 0, above).start()
                cross_copy(cols, c, q, 1, sibling).start()

    def loop(lo, hi, body):
        lax.fori_loop(lo, hi, lambda c, _: (body(c), 0)[1], 0)

    def step(turn):
        for q in range(4):
            c = turn - SLACK * depth[q]

            @pl.when(both(c >= 0, c < CHUNKS))
            def _():
                pass_cols(c, q)

        for q in range(4):
            late = turn - SLACK * (depth[q] + 1)

            @pl.when(both(within == 2, both(late >= 0, late < CROSS)))
            def _():
                cross_copy(cross, late, q, 0, above).wait_recv()
                cross_copy(cross, late, q, 1, sibling).start()

        for k in range(U_PARTS):

            @pl.when(both(within == 2, turn == U_TURN + k))
            def _():
                rows_copy(rows, k, 0, above).wait_recv()
                rows_copy(rows, k, 1, sibling).start()

        @pl.when(both(within == 0, turn == CROSS + SLACK * DEPTH))
        def _():
            load_cross.start()

        @pl.when(both(within == 0, turn == CROSS + SLACK * DEPTH + 3))
        def _():
            load_cross.wait()
            store_cross.start()

    loop(0, CHUNKS + SLACK * DEPTH, step)

    @pl.when(within == 0)
    def _():
        for k in range(U_PARTS):
            rows_copy(front, k, 0, above).wait_send()
            rows_copy(front, k, 1, sibling).wait_send()

        def send_done(c):
            for q in range(4):
                cross_copy(front, c, q, 0, above).wait_send()
                cross_copy(front, c, q, 1, sibling).wait_send()

        loop(0, CROSS, send_done)

    @pl.when(within == 2)
    def _():
        for k in range(U_PARTS):
            rows_copy(rows, k, 1, sibling).wait_send()

        def send_done(c):
            for q in range(4):
                cross_copy(cross, c, q, 1, sibling).wait_send()

        loop(0, CROSS, send_done)

    @pl.when(lax.rem(within, 2) == 1)
    def _():
        for k in range(U_PARTS):
            rows_copy(rows, k, 0, sibling).wait_recv()

        def arrived(c):
            for q in range(4):
                cross_copy(cross, c, q, 0, sibling).wait_recv()

        loop(0, CROSS, arrived)

    def cols_done(c):
        for q in range(4):
            for s in range(3):

                @pl.when(target[q][s] >= 0)
                def _():
                    cols_copy(front, c, q, s).wait_send()

    loop(0, CHUNKS, cols_done)

    @pl.when(within == 0)
    def _():
        store_cross.wait()


def spread(front, collective_id):
    rows, cols = front.shape
    width = CPAN * PANEL
    shapes = [(rows, width), (width, cols), (width, width)]
    dma = pltpu.SemaphoreType.DMA
    return pl.pallas_call(
        spread_kernel,
        out_shape=[jax.ShapeDtypeStruct(s, jnp.float32) for s in shapes],
        in_specs=[pl.BlockSpec(memory_space=pl.ANY)],
        out_specs=[pl.BlockSpec(memory_space=pl.ANY)] * 3,
        scratch_shapes=[
            dma((4, CHUNKS)), dma((4, 3, CHUNKS)), dma((4, CROSS)), dma((2, 4, CROSS)),
            dma((U_PARTS,)), dma((2, U_PARTS)), dma((3,)), pltpu.VMEM(front.shape, jnp.float32),
        ],
        compiler_params=pltpu.CompilerParams(
            collective_id=collective_id, has_side_effects=True, vmem_limit_bytes=62 * 1024 * 1024
        ),
    )(front)


def dot(a, b, precision=HIGH):
    return jnp.dot(a, b, precision=precision, preferred_element_type=jnp.float32)


def newton(block):
    shape = (PANEL, PANEL)
    eye = lax.broadcasted_iota(jnp.int32, shape, 0) == lax.broadcasted_iota(jnp.int32, shape, 1)
    kept = jnp.where(eye, block, 0.0)
    by_col = 1.0 / jnp.sum(kept, axis=0, keepdims=True)
    by_row = 1.0 / jnp.sum(kept, axis=1, keepdims=True)
    identity = jnp.where(eye, 1.0, 0.0)
    error = identity - block * by_col
    product = identity + error
    for _ in range(3):
        error = dot(error, error, HIGHEST)
        product = product + dot(product, error, HIGHEST)
    return product * by_row


def panel(k):
    return slice(k * PANEL, (k + 1) * PANEL)


def finish_kernel(n, row_panels, col_panels, precision, bands, tail, tab, front, *refs):
    cols, rows, cross, outs = refs[:bands], refs[bands:tail], refs[tail], refs[tail + 1 : -3]
    work, inverse, pivots = refs[-3:]
    g = pl.program_id(0)

    @pl.when(g == 0)
    def _():
        work[...] = cross[...]
        for i, part in enumerate(rows):
            span = part.shape[1]
            pivots[:, i * span : (i + 1) * span] = part[...]
        for k in range(n):
            inverse[k] = newton(work[panel(k), panel(k)])
            for p in range(k + 1, n):
                factor = dot(work[panel(p), panel(k)], inverse[k], HIGHEST)
                for q in range(k + 1, n):
                    work[panel(p), panel(q)] -= dot(factor, work[panel(k), panel(q)], HIGHEST)
                pivots[panel(p), :] -= dot(factor, pivots[panel(k), :], HIGHEST)
        for j in range(col_panels):
            for k in range(n):
                pivots[panel(k), panel(j)] = jnp.where(
                    tab[row_panels + j] > k, pivots[panel(k), panel(j)], 0.0
                )

    mine = cols[0][...]
    if bands == 2:
        mine = jnp.where(g < row_panels // 2, mine, cols[1][...])
    band = [mine[:, panel(k)] for k in range(n)]
    for k in range(n):
        band[k] = dot(band[k], inverse[k], HIGHEST)
        for q in range(k + 1, n):
            band[q] = band[q] - dot(band[k], work[panel(k), panel(q)], HIGHEST)
    band = [jnp.where(tab[g] > k, band[k], 0.0) for k in range(n)]
    factors = jnp.concatenate(band, axis=1)
    for j in range(col_panels):
        new = front[:, panel(j)] - dot(factors, pivots[:, panel(j)], precision)
        for k in range(n):
            here = jnp.logical_and(tab[row_panels + j] == k, tab[g] > k)
            new = jnp.where(here, band[k], new)
        outs[0][:, panel(j)] = new
        if len(outs) == 2:
            outs[1][2 * j] = new[:, :BLK]
            outs[1][2 * j + 1] = new[:, BLK:]


def finish(front, bands, pivot_rows, cross, row_step, col_step, precision, blocked=False):
    rows, cols = front.shape
    width = cross.shape[0]
    n, row_panels, col_panels = width // PANEL, rows // PANEL, cols // PANEL
    half = row_panels // 2
    keep = lambda shape: pl.BlockSpec(shape, lambda g, tab: (0, 0))
    if len(bands) == 1:
        band_specs = [pl.BlockSpec((PANEL, width), lambda g, tab: (g, 0))]
    else:
        band_specs = [
            pl.BlockSpec((PANEL, width), lambda g, tab: (jnp.minimum(g, half - 1), 0)),
            pl.BlockSpec((PANEL, width), lambda g, tab: (jnp.maximum(g - half, 0), 0)),
        ]
    return local_call(
        functools.partial(finish_kernel, n, row_panels, col_panels, precision, len(bands), len(bands) + len(pivot_rows)),
        row_panels,
        jnp.concatenate([row_step, col_step]).astype(jnp.int32),
        (front, *bands, *pivot_rows, cross),
        [
            pl.BlockSpec((PANEL, cols), lambda g, tab: (g, 0)),
            *band_specs,
            *[keep(p.shape) for p in pivot_rows],
            keep(cross.shape),
        ],
        [front.shape] + [(cols // BLK, rows, BLK)] * blocked,
        [pl.BlockSpec((PANEL, cols), lambda g, tab: (g, 0))]
        + [pl.BlockSpec((cols // BLK, PANEL, BLK), lambda g, tab: (0, g, 0))] * blocked,
        scratch=[
            pltpu.VMEM((width, width), jnp.float32),
            pltpu.VMEM((n, PANEL, PANEL), jnp.float32),
            pltpu.VMEM((width, cols), jnp.float32),
        ],
    )


def body(child_fronts, root_front, child_map, panel_order):
    y, core = lax.axis_index("y"), lax.axis_index("core")
    r, o = 2 * y + core, 4 * lax.axis_index("x") + lax.axis_index("z")
    within = lax.rem(y, 2) * 2 + core

    pivot_cols, pivot_rows, cross = spread(child_fronts, 10)
    row_panel, col_panel = within * 8 + jnp.arange(8), o * 2 + jnp.arange(2)
    row_step = jnp.where(row_panel < CPAN, row_panel, NEVER)
    col_step = jnp.where(col_panel < CPAN, col_panel, NEVER)
    factored, blocks = finish(
        child_fronts, [pivot_cols], [pivot_rows], cross, row_step, col_step, HIGHEST, True
    )

    assembled = extend_add(blocks, root_front, child_map)

    row_panels, col_panels = 6, 3
    order = panel_order.astype(jnp.uint32)
    each = lambda a: [a[k] for k in range(RPAN)]
    col_off = each(order % col_panels * PANEL)
    row_off = each(order % row_panels * PANEL)
    table = jnp.concatenate(
        [
            order // (4 * col_panels), order // col_panels % 4, order // row_panels,
            order % col_panels,
        ]
    ).astype(jnp.int32)
    cols = jnp.concatenate([lax.dynamic_slice_in_dim(assembled, off, PANEL, 1) for off in col_off], 1)
    rows = jnp.stack([lax.dynamic_slice_in_dim(assembled, off, PANEL, 0) for off in row_off])
    halves, pivot_rows, cross = gather_bands(cols, rows, table, 20)

    def steps(places):
        match = places[:, None] == panel_order[None, :]
        return jnp.min(jnp.where(match, jnp.arange(RPAN)[None, :], NEVER), axis=1)

    row_step = steps(r * row_panels + jnp.arange(row_panels))
    col_step = steps(o * col_panels + jnp.arange(col_panels))
    return factored, finish(assembled, halves, [pivot_rows], cross, row_step, col_step, HIGH)[0]


def solution(mesh):
    grid = Mesh(mesh.devices.reshape(4, 2, 4, 4), ("y", "core", "x", "z"))
    return jax.shard_map(
        body,
        mesh=grid,
        in_specs=(P(ROW, COL), P(ROW, COL), P(), P()),
        out_specs=(P(ROW, COL), P(ROW, COL)),
        check_vma=False,
    )
```

```python
import functools

import jax
import jax.numpy as jnp
from jax import lax
from jax.experimental import pallas as pl
from jax.experimental.pallas import tpu as pltpu
from jax.sharding import Mesh
from jax.sharding import PartitionSpec as P

PANEL = 256
BLK = 128
CPAN = 2
RPAN = 3

ROW = ("y", "core")
COL = ("x", "z")
MESH = pl.DeviceIdType.MESH
NEVER = 99

HIGH = lax.Precision.HIGH
HIGHEST = lax.Precision.HIGHEST


def peers_of(axes):
    y, core = lax.axis_index("y"), lax.axis_index("core")
    if axes == ROW:
        return 2 * y + core, 8, lambda p: {"y": p // 2, "core": lax.rem(p, 2)}
    if axes == "child":
        pair = y // 2 * 2
        me = lax.rem(y, 2) * 2 + core
        return me, 4, lambda p: {"y": pair + p // 2, "core": lax.rem(p, 2)}
    return lax.axis_index(axes), 4, lambda p: {axes: p}


def rank_in(key, group, valid):
    n = key.shape[1]
    earlier = jnp.arange(n)[None, :] < jnp.arange(n)[:, None]
    same = (key[:, :, None] == key[:, None, :]) & (group[:, None] == group[None, :])[None]
    return jnp.sum((same & valid[:, None, :] & earlier[None]).astype(jnp.int32), axis=2)


def routes(child_map):
    y, core = lax.axis_index("y"), lax.axis_index("core")
    x, z = lax.axis_index("x"), lax.axis_index("z")
    within, r, o = lax.rem(y, 2) * 2 + core, 2 * y + core, 4 * x + z
    blocks = jnp.arange(64)
    skip = CPAN * PANEL // BLK
    cyclic = (child_map % 6) * 16 + child_map // 6
    t = jnp.concatenate([jnp.zeros((2, skip), jnp.int32), cyclic], axis=1)
    valid = jnp.broadcast_to(blocks >= skip, (2, 64))
    kz = rank_in(t % 4, blocks // 4, valid)
    kx = rank_in(t % 16, blocks // 16, valid)
    kr = rank_in(t % 16 // 2, blocks // 16, valid)
    child = jnp.arange(2)[:, None]
    device, group = (blocks // 4)[None], (blocks // 16)[None]
    kinds = [
        (device == o, t % 4 * 2 + kz, blocks[None] % 4),
        ((group == x) & (t % 4 == z), t % 16 // 4 * 2 + kx, device % 4 * 2 + kz),
        (t % 16 == o, t // 16, group * 2 + kx),
        (group == within, t % 16 // 2 * 4 + kr, blocks[None] % 16),
        (t % 16 // 2 == r, t % 2 * 6 + t // 16, (child * 4 + group) * 4 + kr),
    ]
    lists = lambda k: jnp.stack([jnp.broadcast_to(a, (2, 64)) for a in k])
    place = jnp.where(lists([valid & k[0] for k in kinds]), lists([k[1] for k in kinds]), -1)
    says = lists([k[2] for k in kinds]) + 1
    match = place[:, :, None, :] == jnp.arange(32)[None, None, :, None]
    return (jnp.sum(jnp.where(match, says[:, :, None, :], 0), axis=3) - 1).reshape(-1)


Z_PICK, X_PICK, COL_FROM, R_PICK, ROW_FROM = (64 * k for k in range(5))


def whole(shape):
    return pl.BlockSpec(shape, lambda g, tab: (0,) * len(shape))


def part(shape):
    return pl.BlockSpec((1,) + shape, lambda g, tab: (g,) + (0,) * len(shape))


def local_call(kernel, grid, table, operands, in_specs, out_shapes, out_specs, scratch=()):
    return pl.pallas_call(
        kernel,
        grid_spec=pltpu.PrefetchScalarGridSpec(
            num_scalar_prefetch=1, grid=(grid,), in_specs=in_specs, out_specs=out_specs,
            scratch_shapes=list(scratch),
        ),
        out_shape=[jax.ShapeDtypeStruct(s, jnp.float32) for s in out_shapes],
        compiler_params=pltpu.CompilerParams(vmem_limit_bytes=62 * 1024 * 1024),
    )(table, *operands)


def at_least_zero(v):
    return jnp.maximum(v, 0)


def lanes(block):
    return pl.ds(pl.multiple_of(block * BLK, BLK), BLK)


PARTS = 4
SLICE = BLK // (2 * PARTS)


def extend_kernel(tab, front, *refs):
    ya_in, xb_in = refs[:PARTS], refs[PARTS : 2 * PARTS]
    send_sem, recv_sem, own_sem = refs[-3:]
    za_out, za_in, xa_out, xa_in, ya_out, yb_out, yb_in, zb_out, zb_in, xb_out = (
        refs[(2 + i) * PARTS : (3 + i) * PARTS] for i in range(10)
    )
    barrier = pltpu.get_barrier_semaphore()
    total = 0
    for ax in ("z", "x", ROW):
        me, size, ident = peers_of(ax)
        for d in range(1, size):
            pl.semaphore_signal(
                barrier, inc=1, device_id=ident(lax.rem(me + d, size)), device_id_type=MESH
            )
        total += size - 1

    started = []

    def send(number, src, dst, axes, count):
        me, size, ident = peers_of(axes)
        slot = lambda p: pl.ds(p * count, count)
        own = pltpu.make_async_copy(src.at[slot(me)], dst.at[slot(me)], own_sem.at[number])
        own.start()
        copies = []
        for d in sorted(range(1, size), key=lambda d: -min(d, size - d)):
            p = lax.rem(me + d, size)
            copy = pltpu.make_async_remote_copy(
                src_ref=src.at[slot(p)],
                dst_ref=dst.at[slot(me)],
                send_sem=send_sem.at[number, d],
                recv_sem=recv_sem.at[number, d],
                device_id=ident(p),
                device_id_type=MESH,
            )
            copy.start()
            copies.append(copy)
        started.extend(copies)
        return own, copies

    def arrive(transfer):
        own, copies = transfer
        own.wait()
        for copy in copies:
            copy.wait_recv()

    def each(count, body):
        lax.fori_loop(0, count, lambda g, _: (body(g), 0)[1], 0)

    own = 32 * (lax.axis_index("y") // 2)

    def entry(at):
        return tab[at]

    def pack_za(ch):
        rows = slice(ch * SLICE, (ch + 1) * SLICE)

        def body(g):
            za_out[ch][g] = front[entry(Z_PICK + own + g), :, rows, :]

        each(8, body)

    def pack_yb(ch):
        rows = slice((PARTS + ch) * SLICE, (PARTS + ch + 1) * SLICE)

        def body(g):
            yb_out[ch][g] = front[:, entry(R_PICK + own + g), rows, :]

        each(32, body)

    def pack_xa(ch):
        def body(g):
            xa_out[ch][g] = za_in[ch][entry(X_PICK + own + g)]

        each(8, body)

    def pack_zb(ch):
        def body(g):
            for c in range(2):
                column = entry(Z_PICK + c * 32 + g)
                for i in range(12):
                    source = entry(ROW_FROM + c * 32 + i)
                    zb_out[ch][g, c * 12 + i] = yb_in[ch][source, column]

        each(8, body)

    def pack_ya(ch):
        def body(g):
            i = entry(R_PICK + own + g)
            for slot in range(6):
                columns = slice(slot * BLK, slot * BLK + BLK)
                ya_out[ch][g, :, columns] = xa_in[ch][entry(COL_FROM + own + slot), i]

        each(32, body)

    def pack_xb(ch):
        def body(g):
            for c in range(2):
                rows = slice(c * 12, c * 12 + 12)
                xb_out[ch][g, rows] = zb_in[ch][entry(X_PICK + c * 32 + g), rows]

        each(8, body)

    stages = {
        "A": [
            (pack_za, "z", za_out, za_in, 2, 2), (pack_xa, "x", xa_out, xa_in, 2, 2),
            (pack_ya, ROW, ya_out, ya_in, 4, 3),
        ],
        "B": [
            (pack_yb, ROW, yb_out, yb_in, 4, 2), (pack_zb, "z", zb_out, zb_in, 2, 3),
            (pack_xb, "x", xb_out, xb_in, 2, 3),
        ],
    }
    free, pending, number = {"z": 0, "x": 0, ROW: 0}, [], 0

    def begin(time, half, ch, stage, packed=False):
        nonlocal number
        pack, axes, out, arriving, count, cost = stages[half][stage]
        if not packed:
            pack(ch)
        free[axes] = max(time, free[axes]) + cost
        pending.append((free[axes], number, half, ch, stage, send(number, out[ch], arriving[ch], axes, count)))
        number += 1

    pack_za(0)
    pl.semaphore_wait(barrier, total)
    begin(0, "A", 0, 0, packed=True)
    begin(0, "B", 0, 0)
    for ch in range(1, PARTS):
        pack_za(ch)
        pack_yb(ch)
    while pending:
        pending.sort(key=lambda p: p[:2])
        time, _, half, ch, stage, transfer = pending.pop(0)
        arrive(transfer)
        if stage == 0 and ch + 1 < PARTS:
            begin(time, half, ch + 1, 0, packed=True)
        if stage < 2:
            begin(time, half, ch, stage + 1)
    for copy in started:
        copy.wait_send()


def add_all(tab, root, *refs):
    i = pl.program_id(0)
    out = refs[-1]
    for slot in range(6):
        columns = slice(slot * BLK, slot * BLK + BLK)
        sums = [root[0, q * SLICE : (q + 1) * SLICE, columns] for q in range(2 * PARTS)]
        for c in range(2):
            mine = refs[c * 2 * PARTS : (c + 1) * 2 * PARTS]
            row, col = tab[ROW_FROM + c * 32 + i], tab[COL_FROM + c * 32 + slot]
            there = jnp.logical_and(row >= 0, col >= 0)
            col = at_least_zero(col)
            arrived = [m[0, :, columns] for m in mine[:PARTS]] + [m[col, 0] for m in mine[PARTS:]]
            sums = [s + jnp.where(there, a, 0.0) for s, a in zip(sums, arrived)]
        for q in range(2 * PARTS):
            out[0, q * SLICE : (q + 1) * SLICE, columns] = sums[q]


def extend_add(front, root_front, child_map):
    table = routes(child_map)
    blocks, rows, wide = (8, 16, SLICE, BLK), (32, SLICE, 768), (8, 24, SLICE, BLK)
    band = (32, 4, SLICE, BLK)
    buffers = [blocks] * (4 * PARTS) + [rows] * PARTS + [band] * (2 * PARTS) + [wide] * (3 * PARTS)
    arrived = pl.pallas_call(
        extend_kernel,
        out_shape=[jax.ShapeDtypeStruct(s, jnp.float32) for s in [rows] * PARTS + [wide] * PARTS],
        in_specs=[
            pl.BlockSpec(memory_space=pltpu.SMEM), pl.BlockSpec(memory_space=pltpu.VMEM),
        ],
        out_specs=[pl.BlockSpec(memory_space=pl.ANY)] * (2 * PARTS),
        scratch_shapes=[
            *[pltpu.VMEM(s, jnp.float32) for s in buffers],
            pltpu.SemaphoreType.DMA((6 * PARTS, 8)),
            pltpu.SemaphoreType.DMA((6 * PARTS, 8)),
            pltpu.SemaphoreType.DMA((6 * PARTS,)),
        ],
        compiler_params=pltpu.CompilerParams(
            collective_id=1, has_side_effects=True, vmem_limit_bytes=62 * 1024 * 1024
        ),
    )(jnp.maximum(table, 0), front.reshape(4, 16, BLK, BLK))
    operands, specs = [], []
    for c in range(2):
        from_rows = lambda g, tab, c=c: (at_least_zero(tab[ROW_FROM + c * 32 + g]), 0, 0)
        from_wide = lambda g, tab, c=c: (0, c * 12 + g, 0, 0)
        operands += arrived
        specs += [pl.BlockSpec((1,) + rows[1:], from_rows)] * PARTS
        specs += [pl.BlockSpec((8, 1, SLICE, BLK), from_wide)] * PARTS
    (assembled,) = local_call(
        add_all, 12, table, (root_front.reshape(12, BLK, 768), *operands),
        [part((BLK, 768)), *specs], [(12, BLK, 768)], [part((BLK, 768))],
    )
    return assembled.reshape(root_front.shape)


def copy_bands(tab, col_in, row_in, col_out, row_out):
    col_out[...] = col_in[...]
    row_out[0] = row_in[...]


def gather_kernel(tab, cols, rows, upper, lower, rows_out, cross_out, *refs):
    (arrived_a, arrived_b, arrived_rows, mine, mine_blocks, cross_a, cross_b, cross_a1, cross_b1,
     cross_a2, cross_b2, cross_a3, cross_b3, cross_all, a1, b1, a2, b2, a3, b3, a4, b4) = refs[:-3]
    send_sem, recv_sem, own_sem = refs[-3:]
    barrier = pltpu.get_barrier_semaphore()
    total = 0
    for ax in ("z", "x", ROW):
        me, size, ident = peers_of(ax)
        for d in range(1, size):
            pl.semaphore_signal(
                barrier, inc=1, device_id=ident(lax.rem(me + d, size)), device_id_type=MESH
            )
        total += size - 1
    started = []

    def send(number, src, dst, axes):
        me, size, ident = peers_of(axes)
        own = pltpu.make_async_copy(src(me), dst(me), own_sem.at[number])
        own.start()
        copies = []
        for d in sorted(range(1, size), key=lambda d: -min(d, size - d)):
            p = lax.rem(me + d, size)
            copy = pltpu.make_async_remote_copy(
                src_ref=src(p),
                dst_ref=dst(me),
                send_sem=send_sem.at[number, d],
                recv_sem=recv_sem.at[number, d],
                device_id=ident(p),
                device_id_type=MESH,
            )
            copy.start()
            copies.append(copy)
        started.extend(copies)
        return own, copies

    def arrive(*transfers):
        for own, copies in transfers:
            own.wait()
            for copy in copies:
                copy.wait_recv()

    def slot(ref):
        return lambda p: ref.at[p]

    def inner(ref):
        return lambda p: ref.at[:, p]

    def same(ref):
        return lambda p: ref

    owner_x = [tab[k] for k in range(RPAN)]
    owner_z = [tab[RPAN + k] for k in range(RPAN)]
    owner_row = [tab[2 * RPAN + k] for k in range(RPAN)]
    owned = [tab[3 * RPAN + k] for k in range(RPAN)]

    pl.semaphore_wait(barrier, total)
    t_rows = send(0, inner(rows), slot(arrived_rows), ROW)
    t_a = send(1, lambda p: cols.at[0, p], slot(arrived_a), "z")
    t_b = send(2, lambda p: cols.at[1, p], slot(arrived_b), "x")

    arrive(t_rows)
    for k in range(RPAN):
        mine[k] = arrived_rows[owner_row[k], k]
        for j in range(3):
            mine_blocks[j, k] = arrived_rows[owner_row[k], k, :, panel(j)]
    half = mine.shape[1] // 2
    for q in range(RPAN):
        block = mine_blocks[owned[q]]
        cross_a[:, :, panel(q)] = block[:, :half]
        cross_b[:, :, panel(q)] = block[:, half:]
    t_cross_a = send(3, same(cross_a), slot(cross_a1), "z")
    t_cross_b = send(4, same(cross_b), slot(cross_b1), "x")
    t_mine = send(5, same(mine), inner(rows_out), ROW)

    piece = a1.shape[1]

    def split(transfer, arrived, owners, out):
        arrive(transfer)
        for q in range(RPAN):
            for p in range(4):
                out[p, :, panel(q)] = arrived[owners[q], p * piece : (p + 1) * piece, panel(q)]

    def select(transfer, arrived, owners, out):
        arrive(transfer)
        for q in range(RPAN):
            out[..., panel(q)] = arrived[owners[q], ..., panel(q)]

    split(t_a, arrived_a, owner_z, a1)
    t_a = send(6, slot(a1), slot(a2), "x")
    split(t_b, arrived_b, owner_x, b1)
    t_b = send(7, slot(b1), slot(b2), "z")
    select(t_cross_a, cross_a1, owner_z, cross_a2)
    t_cross_a = send(8, same(cross_a2), slot(cross_a3), "x")
    select(t_cross_b, cross_b1, owner_x, cross_b2)
    t_cross_b = send(9, same(cross_b2), slot(cross_b3), "z")
    select(t_a, a2, owner_x, a3)
    t_a = send(10, same(a3), slot(a4), "x")
    select(t_b, b2, owner_z, b3)
    t_b = send(11, same(b3), slot(b4), "z")
    arrive(t_cross_a, t_cross_b)
    for q in range(RPAN):
        cross_all[:, :half, panel(q)] = cross_a3[owner_x[q], :, :, panel(q)]
        cross_all[:, half:, panel(q)] = cross_b3[owner_z[q], :, :, panel(q)]
    t_cross = send(12, same(cross_all), inner(cross_out), ROW)
    arrive(t_a)
    t_a = send(13, same(a4), slot(upper), "z")
    arrive(t_b)
    t_b = send(14, same(b4), slot(lower), "x")
    arrive(t_mine, t_cross, t_a, t_b)
    for copy in started:
        copy.wait_send()


def gather_bands(cols, rows, table, collective_id):
    count, width = cols.shape
    piece, span = PANEL // 8, rows.shape[2]
    band, ring = (RPAN, 8, piece, span), (4, count // 8, width)
    small, cross = (4, count // 32, width), (RPAN, piece // 2, width)
    full = (4,) + small
    buffers = [
        ring, ring, (8, RPAN, piece, span), (RPAN, piece, span), (3, RPAN, piece, PANEL),
        cross, cross, (4,) + cross, (4,) + cross, cross, cross, (4,) + cross, (4,) + cross,
        (RPAN, piece, width), small, small, small, small, small[1:], small[1:], small, small,
    ]
    upper, lower, pivot_rows, cross = pl.pallas_call(
        gather_kernel,
        out_shape=[jax.ShapeDtypeStruct(s, jnp.float32) for s in (full, full, band, band)],
        in_specs=[pl.BlockSpec(memory_space=pltpu.SMEM)] + [pl.BlockSpec(memory_space=pl.ANY)] * 2,
        out_specs=[pl.BlockSpec(memory_space=pl.ANY)] * 4,
        scratch_shapes=[
            *[pltpu.VMEM(s, jnp.float32) for s in buffers],
            pltpu.SemaphoreType.DMA((15, 8)),
            pltpu.SemaphoreType.DMA((15, 8)),
            pltpu.SemaphoreType.DMA((15,)),
        ],
        compiler_params=pltpu.CompilerParams(
            collective_id=collective_id, has_side_effects=True, vmem_limit_bytes=62 * 1024 * 1024
        ),
    )(table, cols.reshape(2, 4, count // 8, width), rows.reshape(band))
    halves = [a.reshape(count // 2, width) for a in (upper, lower)]
    return halves, pivot_rows.reshape(width, span), cross.reshape(width, width)


PARENT = {
    (3, 0): (0, 0), (3, 3): (3, 0), (3, 1): (3, 0), (2, 0): (3, 0), (2, 3): (2, 0),
    (3, 2): (3, 1), (0, 1): (3, 1), (0, 3): (3, 3), (2, 1): (3, 1), (1, 0): (2, 0),
    (2, 2): (3, 2), (1, 1): (2, 1), (0, 2): (3, 2), (1, 3): (2, 3), (1, 2): (2, 2),
}


def turned(place, quarter_turns):
    for _ in range(quarter_turns):
        place = (-place[1] % 4, place[0])
    return place


def tree_children(turn):
    children = [[] for _ in range(16)]
    for child, parent in PARENT.items():
        child, parent = turned(child, turn), turned(parent, turn)
        children[4 * parent[0] + parent[1]].append(4 * child[0] + child[1])
    return children


def tree_depth(turn):
    depth = [0] * 16
    for place in PARENT:
        node, hops = place, 0
        while node != (0, 0):
            node, hops = PARENT[node], hops + 1
        place = turned(place, turn)
        depth[4 * place[0] + place[1]] = hops
    return depth


def lookup(values, index):
    result = jnp.int32(values[0])
    for k in range(1, len(values)):
        result = jnp.where(index == k, jnp.int32(values[k]), result)
    return result


CHUNK = 32
CHUNKS = 2048 // (4 * CHUNK)
CROSS = CPAN * PANEL // (4 * CHUNK)
U_PARTS = 4
DEPTH = 5
SLACK = 2
U_TURN = 8


def spread_kernel(front, cols, rows, cross, recv, send, cross_recv, cross_send, rows_recv,
                  rows_send, own_sem, stage):
    y, core = lax.axis_index("y"), lax.axis_index("core")
    x, z = lax.axis_index("x"), lax.axis_index("z")
    place, within = 4 * x + z, lax.rem(y, 2) * 2 + core
    is_root = place == 0
    tables = [tree_children(turn) for turn in range(4)]
    target = [
        [lookup([(t[k] + [-1, -1, -1])[s] for k in range(16)], place) for s in range(3)]
        for t in tables
    ]
    depth = [lookup(tree_depth(turn), place) for turn in range(4)]
    sibling = {"core": 1 - core}
    above = {"y": y // 2 * 2 + 1 - lax.rem(y, 2)}

    barrier = pltpu.get_barrier_semaphore()
    for ident in (
        {"x": lax.rem(x + 1, 4)}, {"x": lax.rem(x + 3, 4)},
        {"z": lax.rem(z + 1, 4)}, {"z": lax.rem(z + 3, 4)}, sibling, above,
    ):
        pl.semaphore_signal(barrier, inc=1, device_id=ident, device_id_type=MESH)

    part = CPAN * PANEL // U_PARTS
    whole_band = pl.ds(0, CPAN * PANEL)
    load_own = pltpu.make_async_copy(front, stage, own_sem.at[0])
    own_cols = pltpu.make_async_copy(stage, cols, own_sem.at[0])
    own_rows = pltpu.make_async_copy(stage.at[whole_band], rows, own_sem.at[1])
    load_own.start()
    load_cross = pltpu.make_async_copy(
        cols.at[whole_band], stage.at[whole_band], own_sem.at[2]
    )
    store_cross = pltpu.make_async_copy(stage.at[whole_band], cross, own_sem.at[2])
    pl.semaphore_wait(barrier, 6)

    def rows_copy(src, k, way, ident):
        span = pl.ds(k * part, part)
        return pltpu.make_async_remote_copy(
            src_ref=src.at[span], dst_ref=rows.at[span], send_sem=rows_send.at[way, k],
            recv_sem=rows_recv.at[k], device_id=ident, device_id_type=MESH,
        )

    def band(c, q):
        return pl.ds(pl.multiple_of((c * 4 + q) * CHUNK, CHUNK), CHUNK)

    def cols_copy(src, c, q, s):
        span = band(c, q)
        there = jnp.maximum(target[q][s], 0)
        return pltpu.make_async_remote_copy(
            src_ref=src.at[span], dst_ref=cols.at[span], send_sem=send.at[q, s, c],
            recv_sem=recv.at[q, c], device_id={"x": there // 4, "z": lax.rem(there, 4)},
            device_id_type=MESH,
        )

    def cross_copy(src, c, q, way, ident):
        span = band(c, q)
        return pltpu.make_async_remote_copy(
            src_ref=src.at[span], dst_ref=cross.at[span], send_sem=cross_send.at[way, q, c],
            recv_sem=cross_recv.at[q, c], device_id=ident, device_id_type=MESH,
        )

    @pl.when(within == 0)
    def _():
        for k in range(U_PARTS):
            rows_copy(front, k, 0, above).start()
            rows_copy(front, k, 1, sibling).start()

    load_own.wait()

    @pl.when(is_root)
    def _():
        own_cols.start()

    @pl.when(within == 0)
    def _():
        own_rows.start()
        own_rows.wait()

    @pl.when(is_root)
    def _():
        own_cols.wait()

    def both(first, second):
        return jnp.logical_and(first, second)

    def pass_cols(c, q):
        @pl.when(is_root)
        def _():
            cols_copy(front, c, q, 0).start()

            @pl.when(both(within == 0, c < CROSS))
            def _():
                cross_copy(front, c, q, 0, above).start()
                cross_copy(front, c, q, 1, sibling).start()

        @pl.when(jnp.logical_not(is_root))
        def _():
            cols_copy(cols, c, q, 0).wait_recv()
            for s in range(3):

                @pl.when(target[q][s] >= 0)
                def _():
                    cols_copy(cols, c, q, s).start()

            @pl.when(both(within == 0, c < CROSS))
            def _():
                cross_copy(cols, c, q, 0, above).start()
                cross_copy(cols, c, q, 1, sibling).start()

    def loop(lo, hi, body):
        lax.fori_loop(lo, hi, lambda c, _: (body(c), 0)[1], 0)

    def step(turn):
        for q in range(4):
            c = turn - SLACK * depth[q]

            @pl.when(both(c >= 0, c < CHUNKS))
            def _():
                pass_cols(c, q)

        for q in range(4):
            late = turn - SLACK * (depth[q] + 1)

            @pl.when(both(within == 2, both(late >= 0, late < CROSS)))
            def _():
                cross_copy(cross, late, q, 0, above).wait_recv()
                cross_copy(cross, late, q, 1, sibling).start()

        for k in range(U_PARTS):

            @pl.when(both(within == 2, turn == U_TURN + k))
            def _():
                rows_copy(rows, k, 0, above).wait_recv()
                rows_copy(rows, k, 1, sibling).start()

        @pl.when(both(within == 0, turn == CROSS + SLACK * DEPTH))
        def _():
            load_cross.start()

        @pl.when(both(within == 0, turn == CROSS + SLACK * DEPTH + 3))
        def _():
            load_cross.wait()
            store_cross.start()

    loop(0, CHUNKS + SLACK * DEPTH, step)

    @pl.when(within == 0)
    def _():
        for k in range(U_PARTS):
            rows_copy(front, k, 0, above).wait_send()
            rows_copy(front, k, 1, sibling).wait_send()

        def send_done(c):
            for q in range(4):
                cross_copy(front, c, q, 0, above).wait_send()
                cross_copy(front, c, q, 1, sibling).wait_send()

        loop(0, CROSS, send_done)

    @pl.when(within == 2)
    def _():
        for k in range(U_PARTS):
            rows_copy(rows, k, 1, sibling).wait_send()

        def send_done(c):
            for q in range(4):
                cross_copy(cross, c, q, 1, sibling).wait_send()

        loop(0, CROSS, send_done)

    @pl.when(lax.rem(within, 2) == 1)
    def _():
        for k in range(U_PARTS):
            rows_copy(rows, k, 0, sibling).wait_recv()

        def arrived(c):
            for q in range(4):
                cross_copy(cross, c, q, 0, sibling).wait_recv()

        loop(0, CROSS, arrived)

    def cols_done(c):
        for q in range(4):
            for s in range(3):

                @pl.when(target[q][s] >= 0)
                def _():
                    cols_copy(front, c, q, s).wait_send()

    loop(0, CHUNKS, cols_done)

    @pl.when(within == 0)
    def _():
        store_cross.wait()


def spread(front, collective_id):
    rows, cols = front.shape
    width = CPAN * PANEL
    shapes = [(rows, width), (width, cols), (width, width)]
    dma = pltpu.SemaphoreType.DMA
    return pl.pallas_call(
        spread_kernel,
        out_shape=[jax.ShapeDtypeStruct(s, jnp.float32) for s in shapes],
        in_specs=[pl.BlockSpec(memory_space=pl.ANY)],
        out_specs=[pl.BlockSpec(memory_space=pl.ANY)] * 3,
        scratch_shapes=[
            dma((4, CHUNKS)), dma((4, 3, CHUNKS)), dma((4, CROSS)), dma((2, 4, CROSS)),
            dma((U_PARTS,)), dma((2, U_PARTS)), dma((3,)), pltpu.VMEM(front.shape, jnp.float32),
        ],
        compiler_params=pltpu.CompilerParams(
            collective_id=collective_id, has_side_effects=True, vmem_limit_bytes=62 * 1024 * 1024
        ),
    )(front)


def dot(a, b, precision=HIGH):
    return jnp.dot(a, b, precision=precision, preferred_element_type=jnp.float32)


def newton(block):
    shape = (PANEL, PANEL)
    eye = lax.broadcasted_iota(jnp.int32, shape, 0) == lax.broadcasted_iota(jnp.int32, shape, 1)
    kept = jnp.where(eye, block, 0.0)
    by_col = 1.0 / jnp.sum(kept, axis=0, keepdims=True)
    by_row = 1.0 / jnp.sum(kept, axis=1, keepdims=True)
    identity = jnp.where(eye, 1.0, 0.0)
    error = identity - block * by_col
    product = identity + error
    for _ in range(3):
        error = dot(error, error, HIGHEST)
        product = product + dot(product, error, HIGHEST)
    return product * by_row


def panel(k):
    return slice(k * PANEL, (k + 1) * PANEL)


def finish_kernel(n, row_panels, col_panels, precision, bands, tail, tab, front, *refs):
    cols, rows, cross, outs = refs[:bands], refs[bands:tail], refs[tail], refs[tail + 1 : -3]
    work, inverse, pivots = refs[-3:]
    g = pl.program_id(0)

    @pl.when(g == 0)
    def _():
        work[...] = cross[...]
        for i, part in enumerate(rows):
            span = part.shape[1]
            pivots[:, i * span : (i + 1) * span] = part[...]
        for k in range(n):
            inverse[k] = newton(work[panel(k), panel(k)])
            for p in range(k + 1, n):
                factor = dot(work[panel(p), panel(k)], inverse[k], HIGHEST)
                for q in range(k + 1, n):
                    work[panel(p), panel(q)] -= dot(factor, work[panel(k), panel(q)], HIGHEST)
                pivots[panel(p), :] -= dot(factor, pivots[panel(k), :], HIGHEST)
        for j in range(col_panels):
            for k in range(n):
                pivots[panel(k), panel(j)] = jnp.where(
                    tab[row_panels + j] > k, pivots[panel(k), panel(j)], 0.0
                )

    mine = cols[0][...]
    if bands == 2:
        mine = jnp.where(g < row_panels // 2, mine, cols[1][...])
    band = [mine[:, panel(k)] for k in range(n)]
    for k in range(n):
        band[k] = dot(band[k], inverse[k], HIGHEST)
        for q in range(k + 1, n):
            band[q] = band[q] - dot(band[k], work[panel(k), panel(q)], HIGHEST)
    band = [jnp.where(tab[g] > k, band[k], 0.0) for k in range(n)]
    factors = jnp.concatenate(band, axis=1)
    for j in range(col_panels):
        new = front[:, panel(j)] - dot(factors, pivots[:, panel(j)], precision)
        for k in range(n):
            here = jnp.logical_and(tab[row_panels + j] == k, tab[g] > k)
            new = jnp.where(here, band[k], new)
        outs[0][:, panel(j)] = new
        if len(outs) == 2:
            outs[1][2 * j] = new[:, :BLK]
            outs[1][2 * j + 1] = new[:, BLK:]


def finish(front, bands, pivot_rows, cross, row_step, col_step, precision, blocked=False):
    rows, cols = front.shape
    width = cross.shape[0]
    n, row_panels, col_panels = width // PANEL, rows // PANEL, cols // PANEL
    half = row_panels // 2
    keep = lambda shape: pl.BlockSpec(shape, lambda g, tab: (0, 0))
    if len(bands) == 1:
        band_specs = [pl.BlockSpec((PANEL, width), lambda g, tab: (g, 0))]
    else:
        band_specs = [
            pl.BlockSpec((PANEL, width), lambda g, tab: (jnp.minimum(g, half - 1), 0)),
            pl.BlockSpec((PANEL, width), lambda g, tab: (jnp.maximum(g - half, 0), 0)),
        ]
    return local_call(
        functools.partial(finish_kernel, n, row_panels, col_panels, precision, len(bands), len(bands) + len(pivot_rows)),
        row_panels,
        jnp.concatenate([row_step, col_step]).astype(jnp.int32),
        (front, *bands, *pivot_rows, cross),
        [
            pl.BlockSpec((PANEL, cols), lambda g, tab: (g, 0)),
            *band_specs,
            *[keep(p.shape) for p in pivot_rows],
            keep(cross.shape),
        ],
        [front.shape] + [(cols // BLK, rows, BLK)] * blocked,
        [pl.BlockSpec((PANEL, cols), lambda g, tab: (g, 0))]
        + [pl.BlockSpec((cols // BLK, PANEL, BLK), lambda g, tab: (0, g, 0))] * blocked,
        scratch=[
            pltpu.VMEM((width, width), jnp.float32),
            pltpu.VMEM((n, PANEL, PANEL), jnp.float32),
            pltpu.VMEM((width, cols), jnp.float32),
        ],
    )


def body(child_fronts, root_front, child_map, panel_order):
    y, core = lax.axis_index("y"), lax.axis_index("core")
    r, o = 2 * y + core, 4 * lax.axis_index("x") + lax.axis_index("z")
    within = lax.rem(y, 2) * 2 + core

    pivot_cols, pivot_rows, cross = spread(child_fronts, 10)
    row_panel, col_panel = within * 8 + jnp.arange(8), o * 2 + jnp.arange(2)
    row_step = jnp.where(row_panel < CPAN, row_panel, NEVER)
    col_step = jnp.where(col_panel < CPAN, col_panel, NEVER)
    factored, blocks = finish(
        child_fronts, [pivot_cols], [pivot_rows], cross, row_step, col_step, HIGHEST, True
    )

    assembled = extend_add(blocks, root_front, child_map)

    row_panels, col_panels = 6, 3
    order = panel_order.astype(jnp.uint32)
    table = jnp.concatenate(
        [
            order // (4 * col_panels), order // col_panels % 4, order // row_panels,
            order % col_panels, order % row_panels,
        ]
    ).astype(jnp.int32)
    cols, rows = local_call(
        copy_bands, RPAN, table, (assembled, assembled),
        [
            pl.BlockSpec((1536, PANEL), lambda k, tab: (0, tab[3 * RPAN + k])),
            pl.BlockSpec((PANEL, 768), lambda k, tab: (tab[4 * RPAN + k], 0)),
        ],
        [(1536, RPAN * PANEL), (RPAN, PANEL, 768)],
        [pl.BlockSpec((1536, PANEL), lambda k, tab: (0, k)), part((PANEL, 768))],
    )
    halves, pivot_rows, cross = gather_bands(cols, rows, table, 20)

    def steps(places):
        match = places[:, None] == panel_order[None, :]
        return jnp.min(jnp.where(match, jnp.arange(RPAN)[None, :], NEVER), axis=1)

    row_step = steps(r * row_panels + jnp.arange(row_panels))
    col_step = steps(o * col_panels + jnp.arange(col_panels))
    return factored, finish(assembled, halves, [pivot_rows], cross, row_step, col_step, HIGH)[0]


def solution(mesh):
    grid = Mesh(mesh.devices.reshape(4, 2, 4, 4), ("y", "core", "x", "z"))
    return jax.shard_map(
        body,
        mesh=grid,
        in_specs=(P(ROW, COL), P(ROW, COL), P(), P()),
        out_specs=(P(ROW, COL), P(ROW, COL)),
        check_vma=False,
    )
```
